32 devices in a mesh: pb: 8 (over z, core), ka: 2 (over y), ha: 2 (over x).
Axes of the slice: x: 2, y: 2, z: 4, core: 2. Of those that a mesh axis runs over, the one named last changes fastest.
Arguments:
- context: bfloat16 [8192, 512], P(('pb', 'ka')), may hold values from -6 to 6
- item_owner: int32 [8192, 1], P(('pb', 'ka')), may hold values from 0 to 15; in each aligned block of 512 rows (0 to 511, 512 to 1023, ...) at most 64 rows name the same one
- item_offset: int32 [8192], P(('pb', 'ka')), may hold values from 0 to 8191
- lengths: int32 [8, 4, 4], P('pb'), may hold values from 1 to 253, as said below
- times: int32 [8, 4, 256], P('pb'), may hold values from 0 to 255
- table: bfloat16 [131072, 512], P(('pb', 'ka')), may hold values from -4 to 4
- cotangent: bfloat16 [8192, 512], P(('pb', 'ka')), may hold values from -6 to 6
- ln_in_gain: float32 [512], replicated, may hold values from 0.5 to 1.5
- w_uvqk: bfloat16 [512, 4, 512], P('pb', None, 'ha'), may hold values from -0.25 to 0.25
- b_uvqk: float32 [4, 512], P(None, 'ha'), may hold values from -2 to 2
- rel_bias: float32 [8, 256], P('ha'), may hold values from -4 to 4
- time_bias: float32 [8, 128], P('ha'), may hold values from -4 to 4
- ln_out_gain: float32 [512], P('ha'), may hold values from 0.5 to 1.5
- w_out: bfloat16 [512, 512], P('ha', 'pb'), may hold values from -0.25 to 0.25
- b_out: float32 [512], replicated, may hold values from -2 to 2
Outputs:
- mixed: bfloat16 [8192, 512], P(('pb', 'ka'), 'ha')
- input_grad: bfloat16 [8192, 512], P(('pb', 'ka'))
- table_grad: float32 [131072, 512], P(('pb', 'ka'))
- grad_ln_in_gain: float32 [512], replicated
- grad_w_uvqk: float32 [512, 4, 512], P(('pb', 'ka'), None, 'ha')
- grad_b_uvqk: float32 [4, 512], P(None, 'ha')
- grad_rel_bias: float32 [8, 256], P('ha')
- grad_time_bias: float32 [8, 128], P('ha')
- grad_ln_out_gain: float32 [512], P('ha')
- grad_w_out: float32 [512, 512], P('ha', ('pb', 'ka'))
- grad_b_out: float32 [512], replicated
The draws below stay inside these ranges and needn't reach their ends.
Inputs may be any that keep to these rules, and one draw needn't show every extreme that they name: `item_owner`: among the 512 rows of one device (aligned blocks), no owner is named more than 64 times. The 4 lengths of a stream sum to at most 256; positions after their sum are padding.
All inputs are finite; a program needn't handle non-finite values.
Results may differ from the reference program's by a relative error of at most 0.0094.
Values may be sent and summed in bfloat16 or wider, within the bound.
A program may use at most 192 MiB of HBM per device.

```python
import math
import jax
import jax.numpy as jnp
import numpy as np
from jax import lax

D = 512
H = 8
DH = 64
HD = 512
TOK_DEV = 128
MB = 4
SEQ_GRP = 4
NB = 128
TAB_DEV = 8192
OWNERS = 16
TABLE = 131072
GROUP = 256
CAP = 64
TOKENS = 8192
N_PB = 8
N_KA = 2


def draw_lengths(key, part):
    key = jax.random.fold_in(key, 11)
    streams = N_PB * MB
    short_most = max(1, TOK_DEV // 8)
    key_list = jax.random.split(key, 4)
    shorts = jax.random.randint(key_list[0], (streams, SEQ_GRP), 1, short_most + 1)
    paddings = jax.random.randint(key_list[1], (streams,), 0, TOK_DEV // 2)
    longest = jax.random.randint(key_list[2], (streams,), 0, SEQ_GRP)
    chosen_stream = jax.random.randint(key_list[3], (), 0, streams)
    chosen = jnp.arange(streams) == chosen_stream
    shorts = jnp.where(chosen[:, None], 1, shorts)
    paddings = jnp.where(chosen, 0, paddings)
    is_long = jnp.arange(SEQ_GRP)[None, :] == longest[:, None]
    others = jnp.sum(jnp.where(is_long, 0, shorts), axis=1)
    long_length = GROUP - others - paddings
    result = jnp.where(is_long, long_length[:, None], shorts)
    return result.reshape(N_PB, MB, SEQ_GRP).astype(jnp.int32)


def place_ends(values, own_key, low, largest):
    dims = values.shape
    spot = [jax.random.randint(jax.random.fold_in(own_key, axis), (), 0, dims[axis]) for axis in range(len(dims))]
    values = values.at[tuple(spot)].set(low)
    longest = dims.index(max(dims))
    spot[longest] = (spot[longest] + 1) % dims[longest]
    return values.at[tuple(spot)].set(largest)


def shard_levels(stream_key, extent, shards, least, largest):
    level = 1.0
    for axis_at, parts in shards:
        heights = jax.random.uniform(jax.random.fold_in(jax.random.fold_in(stream_key, 6), axis_at), (parts,), jnp.float32, least / len(shards), largest / len(shards))
        level = level * jnp.repeat(jnp.exp(heights), extent[axis_at] // parts).reshape((-1,) + (1,) * (len(extent) - 1 - axis_at))
    return level


def deal_out(rng, own, number, rows, amount, top, most, lean):
    order = jax.random.permutation(rng, amount)
    packed, ordinary = shares(amount, rows * top, most, lean, True), shares(amount, rows * top, most, lean, False)
    places = jnp.arange(amount)

    def named(sizes, rotation):
        used = int((sizes > 0).sum())
        fixed = max(1, used // 4)
        moved = fixed + (places - fixed + rotation * (used - fixed)) % max(1, amount - fixed)
        return jnp.zeros((amount,), jnp.int32).at[order[jnp.where(places < fixed, places, moved)]].set(jnp.asarray(sizes, jnp.int32))

    sizes = jnp.where(number % 4 == 0, named(packed, number // 4), named(ordinary, number - number // 4 - 1))
    mixed = jax.random.permutation(jax.random.fold_in(own, 3), amount)
    giver, receiver = mixed[0:amount // 2 * 2:2], mixed[1:amount // 2 * 2:2]
    room = jnp.minimum(sizes[giver] - 1, most - sizes[receiver]) // 2
    room = jnp.where((giver == order[0]) | (receiver == order[0]) | (sizes[receiver] == 0), 0, jnp.maximum(room, 0))
    moved = jax.random.randint(jax.random.fold_in(own, 4), (amount // 2,), 0, 1 << 20) % (room + 1)
    sizes = sizes.at[giver].add(-moved).at[receiver].add(moved)
    labels = jnp.searchsorted(jnp.cumsum(sizes), jnp.arange(rows * top), side="right").astype(jnp.int32)
    listing = labels.reshape(top, rows).T
    listing = listing[jax.random.permutation(jax.random.fold_in(own, 1), rows)]
    rotation = jax.random.randint(jax.random.fold_in(own, 2), (rows, 1), 0, top)
    return jnp.take_along_axis(listing, (jnp.arange(top)[None, :] + rotation) % top, axis=1)


def shares(number_of, total, limit, lean, full):
    portions = [(1 << 20) // math.isqrt(rank ** lean) + 1 for rank in range(1, number_of + 1)]
    largest = limit if full else min(limit, max(-(-total // number_of), total * portions[0] // sum(portions)))
    least = 1 if total - largest >= number_of - 1 else 0
    counts, surplus = [largest] + [least] * (number_of - 1), total - largest - least * (number_of - 1)
    while surplus > 0:
        movable = [i for i in range(1, number_of) if counts[i] < largest] or [i for i in range(1, number_of) if counts[i] < limit]
        pool, remaining = sum([portions[i] for i in movable]), surplus
        for i in movable:
            more = min(limit - counts[i], max(1, remaining * portions[i] // pool), surplus)
            counts[i] = counts[i] + more
            surplus = surplus - more
    return np.array(counts)


def noise(own_key, dims, scale, most, cuts=(), held_as=jnp.bfloat16):
    values = scale * jax.random.normal(own_key, dims, jnp.float32)
    if cuts:
        values = values * shard_levels(own_key, dims, cuts, -0.22, 0.18)
    return jnp.clip(values, -most, most).astype(held_as)


def setup_inputs(seed: int = 0) -> dict:
    keys = jax.random.split(jax.random.key(seed), 16)
    context = noise(keys[0], (TOKENS, D), 1.0, 6.0, ((0, 16),))
    item_owner_keys = jax.random.split(jax.random.fold_in(keys[1], 1), TOKENS // (MB * TOK_DEV))
    item_owner_turns = jax.random.permutation(jax.random.fold_in(keys[1], 3), TOKENS // (MB * TOK_DEV))
    item_owner = jax.vmap(lambda own, number: deal_out(jax.random.fold_in(keys[1], 2), own, number, MB * TOK_DEV, OWNERS, 1, CAP, 2))(item_owner_keys, item_owner_turns).reshape((TOKENS, 1))
    item_offset = place_ends(jax.random.randint(keys[2], (TOKENS,), 0, TAB_DEV), jax.random.fold_in(keys[2], 1), 0, TAB_DEV - 1).astype(jnp.int32)
    lengths = draw_lengths(jax.random.fold_in(keys[15], 71), 0)
    times = place_ends(jax.random.randint(keys[4], (N_PB, MB, GROUP), 0, 2 * NB), jax.random.fold_in(keys[4], 1), 0, (2 * NB) - 1).astype(jnp.int32)
    table = noise(keys[5], (TABLE, D), 0.5, 4.0, ((0, 16),))
    cotangent = noise(keys[6], (TOKENS, D), 1.0, 6.0, ((0, 16),))
    ln_in_gain = jnp.clip(1.0 + 0.1 * jax.random.normal(keys[7], (D,), jnp.float32), 0.5, 1.5)
    w_uvqk = noise(keys[8], (D, 4, HD), D ** -0.5, 0.25, ((0, 8), (2, 2)))
    b_uvqk = noise(keys[9], (4, HD), 0.3, 2.0, ((1, 2),), jnp.float32)
    rel_bias = noise(keys[10], (H, GROUP), 1.0, 4.0, ((0, 2),), jnp.float32)
    time_bias = noise(keys[11], (H, NB), 1.0, 4.0, ((0, 2),), jnp.float32)
    ln_out_gain = jnp.clip(1.0 + 0.1 * jax.random.normal(keys[12], (HD,), jnp.float32), 0.5, 1.5)
    w_out = noise(keys[13], (HD, D), HD ** -0.5, 0.25, ((0, 2), (1, 8)))
    b_out = noise(keys[14], (D,), 0.3, 2.0, (), jnp.float32)
    return {"context": context, "item_owner": item_owner, "item_offset": item_offset, "lengths": lengths, "times": times, "table": table, "cotangent": cotangent, "ln_in_gain": ln_in_gain, "w_uvqk": w_uvqk, "b_uvqk": b_uvqk, "rel_bias": rel_bias, "time_bias": time_bias, "ln_out_gain": ln_out_gain, "w_out": w_out, "b_out": b_out}


@jax.custom_vjp
def low(v):
    return lax.optimization_barrier(v.astype(jnp.bfloat16)).astype(jnp.float32)

@jax.custom_vjp
def low_back(v):
    return v

def low_keep(v):
    return (low(v), None)

def low_pass(kept, grad):
    return (grad,)

def back_keep(v):
    return (v, None)

def back_low(kept, grad):
    return (low(grad),)
low.defvjp(low_keep, low_pass)
low_back.defvjp(back_keep, back_low)
epsilon = 1e-05
highest = lax.Precision.HIGHEST

def layer_norm(values, gain):
    centered = values - lax.optimization_barrier(jnp.mean(values, axis=-1, keepdims=True))
    variance = lax.optimization_barrier(jnp.mean(centered * centered, axis=-1, keepdims=True))
    return centered * lax.rsqrt(variance + epsilon) * gain

def stream_layout(lengths_row):
    places = jnp.arange(GROUP, dtype=jnp.int32)
    ends = jnp.cumsum(lengths_row, dtype=jnp.int32)
    member = lax.optimization_barrier(jnp.sum((ends[None, :] <= places[:, None]).astype(jnp.int32), axis=1)).astype(jnp.int32)
    onehot = (member[:, None] == jnp.arange(SEQ_GRP, dtype=jnp.int32)[None, :]).astype(jnp.float32)
    counted = jnp.maximum(lax.optimization_barrier(jnp.sum(onehot * lengths_row.astype(jnp.float32)[None, :], axis=1)), 1.0)
    return (places, member, counted)

def attend_block(block_in, key_heads, value_heads, places, member, stamps, rel_bias, time_bias):
    query_heads, query_pos, query_member, query_count, query_stamp = block_in
    distance = query_pos[:, None] - places[None, :]
    pos_index = jnp.clip(distance, 0, GROUP - 1)
    time_index = jnp.clip(query_stamp[:, None] - stamps[None, :], 0, NB - 1)
    scores = jnp.einsum('qhd,khd->hqk', query_heads, key_heads, precision=highest) * DH ** (-0.5)
    scores = low_back(scores + rel_bias[:, pos_index] + time_bias[:, time_index])
    allowed = (query_member[:, None] == member[None, :]) & (query_member[:, None] < SEQ_GRP) & (distance >= 0)
    weights = low(jnp.where(allowed[None], jax.nn.silu(scores), 0.0) / query_count[None, :, None])
    return jnp.einsum('hqk,khd->qhd', weights, value_heads, precision=highest)

def stream_forward(h_in, params, places, member, counted, stamps):
    gain_in, w_proj, b_proj, rel_bias, time_bias, gain_out, w_final, b_final = params
    normed = low(layer_norm(h_in, gain_in))
    pre_act = low_back(jnp.einsum('td,dgc->tgc', normed, w_proj, precision=highest) + b_proj)
    activated = jax.nn.silu(pre_act)
    gate_part = activated[:, 0]
    values = low(activated[:, 1]).reshape(GROUP, H, DH)
    queries = low(activated[:, 2]).reshape(GROUP, H, DH)
    key_rows = low(activated[:, 3]).reshape(GROUP, H, DH)

    def split_blocks(array):
        return array.reshape((N_KA, TOK_DEV) + array.shape[1:])

    def one_block(block_in):
        return attend_block(block_in, key_rows, values, places, member, stamps, rel_bias, time_bias)
    outputs = lax.map(jax.checkpoint(one_block), (split_blocks(queries), split_blocks(places), split_blocks(member), split_blocks(counted), split_blocks(stamps)))
    attended = low_back(outputs.reshape(GROUP, HD))
    mixed_in = low(layer_norm(attended, gain_out) * gate_part)
    return jnp.dot(mixed_in, w_final, precision=highest) + b_final + h_in

def to_streams(array):
    return array.reshape(N_PB, N_KA, MB, TOK_DEV, -1).transpose(0, 2, 1, 3, 4).reshape(N_PB * MB, GROUP, -1)

def from_streams(array):
    return array.reshape(N_PB, MB, N_KA, TOK_DEV, -1).transpose(0, 2, 1, 3, 4).reshape(TOKENS, -1)

def reference(context, item_owner, item_offset, lengths, times, table, cotangent, ln_in_gain, w_uvqk, b_uvqk, rel_bias, time_bias, ln_out_gain, w_out, b_out):
    item_ids = (item_owner[:, 0] * TAB_DEV + item_offset).astype(jnp.int32)
    start = context.astype(jnp.float32) + table[item_ids].astype(jnp.float32)
    start_streams = to_streams(start)
    cot_streams = to_streams(cotangent.astype(jnp.float32))
    lens_all = lengths.reshape(N_PB * MB, SEQ_GRP)
    stamps_all = times.reshape(N_PB * MB, GROUP)
    params = (ln_in_gain.astype(jnp.float32), w_uvqk.astype(jnp.float32), b_uvqk.astype(jnp.float32), rel_bias.astype(jnp.float32), time_bias.astype(jnp.float32), ln_out_gain.astype(jnp.float32), w_out.astype(jnp.float32), b_out.astype(jnp.float32))
    totals = jax.tree.map(jnp.zeros_like, params)

    def stream_step(carried, stream_in):
        h_in, cot_in, lens_row, stamp_row = stream_in
        places, member, counted = stream_layout(lens_row)

        def forward(h_value, param_value):
            return stream_forward(h_value, param_value, places, member, counted, stamp_row)
        result, pull_back = jax.vjp(forward, h_in, params)
        grad_h, grad_params = pull_back(cot_in)
        return (jax.tree.map(jnp.add, carried, grad_params), (result, grad_h))
    totals, (results, grad_starts) = lax.scan(stream_step, totals, (start_streams, cot_streams, lens_all, stamps_all))
    mixed = from_streams(results)
    grad_start = from_streams(grad_starts)
    table_grad = jax.ops.segment_sum(grad_start, item_ids, num_segments=TABLE)
    return (mixed.astype(jnp.bfloat16), grad_start.astype(jnp.bfloat16), table_grad, totals[0], totals[1], totals[2], totals[3], totals[4], totals[5], totals[6], totals[7])
```

```python
import functools

import jax
import jax.numpy as jnp
from jax import lax
from jax.experimental import pallas as pl
from jax.experimental.pallas import tpu as pltpu
from jax.sharding import PartitionSpec as P

DH = 64
TOK_DEV = 128
MB = 4
SEQ_GRP = 4
F32 = jnp.float32
BF16 = jnp.bfloat16


epsilon = 1e-05


def silu_slope(values):
    sigma = jax.nn.sigmoid(values)
    return sigma * (1.0 + values * (1.0 - sigma))


def norm_rows(values, gain):
    centered = values - jnp.mean(values, axis=-1, keepdims=True)
    inverse = lax.rsqrt(jnp.mean(centered * centered, axis=-1, keepdims=True) + epsilon)
    unit_rows = centered * inverse
    return (unit_rows * gain, unit_rows, inverse)


def norm_back(grad_unit, unit_rows, inverse):
    first_mean = jnp.mean(grad_unit, axis=-1, keepdims=True)
    second_mean = jnp.mean(grad_unit * unit_rows, axis=-1, keepdims=True)
    return inverse * (grad_unit - first_mean - unit_rows * second_mean)


def stream_layout(lengths_row, group):
    places = jnp.arange(group, dtype=jnp.int32)
    ends = jnp.cumsum(lengths_row, dtype=jnp.int32)
    member = jnp.sum((ends[None, :] <= places[:, None]).astype(jnp.int32), axis=1)
    onehot = (member[:, None] == jnp.arange(SEQ_GRP, dtype=jnp.int32)[None, :]).astype(jnp.float32)
    counted = jnp.maximum(jnp.sum(onehot * lengths_row.astype(jnp.float32)[None, :], axis=1), 1.0)
    return (places, member, counted)


def diagonal_bias(rel_bias, query_first, key_first, query_len, key_len):
    heads, group = rel_bias.shape
    span = query_len + key_len - 1
    padded = jnp.concatenate([jnp.zeros((heads, group), jnp.float32), rel_bias], axis=1)
    window = lax.dynamic_slice_in_dim(
        padded, query_first - key_first - key_len + 1 + group, span, 1
    )
    flipped = jnp.concatenate([window[:, ::-1], jnp.zeros((heads, 1), jnp.float32)], axis=1)
    skewed = jnp.tile(flipped, (1, query_len))[:, : query_len * span].reshape(
        heads, query_len, span
    )
    return skewed[:, :, query_len - 1 : query_len - 1 + key_len]


def diagonal_sums(grad_scores, query_first, key_first, group):
    heads, query_len, key_len = grad_scores.shape
    span = query_len + key_len - 1
    widened = jnp.pad(grad_scores.astype(jnp.float32), ((0, 0), (0, 0), (query_len - 1, 0)))
    flat = jnp.pad(widened.reshape(heads, query_len * span), ((0, 0), (0, query_len)))
    totals = jnp.sum(flat.reshape(heads, query_len, span + 1), axis=1)
    window = totals[:, :span][:, ::-1]
    placed = lax.dynamic_update_slice_in_dim(
        jnp.zeros((heads, 2 * group), jnp.float32),
        window,
        query_first - key_first - key_len + 1 + group,
        1,
    )
    return placed[:, group:]


def bucket_lookup(time_bias, bucket_hot):
    high = time_bias.astype(jnp.bfloat16)
    rest = time_bias - high.astype(jnp.float32)
    middle = rest.astype(jnp.bfloat16)
    lowest = (rest - middle.astype(jnp.float32)).astype(jnp.bfloat16)
    pieces = jnp.einsum(
        "phb,qkb->phqk",
        jnp.stack([high, middle, lowest]),
        bucket_hot,
        preferred_element_type=jnp.float32,
    )
    return pieces[0] + pieces[1] + pieces[2]


def tile_scores(query_heads, key_heads, query_info, key_info, rel_bias, time_bias):
    query_pos, query_member, query_count, query_stamp = query_info
    key_pos, key_member, key_stamp = key_info
    distance = query_pos[:, None] - key_pos[None, :]
    time_index = jnp.clip(query_stamp[:, None] - key_stamp[None, :], 0, time_bias.shape[1] - 1)
    bucket_hot = (
        time_index[:, :, None] == jnp.arange(time_bias.shape[1], dtype=jnp.int32)[None, None, :]
    ).astype(jnp.bfloat16)
    scores = jnp.einsum(
        "qhd,khd->hqk", query_heads, key_heads, preferred_element_type=jnp.float32
    ) * DH ** (-0.5)
    scores = (
        scores
        + diagonal_bias(rel_bias, query_pos[0], key_pos[0], query_pos.shape[0], key_pos.shape[0])
        + bucket_lookup(time_bias, bucket_hot)
    )
    allowed = (
        (query_member[:, None] == key_member[None, :])
        & (query_member[:, None] < SEQ_GRP)
        & (distance >= 0)
    )[None]
    weights = (jnp.where(allowed, jax.nn.silu(scores), 0.0) / query_count[None, :, None]).astype(
        jnp.bfloat16
    )
    return (scores, allowed, weights, bucket_hot)


def score_grads(grad_weights, scores, allowed, query_count):
    return (
        jnp.where(allowed, grad_weights / query_count[None, :, None], 0.0) * silu_slope(scores)
    ).astype(jnp.bfloat16)


def local_general(
    context,
    item_owner,
    item_offset,
    lengths,
    times,
    table,
    cotangent,
    ln_in_gain,
    w_uvqk,
    b_uvqk,
    rel_bias,
    time_bias,
    ln_out_gain,
    w_out,
    b_out,
):
    owners = lax.axis_size(("pb", "ka"))
    row_count = context.shape[0]
    width = context.shape[1]
    capacity = max(2, 2 * row_count // owners)
    owner_ids = item_owner[:, 0]
    owner_hits = (owner_ids[:, None] == jnp.arange(owners, dtype=jnp.int32)[None, :]).astype(
        jnp.int32
    )
    earlier = jnp.sum((jnp.cumsum(owner_hits, axis=0) - owner_hits) * owner_hits, axis=1)
    slot_index = owner_ids * capacity + earlier
    requests = jnp.zeros((owners * capacity,), jnp.int32).at[slot_index].set(item_offset + 1)
    arrived = lax.all_to_all(
        requests.reshape(owners, capacity), ("pb", "ka"), split_axis=0, concat_axis=0, tiled=True
    ).reshape(-1)
    present = arrived > 0
    local_rows = jnp.maximum(arrived - 1, 0)
    fetched = jnp.where(present[:, None], table[local_rows], jnp.zeros((), jnp.bfloat16))
    returned = lax.all_to_all(
        fetched.reshape(owners, capacity, width),
        ("pb", "ka"),
        split_axis=0,
        concat_axis=0,
        tiled=True,
    )
    embedded = returned.reshape(owners * capacity, width)[slot_index]
    start = context.astype(jnp.float32) + embedded.astype(jnp.float32)
    group = lax.axis_size("ka") * TOK_DEV
    block_start = lax.axis_index("ka") * TOK_DEV
    half_cols = w_out.shape[0]
    heads = half_cols // DH
    full_cols = half_cols * lax.axis_size("ha")
    out_cols = width // lax.axis_size("ha")
    out_start = lax.axis_index("ha") * out_cols
    bias_half = lax.dynamic_slice_in_dim(b_out, out_start, out_cols)
    scale = DH ** (-0.5)
    grad_gain_in = jnp.zeros(ln_in_gain.shape, jnp.float32)
    grad_bias_proj = jnp.zeros(b_uvqk.shape, jnp.float32)
    grad_rel = jnp.zeros(rel_bias.shape, jnp.float32)
    grad_time = jnp.zeros(time_bias.shape, jnp.float32)
    grad_gain_out = jnp.zeros(ln_out_gain.shape, jnp.float32)
    grad_bias_out = jnp.zeros(b_out.shape, jnp.float32)
    weight_total = None
    mixed_parts = []
    grad_parts = []
    for micro in range(MB):
        w_full, w_final = (
            lax.all_gather(w_uvqk, "pb", axis=0, tiled=True),
            lax.all_gather(w_out, "pb", axis=1, tiled=True),
        )
        x_in = start[micro * TOK_DEV : (micro + 1) * TOK_DEV]
        cot_rows = cotangent[micro * TOK_DEV : (micro + 1) * TOK_DEV]
        stamps = times[0, micro]
        places, member, counted = stream_layout(lengths[0, micro], group)
        query_pos = lax.dynamic_slice_in_dim(places, block_start, TOK_DEV)
        query_member = lax.dynamic_slice_in_dim(member, block_start, TOK_DEV)
        query_count = lax.dynamic_slice_in_dim(counted, block_start, TOK_DEV)
        query_stamp = lax.dynamic_slice_in_dim(stamps, block_start, TOK_DEV)
        normed_float, unit_in, inverse_in = norm_rows(x_in, ln_in_gain)
        normed = normed_float.astype(jnp.bfloat16)
        pre_act = (
            jnp.einsum("td,dgc->tgc", normed, w_full, preferred_element_type=jnp.float32) + b_uvqk
        )
        activated = jax.nn.silu(pre_act)
        gate_part = activated[:, 0]
        values = activated[:, 1].astype(jnp.bfloat16)
        queries = activated[:, 2].astype(jnp.bfloat16)
        key_rows = activated[:, 3].astype(jnp.bfloat16)
        key_pair = lax.all_gather(jnp.stack([key_rows, values]), "ka", axis=1, tiled=True)
        all_keys = key_pair[0].reshape(group, heads, DH)
        all_values = key_pair[1].reshape(group, heads, DH)
        query_heads = queries.reshape(TOK_DEV, heads, DH)
        scores, allowed, weights, bucket_hot = tile_scores(
            query_heads,
            all_keys,
            (query_pos, query_member, query_count, query_stamp),
            (places, member, stamps),
            rel_bias,
            time_bias,
        )
        attended = jnp.einsum(
            "hqk,khd->qhd", weights, all_values, preferred_element_type=jnp.float32
        ).reshape(TOK_DEV, half_cols)
        row_total, row_square = lax.psum(
            (jnp.sum(attended, axis=1), jnp.sum(attended * attended, axis=1)), "ha"
        )
        row_mean = row_total / full_cols
        inverse_out = lax.rsqrt(row_square / full_cols - row_mean * row_mean + epsilon)[:, None]
        unit_out = (attended - row_mean[:, None]) * inverse_out
        mixed_in = (unit_out * ln_out_gain * gate_part).astype(jnp.bfloat16)
        partial_out = jnp.dot(mixed_in, w_final, preferred_element_type=jnp.float32)
        summed_out = lax.psum_scatter(partial_out, "ha", scatter_dimension=1, tiled=True)
        residual = lax.dynamic_slice_in_dim(x_in, out_start, out_cols, 1)
        mixed_parts.append((summed_out + bias_half + residual).astype(jnp.bfloat16))
        grad_final_part = jnp.einsum(
            "tc,td->cd", mixed_in, cot_rows, preferred_element_type=jnp.float32
        )
        grad_bias_out = grad_bias_out + jnp.sum(cot_rows.astype(jnp.float32), axis=0)
        grad_mixed = jnp.einsum("td,cd->tc", cot_rows, w_final, preferred_element_type=jnp.float32)
        grad_gate = grad_mixed * unit_out * ln_out_gain
        grad_gain_out = grad_gain_out + jnp.sum(grad_mixed * unit_out * gate_part, axis=0)
        grad_unit = grad_mixed * gate_part * ln_out_gain
        first_total, second_total = lax.psum(
            (jnp.sum(grad_unit, axis=1), jnp.sum(grad_unit * unit_out, axis=1)), "ha"
        )
        grad_attended = (
            inverse_out
            * (
                grad_unit
                - first_total[:, None] / full_cols
                - unit_out * second_total[:, None] / full_cols
            )
        ).astype(jnp.bfloat16)
        grad_heads = grad_attended.reshape(TOK_DEV, heads, DH)
        grad_weights = jnp.einsum(
            "qhd,khd->hqk", grad_heads, all_values, preferred_element_type=jnp.float32
        )
        grad_scores = score_grads(grad_weights, scores, allowed, query_count)
        grad_rel = grad_rel + diagonal_sums(grad_scores, query_pos[0], places[0], rel_bias.shape[1])
        grad_time = grad_time + jnp.einsum(
            "hqk,qkb->hb", grad_scores, bucket_hot, preferred_element_type=jnp.float32
        )
        grad_queries = (
            jnp.einsum("hqk,khd->qhd", grad_scores, all_keys, preferred_element_type=jnp.float32)
            * scale
        ).reshape(TOK_DEV, half_cols)
        key_part = (
            jnp.einsum("hqk,qhd->khd", grad_scores, query_heads, preferred_element_type=jnp.float32)
            * scale
        )
        value_part = jnp.einsum(
            "hqk,qhd->khd", weights, grad_heads, preferred_element_type=jnp.float32
        )
        stacked = jnp.stack(
            [key_part.reshape(group, half_cols), value_part.reshape(group, half_cols)]
        )
        owned_grads = lax.psum_scatter(stacked, "ka", scatter_dimension=1, tiled=True)
        grad_keys = owned_grads[0]
        grad_values = owned_grads[1]
        grad_act = jnp.stack([grad_gate, grad_values, grad_queries, grad_keys], axis=1)
        grad_pre = (grad_act * silu_slope(pre_act)).astype(jnp.bfloat16)
        grad_proj_part = jnp.einsum(
            "td,tgc->dgc", normed, grad_pre, preferred_element_type=jnp.float32
        )
        grad_bias_proj = grad_bias_proj + jnp.sum(grad_pre.astype(jnp.float32), axis=0)
        grad_normed = lax.psum(
            jnp.einsum("tgc,dgc->td", grad_pre, w_full, preferred_element_type=jnp.float32), "ha"
        )
        grad_gain_in = grad_gain_in + jnp.sum(grad_normed * unit_in, axis=0)
        grad_parts.append(
            cot_rows.astype(jnp.float32) + norm_back(grad_normed * ln_in_gain, unit_in, inverse_in)
        )
        local_pair = (grad_proj_part, grad_final_part)
        local_pair = (
            lax.psum_scatter(local_pair[0], ("pb", "ka"), scatter_dimension=0, tiled=True),
            lax.psum_scatter(local_pair[1], ("pb", "ka"), scatter_dimension=1, tiled=True),
        )
        weight_total = (
            local_pair if weight_total is None else jax.tree.map(jnp.add, weight_total, local_pair)
        )
    grad_start = jnp.concatenate(grad_parts, axis=0)
    outgoing = jnp.zeros((owners * capacity, width), jnp.float32).at[slot_index].set(grad_start)
    incoming = lax.all_to_all(
        outgoing.reshape(owners, capacity, width),
        ("pb", "ka"),
        split_axis=0,
        concat_axis=0,
        tiled=True,
    ).reshape(owners * capacity, width)
    table_grad = jax.ops.segment_sum(
        jnp.where(present[:, None], incoming, 0.0), local_rows, num_segments=table.shape[0]
    )
    small_total = lax.psum(
        (grad_gain_in, grad_bias_proj, grad_rel, grad_time, grad_gain_out, grad_bias_out),
        ("pb", "ka"),
    )
    mixed = jnp.concatenate(mixed_parts, axis=0)
    return (
        mixed,
        grad_start.astype(jnp.bfloat16),
        table_grad,
        small_total[0],
        weight_total[0],
        small_total[1],
        small_total[2],
        small_total[3],
        small_total[4],
        weight_total[1],
        small_total[5],
    )


def mm(a, b):
    return jnp.dot(a, b, preferred_element_type=F32)


def mm_nt(a, b):
    return lax.dot_general(a, b, (((1,), (1,)), ((), ())), preferred_element_type=F32)


def mm_tn(a, b):
    return lax.dot_general(a, b, (((0,), (0,)), ((), ())), preferred_element_type=F32)


def sigmoid(v):
    return 0.5 * jnp.tanh(0.5 * v) + 0.5


def layer_kernel(
    lengths_ref, times_ref, emb_ref, ctx_ref, cot_ref, w_ref, wout_ref, small_ref, gain_in_ref, bout_ref,
    mixed_ref, grad_start_ref, grad_w_ref, grad_small_ref,
    slope_ref, qkv_ref, w_att_ref, sm_ref, gs_ref, grad_pre_ref, att_ref,
):
    group, width = ctx_ref.shape
    half = width // 2
    lane = lax.broadcasted_iota(jnp.int32, (group, group), 1)
    row = lax.broadcasted_iota(jnp.int32, (group, group), 0)
    ends = []
    total = jnp.int32(0)
    for i in range(SEQ_GRP):
        total = total + lengths_ref[i]
        ends.append(total)
    member_row = jnp.zeros((group, group), jnp.int32)
    member_col = jnp.zeros((group, group), jnp.int32)
    for i in range(SEQ_GRP):
        member_row = member_row + (ends[i] <= row).astype(jnp.int32)
        member_col = member_col + (ends[i] <= lane).astype(jnp.int32)
    inv_count = jnp.zeros((group, group), F32)
    for i in range(SEQ_GRP):
        count = jnp.maximum(lengths_ref[i], 1).astype(F32)
        inv_count = jnp.where(member_row == i, 1.0 / jnp.full((group, group), count, F32), inv_count)
    allowed = (member_row == member_col) & (member_row < SEQ_GRP) & (lane <= row)
    maskscale = jnp.where(allowed, inv_count, 0.0)
    times_row = jnp.broadcast_to(times_ref[...], (group, group))
    times_col = jnp.sum(jnp.where(lane == row, times_row, 0).astype(F32), axis=1, keepdims=True).astype(jnp.int32)
    buckets = small_ref.shape[2] // 2
    time_index = jnp.clip(times_col - times_row, 0, buckets - 1)
    hot_cols = (times_row == row).astype(F32).astype(BF16)

    start = ctx_ref[...].astype(F32) + jnp.concatenate(
        [
            emb_ref[0].astype(F32) + emb_ref[1].astype(F32),
            emb_ref[2].astype(F32) + emb_ref[3].astype(F32),
        ],
        axis=0,
    )
    centered = start - jnp.mean(start, axis=1, keepdims=True)
    inv_in = lax.rsqrt(jnp.mean(centered * centered, axis=1, keepdims=True) + epsilon)
    unit_in = centered * inv_in
    normed = (unit_in * gain_in_ref[...]).astype(BF16)

    gates = []
    for hf in range(2):
        for g in range(4):
            cols = slice(g * half, (g + 1) * half)
            pre = mm(normed, w_ref[hf, :, cols]) + small_ref[hf, g : g + 1, :]
            sig = sigmoid(pre)
            act = pre * sig
            slope_ref[hf, :, cols] = sig + act * (1.0 - sig)
            if g == 0:
                gates.append(act)
            elif g == 2:
                qkv_ref[hf, 1] = (act * 0.125).astype(BF16).astype(BF16)
            else:
                qkv_ref[hf, {1: 0, 3: 2}[g]] = act.astype(BF16)
    gate = jnp.concatenate(gates, axis=1)

    lane_pair = lax.broadcasted_iota(jnp.int32, (group, 128), 1)
    low_half = lane_pair < 64

    def split(tile):
        zero = jnp.zeros_like(tile)
        return jnp.where(low_half, tile, zero), jnp.where(low_half, zero, tile)

    for hf in range(2):
        for pair in range(half // 128):
            cols = slice(pair * 128, (pair + 1) * 128)
            values = split(qkv_ref[hf, 0, :, cols])
            queries = split(qkv_ref[hf, 1, :, cols])
            keys = qkv_ref[hf, 2, :, cols]
            attended = None
            for sub in range(2):
                head_in = pair * 2 + sub
                head = hf * (half // 64) + head_in
                rel = pltpu.roll(
                    jnp.broadcast_to(small_ref[hf, 4 + head_in : 5 + head_in, :], (group, group)),
                    0, 1, stride=1, stride_axis=0,
                )
                table = small_ref[hf, 8 + head_in // 2 : 9 + head_in // 2, (head_in % 2) * buckets : (head_in % 2 + 1) * buckets]
                table = jnp.broadcast_to(table, (group, buckets))
                scores = mm_nt(queries[sub], keys) + rel + jnp.concatenate(
                    [
                        jnp.take_along_axis(table, time_index[:, c : c + buckets], axis=1, mode="promise_in_bounds")
                        for c in range(0, group, buckets)
                    ],
                    axis=1,
                )
                sig = sigmoid(scores)
                act = scores * sig
                weights = (act * maskscale).astype(BF16)
                w_att_ref[head] = weights
                sm_ref[head] = (sig + act * (1.0 - sig)) * maskscale
                part = mm(weights, values[sub])
                attended = part if attended is None else attended + part
            att_ref[:, hf * half + pair * 128 : hf * half + (pair + 1) * 128] = attended

    attended = att_ref[...]
    centered = attended - jnp.mean(attended, axis=1, keepdims=True)
    inv_out = lax.rsqrt(jnp.mean(centered * centered, axis=1, keepdims=True) + epsilon)
    unit_out = centered * inv_out
    gain_out = jnp.concatenate([small_ref[0, 10:11, :], small_ref[1, 10:11, :]], axis=1)
    mixed_in = (unit_out * gain_out * gate).astype(BF16)
    mixed_ref[...] = (mm(mixed_in, wout_ref[...]) + bout_ref[...] + start).astype(BF16)
    cot = cot_ref[...]
    grad_mixed = mm_nt(cot, wout_ref[...])
    for hf in range(2):
        grad_w_ref[hf, :, 4 * half : 5 * half] = mm_tn(cot, mixed_in[:, hf * half : (hf + 1) * half]).astype(grad_w_ref.dtype)
    grad_unit_raw = grad_mixed * unit_out
    grad_gate = grad_unit_raw * gain_out
    grad_gain_out = jnp.sum(grad_unit_raw * gate, axis=0, keepdims=True)
    grad_unit = grad_mixed * gate * gain_out
    first = jnp.mean(grad_unit, axis=1, keepdims=True)
    second = jnp.mean(grad_unit * unit_out, axis=1, keepdims=True)
    grad_att = (inv_out * (grad_unit - first - unit_out * second)).astype(BF16)
    for hf in range(2):
        cols = slice(hf * half, (hf + 1) * half)
        grad_pre_ref[hf, :, 0:half] = (grad_gate[:, cols] * slope_ref[hf, :, 0:half]).astype(BF16)
        grad_small_ref[hf, 10:11, :] = grad_gain_out[:, cols]

    for hf in range(2):
        for pair in range(half // 128):
            cols = slice(pair * 128, (pair + 1) * 128)
            values = qkv_ref[hf, 0, :, cols]
            queries = split(qkv_ref[hf, 1, :, cols])
            keys = split(qkv_ref[hf, 2, :, cols])
            grads = split(grad_att[:, hf * half + pair * 128 : hf * half + (pair + 1) * 128])
            sums = None
            for sub in range(2):
                head_in = pair * 2 + sub
                head = hf * (half // 64) + head_in
                grad_scores = (mm_nt(grads[sub], values) * sm_ref[head]).astype(BF16)
                gs_ref[:, head * group : (head + 1) * group] = grad_scores
                parts = (
                    mm_tn(w_att_ref[head], grads[sub]),
                    mm(grad_scores, keys[sub]),
                    mm_tn(grad_scores, queries[sub]),
                )
                sums = parts if sums is None else [a + b for a, b in zip(sums, parts)]
            for g, part in ((1, sums[0]), (2, sums[1] * 0.125), (3, sums[2])):
                place = slice(g * half + pair * 128, g * half + (pair + 1) * 128)
                grad_pre_ref[hf, :, place] = (part * slope_ref[hf, :, place]).astype(BF16)

    flip = (lane + row == group - 1).astype(F32)
    kept_pairs = lane + row <= group - 1
    hot_back = (times_row == group - 1 - row).astype(F32).astype(BF16)
    folded = mm(jnp.concatenate([flip.astype(BF16), hot_back], axis=0), gs_ref[...])
    rel_rows = []
    time_rows = []
    early_rows = []
    for head in range(2 * (half // 64)):
        places = slice(head * group, (head + 1) * group)
        rel_rows.append(jnp.sum(skew(folded[:group, places]), axis=0, keepdims=True))
        both = mm_nt(folded[group:, places].astype(BF16), hot_cols)
        kept = jnp.where(kept_pairs, both, 0.0)
        time_rows.append(jnp.sum(skew(kept), axis=0, keepdims=True))
        early_rows.append(jnp.sum(both - kept, axis=0, keepdims=True))
    flipped = jnp.dot(jnp.concatenate(rel_rows + time_rows, axis=0), flip, preferred_element_type=F32, precision=lax.Precision.HIGHEST)
    early = jnp.sum(jnp.concatenate(early_rows, axis=0), axis=1, keepdims=True)
    heads = 2 * (half // 64)
    first_lane = lax.broadcasted_iota(jnp.int32, (heads, buckets), 1) == 0
    last_lane = lax.broadcasted_iota(jnp.int32, (heads, buckets), 1) == buckets - 1
    times_flipped = flipped[heads:]
    late = jnp.sum(times_flipped[:, buckets:], axis=1, keepdims=True)
    time_grad = times_flipped[:, :buckets] + jnp.where(first_lane, early, 0.0) + jnp.where(last_lane, late, 0.0)
    for hf in range(2):
        for head_in in range(half // 64):
            head = hf * (half // 64) + head_in
            grad_small_ref[hf, 4 + head_in : 5 + head_in, :] = flipped[head : head + 1]
            grad_small_ref[hf, 8 + head_in // 2 : 9 + head_in // 2, (head_in % 2) * buckets : (head_in % 2 + 1) * buckets] = time_grad[head : head + 1]

    grad_normed = None
    for hf in range(2):
        grad_pre = grad_pre_ref[hf]
        part = mm_nt(grad_pre, w_ref[hf])
        grad_normed = part if grad_normed is None else grad_normed + part
    grad_unit_in = grad_normed * gain_in_ref[...]
    first = jnp.mean(grad_unit_in, axis=1, keepdims=True)
    second = jnp.mean(grad_unit_in * unit_in, axis=1, keepdims=True)
    cot32 = cot.astype(F32)
    grad_start_ref[...] = (cot32 + inv_in * (grad_unit_in - first - unit_in * second)).astype(BF16)
    gain_grad = jnp.sum(grad_normed * unit_in, axis=0, keepdims=True)
    bout_grad = jnp.sum(cot32, axis=0, keepdims=True)
    for hf in range(2):
        grad_pre = grad_pre_ref[hf]
        sums = jnp.sum(grad_pre.astype(F32), axis=0, keepdims=True)
        for g in range(4):
            grad_small_ref[hf, g : g + 1, :] = sums[:, g * half : (g + 1) * half]
            grad_w_ref[hf, :, g * half : (g + 1) * half] = mm_tn(normed, grad_pre[:, g * half : (g + 1) * half]).astype(grad_w_ref.dtype)
        grad_small_ref[hf, 11:12, :] = gain_grad[:, hf * half : (hf + 1) * half]
        grad_small_ref[hf, 12:13, :] = bout_grad[:, hf * half : (hf + 1) * half]
        grad_small_ref[hf, 13:16, :] = jnp.zeros((3, half), F32)


def skew(tile):
    return pltpu.roll(tile, 0, 1, stride=1, stride_axis=0)


def layer(lengths, times, emb, ctx, cot, w, wout, small, gain_in, bout, grad_dtype=F32):
    group, width = ctx.shape
    half = width // 2
    heads = width // 64
    vmem = pl.BlockSpec(memory_space=pltpu.VMEM)
    return pl.pallas_call(
        layer_kernel,
        out_shape=(
            jax.ShapeDtypeStruct((group, width), BF16),
            jax.ShapeDtypeStruct((group, width), BF16),
            jax.ShapeDtypeStruct((2, width, 5 * half), grad_dtype),
            jax.ShapeDtypeStruct((2, 16, half), F32),
        ),
        in_specs=[pl.BlockSpec(memory_space=pltpu.SMEM)] + [vmem] * 9,
        out_specs=(vmem,) * 4,
        scratch_shapes=[
            pltpu.VMEM((2, group, 4 * half), F32),
            pltpu.VMEM((2, 3, group, half), BF16),
            pltpu.VMEM((heads, group, group), BF16),
            pltpu.VMEM((heads, group, group), F32),
            pltpu.VMEM((group, heads * group), BF16),
            pltpu.VMEM((2, group, 4 * half), BF16),
            pltpu.VMEM((group, width), F32),
        ],
        compiler_params=pltpu.CompilerParams(vmem_limit_bytes=56 * 1024 * 1024),
    )(lengths, times, emb, ctx, cot, w, wout, small, gain_in, bout)


def gather_kernel(ids_ref, table_ref, out_ref, total):
    step = pl.program_id(0)
    rows = table_ref.shape[0]
    lane = lax.broadcasted_iota(jnp.int32, (ids_ref.shape[0], rows), 1) + step * rows
    hot = (ids_ref[...] == lane).astype(F32).astype(BF16)
    part = mm(hot, table_ref[...])

    @pl.when(step == 0)
    def _():
        total[...] = part

    @pl.when(step > 0)
    def _():
        total[...] += part

    @pl.when(step == pl.num_programs(0) - 1)
    def _():
        out_ref[...] = total[...].astype(BF16)


def gather_rows(ids, table, tile=1024):
    count, width = ids.shape[0], table.shape[1]
    return pl.pallas_call(
        gather_kernel,
        grid=(table.shape[0] // tile,),
        out_shape=jax.ShapeDtypeStruct((count, width), BF16),
        in_specs=[
            pl.BlockSpec((count, 1), lambda i: (0, 0)),
            pl.BlockSpec((tile, width), lambda i: (i, 0)),
        ],
        out_specs=pl.BlockSpec((count, width), lambda i: (0, 0)),
        scratch_shapes=[pltpu.VMEM((count, width), F32)],
        compiler_params=pltpu.CompilerParams(vmem_limit_bytes=40 * 1024 * 1024),
    )(ids, table)


def scatter_kernel(ids_ref, rows_ref, out_ref):
    tile = out_ref.shape[0]
    row = lax.broadcasted_iota(jnp.int32, (tile, ids_ref.shape[1]), 0) + pl.program_id(0) * tile
    hot = (ids_ref[...] == row).astype(F32).astype(BF16)
    out_ref[...] = mm(hot, rows_ref[...])


def scatter_rows(ids, rows, table_rows, tile=512):
    count, width = rows.shape
    return pl.pallas_call(
        scatter_kernel,
        grid=(table_rows // tile,),
        out_shape=jax.ShapeDtypeStruct((table_rows, width), F32),
        in_specs=[
            pl.BlockSpec((1, count), lambda i: (0, 0)),
            pl.BlockSpec((count, width), lambda i: (0, 0)),
        ],
        out_specs=pl.BlockSpec((tile, width), lambda i: (i, 0)),
        compiler_params=pltpu.CompilerParams(vmem_limit_bytes=40 * 1024 * 1024),
    )(ids, rows)


def local_streams(
    context,
    item_owner,
    item_offset,
    lengths,
    times,
    table,
    cotangent,
    ln_in_gain,
    w_uvqk,
    b_uvqk,
    rel_bias,
    time_bias,
    ln_out_gain,
    w_out,
    b_out,
):
    owners = lax.axis_size(("pb", "ka"))
    pbs = lax.axis_size("pb")
    row_count, width = context.shape
    half = width // 2
    group = 2 * TOK_DEV
    capacity = max(2, 2 * row_count // owners)
    share = capacity // 2
    ka = lax.axis_index("ka")
    ha = lax.axis_index("ha")
    stream = 2 * ka + ha
    owner_ids = item_owner[:, 0]
    owner_hits = (owner_ids[:, None] == jnp.arange(owners, dtype=jnp.int32)[None, :]).astype(jnp.int32)
    earlier = jnp.sum((jnp.cumsum(owner_hits, axis=0) - owner_hits) * owner_hits, axis=1)
    slot_index = owner_ids * capacity + earlier
    requests = jnp.full((owners * capacity,), -1, jnp.int32).at[slot_index].set(item_offset)
    arrived = lax.all_to_all(
        requests.reshape(owners, capacity), ("pb", "ka"), split_axis=0, concat_axis=0, tiled=True
    )
    mine = lax.dynamic_slice_in_dim(arrived, ha * share, share, 1).reshape(owners * share, 1)
    fetched = gather_rows(mine, table).reshape(owners, share, width)
    returned = lax.all_to_all(fetched, ("pb", "ka"), split_axis=0, concat_axis=0, tiled=True)
    returned = returned.reshape(owners * share, width)
    place = earlier - ha * share
    place = jnp.where((place >= 0) & (place < share), owner_ids * share + place, -1)
    hot = (place[:, None] == jnp.arange(owners * share, dtype=jnp.int32)[None, :]).astype(BF16)
    embedded = jnp.dot(hot, returned, preferred_element_type=F32).astype(BF16)
    emb = lax.all_to_all(
        embedded.reshape(MB, TOK_DEV, width), ("ka", "ha"), split_axis=0, concat_axis=0, tiled=True
    )

    def both_halves(array):
        away = lax.dynamic_slice_in_dim(array, (2 * (1 - ka) + ha) * TOK_DEV, TOK_DEV, 0)
        own = lax.dynamic_slice_in_dim(array, stream * TOK_DEV, TOK_DEV, 0)
        other = lax.ppermute(away, "ka", [(0, 1), (1, 0)])
        first = jnp.where(ka == 0, own, other)
        second = jnp.where(ka == 0, other, own)
        return jnp.concatenate([first, second], axis=0)

    ctx = both_halves(context)
    cot = both_halves(cotangent)
    w_full = lax.all_gather(w_uvqk.reshape(w_uvqk.shape[0], 4 * half), ("ha", "pb"), axis=0, tiled=True)
    w_full = w_full.reshape(2, width, 4 * half)
    w_final = lax.all_gather(w_out, "pb", axis=1, tiled=True)
    w_final = lax.all_gather(w_final, "ha", axis=0, tiled=True)
    small = jnp.concatenate(
        [
            b_uvqk,
            jnp.roll(rel_bias[:, ::-1], 1, axis=1),
            time_bias.reshape(2, half),
            ln_out_gain.reshape(1, half),
        ],
        axis=0,
    )
    small = lax.all_gather(small, "ha", axis=0)
    mixed, grad_start, grad_w, grad_small = layer(
        lax.dynamic_index_in_dim(lengths[0], stream, 0, False),
        lax.dynamic_slice_in_dim(times[0], stream, 1, 0),
        emb,
        ctx,
        cot,
        w_full,
        w_final,
        small,
        ln_in_gain.reshape(1, width),
        b_out.reshape(1, width),
    )
    mixed_out = lax.all_to_all(
        mixed.reshape(2, TOK_DEV, 2, half).transpose(0, 2, 1, 3).reshape(4, TOK_DEV, half),
        ("ka", "ha"), split_axis=0, concat_axis=0, tiled=True,
    ).reshape(row_count, half)
    grad_rows = lax.all_to_all(
        jnp.broadcast_to(grad_start.reshape(2, 1, TOK_DEV, width), (2, 2, TOK_DEV, width)).reshape(4, TOK_DEV, width),
        ("ka", "ha"), split_axis=0, concat_axis=0, tiled=True,
    ).reshape(row_count, width)
    outgoing = lax.dot_general(hot, grad_rows, (((0,), (0,)), ((), ())), preferred_element_type=F32).astype(BF16)
    incoming = lax.all_to_all(
        outgoing.reshape(owners, share, width), ("pb", "ka"), split_axis=0, concat_axis=0, tiled=True
    ).reshape(owners * share, width)
    incoming = lax.all_gather(incoming, "ha", axis=0, tiled=True)
    ids = arrived.reshape(owners, 2, share).transpose(1, 0, 2).reshape(1, 2 * owners * share)
    table_grad = scatter_rows(ids, incoming, table.shape[0])
    grad_w = lax.psum_scatter(grad_w, "ha", scatter_dimension=0, tiled=True)
    grad_w = lax.psum_scatter(grad_w[0], ("pb", "ka"), scatter_dimension=0, tiled=True)
    grad_small = lax.psum(grad_small, ("pb", "ka", "ha"))
    mine = lax.dynamic_index_in_dim(grad_small, ha, 0, False)
    return (
        mixed_out,
        grad_rows,
        table_grad,
        grad_small[:, 11].reshape(width),
        grad_w[:, : 4 * half].reshape(-1, 4, half),
        mine[0:4],
        mine[4:8],
        mine[8:10].reshape(4, half // 2),
        mine[10],
        grad_w[:, 4 * half :].T,
        grad_small[:, 12].reshape(width),
    )


def solution(mesh):
    one_stream = mesh.shape["ka"] * mesh.shape["ha"] == MB and mesh.shape["ka"] == 2
    return jax.shard_map(
        local_streams if one_stream else local_general,
        mesh=mesh,
        in_specs=(
            P(("pb", "ka"), None),
            P(("pb", "ka"), None),
            P(("pb", "ka")),
            P("pb", None, None),
            P("pb", None, None),
            P(("pb", "ka"), None),
            P(("pb", "ka"), None),
            P(),
            P("pb", None, "ha"),
            P(None, "ha"),
            P("ha", None),
            P("ha", None),
            P("ha"),
            P("ha", "pb"),
            P(),
        ),
        out_specs=(
            P(("pb", "ka"), "ha"),
            P(("pb", "ka"), None),
            P(("pb", "ka"), None),
            P(),
            P(("pb", "ka"), None, "ha"),
            P(None, "ha"),
            P("ha", None),
            P("ha", None),
            P("ha"),
            P("ha", ("pb", "ka")),
            P(),
        ),
        check_vma=False,
    )
```

```python
import functools

import jax
import jax.numpy as jnp
from jax import lax
from jax.experimental import pallas as pl
from jax.experimental.pallas import tpu as pltpu
from jax.sharding import PartitionSpec as P

DH = 64
TOK_DEV = 128
MB = 4
SEQ_GRP = 4
F32 = jnp.float32
BF16 = jnp.bfloat16


epsilon = 1e-05


def silu_slope(values):
    sigma = jax.nn.sigmoid(values)
    return sigma * (1.0 + values * (1.0 - sigma))


def norm_rows(values, gain):
    centered = values - jnp.mean(values, axis=-1, keepdims=True)
    inverse = lax.rsqrt(jnp.mean(centered * centered, axis=-1, keepdims=True) + epsilon)
    unit_rows = centered * inverse
    return (unit_rows * gain, unit_rows, inverse)


def norm_back(grad_unit, unit_rows, inverse):
    first_mean = jnp.mean(grad_unit, axis=-1, keepdims=True)
    second_mean = jnp.mean(grad_unit * unit_rows, axis=-1, keepdims=True)
    return inverse * (grad_unit - first_mean - unit_rows * second_mean)


def stream_layout(lengths_row, group):
    places = jnp.arange(group, dtype=jnp.int32)
    ends = jnp.cumsum(lengths_row, dtype=jnp.int32)
    member = jnp.sum((ends[None, :] <= places[:, None]).astype(jnp.int32), axis=1)
    onehot = (member[:, None] == jnp.arange(SEQ_GRP, dtype=jnp.int32)[None, :]).astype(jnp.float32)
    counted = jnp.maximum(jnp.sum(onehot * lengths_row.astype(jnp.float32)[None, :], axis=1), 1.0)
    return (places, member, counted)


def diagonal_bias(rel_bias, query_first, key_first, query_len, key_len):
    heads, group = rel_bias.shape
    span = query_len + key_len - 1
    padded = jnp.concatenate([jnp.zeros((heads, group), jnp.float32), rel_bias], axis=1)
    window = lax.dynamic_slice_in_dim(
        padded, query_first - key_first - key_len + 1 + group, span, 1
    )
    flipped = jnp.concatenate([window[:, ::-1], jnp.zeros((heads, 1), jnp.float32)], axis=1)
    skewed = jnp.tile(flipped, (1, query_len))[:, : query_len * span].reshape(
        heads, query_len, span
    )
    return skewed[:, :, query_len - 1 : query_len - 1 + key_len]


def diagonal_sums(grad_scores, query_first, key_first, group):
    heads, query_len, key_len = grad_scores.shape
    span = query_len + key_len - 1
    widened = jnp.pad(grad_scores.astype(jnp.float32), ((0, 0), (0, 0), (query_len - 1, 0)))
    flat = jnp.pad(widened.reshape(heads, query_len * span), ((0, 0), (0, query_len)))
    totals = jnp.sum(flat.reshape(heads, query_len, span + 1), axis=1)
    window = totals[:, :span][:, ::-1]
    placed = lax.dynamic_update_slice_in_dim(
        jnp.zeros((heads, 2 * group), jnp.float32),
        window,
        query_first - key_first - key_len + 1 + group,
        1,
    )
    return placed[:, group:]


def bucket_lookup(time_bias, bucket_hot):
    high = time_bias.astype(jnp.bfloat16)
    rest = time_bias - high.astype(jnp.float32)
    middle = rest.astype(jnp.bfloat16)
    lowest = (rest - middle.astype(jnp.float32)).astype(jnp.bfloat16)
    pieces = jnp.einsum(
        "phb,qkb->phqk",
        jnp.stack([high, middle, lowest]),
        bucket_hot,
        preferred_element_type=jnp.float32,
    )
    return pieces[0] + pieces[1] + pieces[2]


def tile_scores(query_heads, key_heads, query_info, key_info, rel_bias, time_bias):
    query_pos, query_member, query_count, query_stamp = query_info
    key_pos, key_member, key_stamp = key_info
    distance = query_pos[:, None] - key_pos[None, :]
    time_index = jnp.clip(query_stamp[:, None] - key_stamp[None, :], 0, time_bias.shape[1] - 1)
    bucket_hot = (
        time_index[:, :, None] == jnp.arange(time_bias.shape[1], dtype=jnp.int32)[None, None, :]
    ).astype(jnp.bfloat16)
    scores = jnp.einsum(
        "qhd,khd->hqk", query_heads, key_heads, preferred_element_type=jnp.float32
    ) * DH ** (-0.5)
    scores = (
        scores
        + diagonal_bias(rel_bias, query_pos[0], key_pos[0], query_pos.shape[0], key_pos.shape[0])
        + bucket_lookup(time_bias, bucket_hot)
    )
    allowed = (
        (query_member[:, None] == key_member[None, :])
        & (query_member[:, None] < SEQ_GRP)
        & (distance >= 0)
    )[None]
    weights = (jnp.where(allowed, jax.nn.silu(scores), 0.0) / query_count[None, :, None]).astype(
        jnp.bfloat16
    )
    return (scores, allowed, weights, bucket_hot)


def score_grads(grad_weights, scores, allowed, query_count):
    return (
        jnp.where(allowed, grad_weights / query_count[None, :, None], 0.0) * silu_slope(scores)
    ).astype(jnp.bfloat16)


def local_general(
    context,
    item_owner,
    item_offset,
    lengths,
    times,
    table,
    cotangent,
    ln_in_gain,
    w_uvqk,
    b_uvqk,
    rel_bias,
    time_bias,
    ln_out_gain,
    w_out,
    b_out,
):
    owners = lax.axis_size(("pb", "ka"))
    row_count = context.shape[0]
    width = context.shape[1]
    capacity = max(2, 2 * row_count // owners)
    owner_ids = item_owner[:, 0]
    owner_hits = (owner_ids[:, None] == jnp.arange(owners, dtype=jnp.int32)[None, :]).astype(
        jnp.int32
    )
    earlier = jnp.sum((jnp.cumsum(owner_hits, axis=0) - owner_hits) * owner_hits, axis=1)
    slot_index = owner_ids * capacity + earlier
    requests = jnp.zeros((owners * capacity,), jnp.int32).at[slot_index].set(item_offset + 1)
    arrived = lax.all_to_all(
        requests.reshape(owners, capacity), ("pb", "ka"), split_axis=0, concat_axis=0, tiled=True
    ).reshape(-1)
    present = arrived > 0
    local_rows = jnp.maximum(arrived - 1, 0)
    fetched = jnp.where(present[:, None], table[local_rows], jnp.zeros((), jnp.bfloat16))
    returned = lax.all_to_all(
        fetched.reshape(owners, capacity, width),
        ("pb", "ka"),
        split_axis=0,
        concat_axis=0,
        tiled=True,
    )
    embedded = returned.reshape(owners * capacity, width)[slot_index]
    start = context.astype(jnp.float32) + embedded.astype(jnp.float32)
    group = lax.axis_size("ka") * TOK_DEV
    block_start = lax.axis_index("ka") * TOK_DEV
    half_cols = w_out.shape[0]
    heads = half_cols // DH
    full_cols = half_cols * lax.axis_size("ha")
    out_cols = width // lax.axis_size("ha")
    out_start = lax.axis_index("ha") * out_cols
    bias_half = lax.dynamic_slice_in_dim(b_out, out_start, out_cols)
    scale = DH ** (-0.5)
    grad_gain_in = jnp.zeros(ln_in_gain.shape, jnp.float32)
    grad_bias_proj = jnp.zeros(b_uvqk.shape, jnp.float32)
    grad_rel = jnp.zeros(rel_bias.shape, jnp.float32)
    grad_time = jnp.zeros(time_bias.shape, jnp.float32)
    grad_gain_out = jnp.zeros(ln_out_gain.shape, jnp.float32)
    grad_bias_out = jnp.zeros(b_out.shape, jnp.float32)
    weight_total = None
    mixed_parts = []
    grad_parts = []
    for micro in range(MB):
        w_full, w_final = (
            lax.all_gather(w_uvqk, "pb", axis=0, tiled=True),
            lax.all_gather(w_out, "pb", axis=1, tiled=True),
        )
        x_in = start[micro * TOK_DEV : (micro + 1) * TOK_DEV]
        cot_rows = cotangent[micro * TOK_DEV : (micro + 1) * TOK_DEV]
        stamps = times[0, micro]
        places, member, counted = stream_layout(lengths[0, micro], group)
        query_pos = lax.dynamic_slice_in_dim(places, block_start, TOK_DEV)
        query_member = lax.dynamic_slice_in_dim(member, block_start, TOK_DEV)
        query_count = lax.dynamic_slice_in_dim(counted, block_start, TOK_DEV)
        query_stamp = lax.dynamic_slice_in_dim(stamps, block_start, TOK_DEV)
        normed_float, unit_in, inverse_in = norm_rows(x_in, ln_in_gain)
        normed = normed_float.astype(jnp.bfloat16)
        pre_act = (
            jnp.einsum("td,dgc->tgc", normed, w_full, preferred_element_type=jnp.float32) + b_uvqk
        )
        activated = jax.nn.silu(pre_act)
        gate_part = activated[:, 0]
        values = activated[:, 1].astype(jnp.bfloat16)
        queries = activated[:, 2].astype(jnp.bfloat16)
        key_rows = activated[:, 3].astype(jnp.bfloat16)
        key_pair = lax.all_gather(jnp.stack([key_rows, values]), "ka", axis=1, tiled=True)
        all_keys = key_pair[0].reshape(group, heads, DH)
        all_values = key_pair[1].reshape(group, heads, DH)
        query_heads = queries.reshape(TOK_DEV, heads, DH)
        scores, allowed, weights, bucket_hot = tile_scores(
            query_heads,
            all_keys,
            (query_pos, query_member, query_count, query_stamp),
            (places, member, stamps),
            rel_bias,
            time_bias,
        )
        attended = jnp.einsum(
            "hqk,khd->qhd", weights, all_values, preferred_element_type=jnp.float32
        ).reshape(TOK_DEV, half_cols)
        row_total, row_square = lax.psum(
            (jnp.sum(attended, axis=1), jnp.sum(attended * attended, axis=1)), "ha"
        )
        row_mean = row_total / full_cols
        inverse_out = lax.rsqrt(row_square / full_cols - row_mean * row_mean + epsilon)[:, None]
        unit_out = (attended - row_mean[:, None]) * inverse_out
        mixed_in = (unit_out * ln_out_gain * gate_part).astype(jnp.bfloat16)
        partial_out = jnp.dot(mixed_in, w_final, preferred_element_type=jnp.float32)
        summed_out = lax.psum_scatter(partial_out, "ha", scatter_dimension=1, tiled=True)
        residual = lax.dynamic_slice_in_dim(x_in, out_start, out_cols, 1)
        mixed_parts.append((summed_out + bias_half + residual).astype(jnp.bfloat16))
        grad_final_part = jnp.einsum(
            "tc,td->cd", mixed_in, cot_rows, preferred_element_type=jnp.float32
        )
        grad_bias_out = grad_bias_out + jnp.sum(cot_rows.astype(jnp.float32), axis=0)
        grad_mixed = jnp.einsum("td,cd->tc", cot_rows, w_final, preferred_element_type=jnp.float32)
        grad_gate = grad_mixed * unit_out * ln_out_gain
        grad_gain_out = grad_gain_out + jnp.sum(grad_mixed * unit_out * gate_part, axis=0)
        grad_unit = grad_mixed * gate_part * ln_out_gain
        first_total, second_total = lax.psum(
            (jnp.sum(grad_unit, axis=1), jnp.sum(grad_unit * unit_out, axis=1)), "ha"
        )
        grad_attended = (
            inverse_out
            * (
                grad_unit
                - first_total[:, None] / full_cols
                - unit_out * second_total[:, None] / full_cols
            )
        ).astype(jnp.bfloat16)
        grad_heads = grad_attended.reshape(TOK_DEV, heads, DH)
        grad_weights = jnp.einsum(
            "qhd,khd->hqk", grad_heads, all_values, preferred_element_type=jnp.float32
        )
        grad_scores = score_grads(grad_weights, scores, allowed, query_count)
        grad_rel = grad_rel + diagonal_sums(grad_scores, query_pos[0], places[0], rel_bias.shape[1])
        grad_time = grad_time + jnp.einsum(
            "hqk,qkb->hb", grad_scores, bucket_hot, preferred_element_type=jnp.float32
        )
        grad_queries = (
            jnp.einsum("hqk,khd->qhd", grad_scores, all_keys, preferred_element_type=jnp.float32)
            * scale
        ).reshape(TOK_DEV, half_cols)
        key_part = (
            jnp.einsum("hqk,qhd->khd", grad_scores, query_heads, preferred_element_type=jnp.float32)
            * scale
        )
        value_part = jnp.einsum(
            "hqk,qhd->khd", weights, grad_heads, preferred_element_type=jnp.float32
        )
        stacked = jnp.stack(
            [key_part.reshape(group, half_cols), value_part.reshape(group, half_cols)]
        )
        owned_grads = lax.psum_scatter(stacked, "ka", scatter_dimension=1, tiled=True)
        grad_keys = owned_grads[0]
        grad_values = owned_grads[1]
        grad_act = jnp.stack([grad_gate, grad_values, grad_queries, grad_keys], axis=1)
        grad_pre = (grad_act * silu_slope(pre_act)).astype(jnp.bfloat16)
        grad_proj_part = jnp.einsum(
            "td,tgc->dgc", normed, grad_pre, preferred_element_type=jnp.float32
        )
        grad_bias_proj = grad_bias_proj + jnp.sum(grad_pre.astype(jnp.float32), axis=0)
        grad_normed = lax.psum(
            jnp.einsum("tgc,dgc->td", grad_pre, w_full, preferred_element_type=jnp.float32), "ha"
        )
        grad_gain_in = grad_gain_in + jnp.sum(grad_normed * unit_in, axis=0)
        grad_parts.append(
            cot_rows.astype(jnp.float32) + norm_back(grad_normed * ln_in_gain, unit_in, inverse_in)
        )
        local_pair = (grad_proj_part, grad_final_part)
        local_pair = (
            lax.psum_scatter(local_pair[0], ("pb", "ka"), scatter_dimension=0, tiled=True),
            lax.psum_scatter(local_pair[1], ("pb", "ka"), scatter_dimension=1, tiled=True),
        )
        weight_total = (
            local_pair if weight_total is None else jax.tree.map(jnp.add, weight_total, local_pair)
        )
    grad_start = jnp.concatenate(grad_parts, axis=0)
    outgoing = jnp.zeros((owners * capacity, width), jnp.float32).at[slot_index].set(grad_start)
    incoming = lax.all_to_all(
        outgoing.reshape(owners, capacity, width),
        ("pb", "ka"),
        split_axis=0,
        concat_axis=0,
        tiled=True,
    ).reshape(owners * capacity, width)
    table_grad = jax.ops.segment_sum(
        jnp.where(present[:, None], incoming, 0.0), local_rows, num_segments=table.shape[0]
    )
    small_total = lax.psum(
        (grad_gain_in, grad_bias_proj, grad_rel, grad_time, grad_gain_out, grad_bias_out),
        ("pb", "ka"),
    )
    mixed = jnp.concatenate(mixed_parts, axis=0)
    return (
        mixed,
        grad_start.astype(jnp.bfloat16),
        table_grad,
        small_total[0],
        weight_total[0],
        small_total[1],
        small_total[2],
        small_total[3],
        small_total[4],
        weight_total[1],
        small_total[5],
    )


def mm(a, b):
    return jnp.dot(a, b, preferred_element_type=F32)


def mm_nt(a, b):
    return lax.dot_general(a, b, (((1,), (1,)), ((), ())), preferred_element_type=F32)


def mm_tn(a, b):
    return lax.dot_general(a, b, (((0,), (0,)), ((), ())), preferred_element_type=F32)


def sigmoid(v):
    return 0.5 * jnp.tanh(0.5 * v) + 0.5


def layer_kernel(
    lengths_ref, times_ref, emb_ref, ctx_ref, cot_ref, w_ref, small_ref, gain_in_ref, bout_ref,
    mixed_ref, grad_start_ref, grad_w_ref, grad_small_ref,
    slope_ref, qkv_ref, w_att_ref, sm_ref, gs_ref, grad_pre_ref, att_ref,
):
    group, width = ctx_ref.shape
    half = width // 2
    lane = lax.broadcasted_iota(jnp.int32, (group, group), 1)
    row = lax.broadcasted_iota(jnp.int32, (group, group), 0)
    ends = []
    total = jnp.int32(0)
    for i in range(SEQ_GRP):
        total = total + lengths_ref[i]
        ends.append(total)
    member_row = jnp.zeros((group, group), jnp.int32)
    member_col = jnp.zeros((group, group), jnp.int32)
    for i in range(SEQ_GRP):
        member_row = member_row + (ends[i] <= row).astype(jnp.int32)
        member_col = member_col + (ends[i] <= lane).astype(jnp.int32)
    inv_count = jnp.zeros((group, group), F32)
    for i in range(SEQ_GRP):
        count = jnp.maximum(lengths_ref[i], 1).astype(F32)
        inv_count = jnp.where(member_row == i, 1.0 / jnp.full((group, group), count, F32), inv_count)
    allowed = (member_row == member_col) & (member_row < SEQ_GRP) & (lane <= row)
    maskscale = jnp.where(allowed, inv_count, 0.0)
    times_row = jnp.broadcast_to(times_ref[...], (group, group))
    times_col = jnp.sum(jnp.where(lane == row, times_row, 0).astype(F32), axis=1, keepdims=True).astype(jnp.int32)
    buckets = small_ref.shape[2] // 2
    time_index = jnp.clip(times_col - times_row, 0, buckets - 1)
    hot_cols = (times_row == row).astype(F32).astype(BF16)

    start = ctx_ref[...].astype(F32) + jnp.concatenate(
        [
            emb_ref[0].astype(F32) + emb_ref[1].astype(F32),
            emb_ref[2].astype(F32) + emb_ref[3].astype(F32),
        ],
        axis=0,
    )
    centered = start - jnp.mean(start, axis=1, keepdims=True)
    inv_in = lax.rsqrt(jnp.mean(centered * centered, axis=1, keepdims=True) + epsilon)
    unit_in = centered * inv_in
    normed = (unit_in * gain_in_ref[...]).astype(BF16)

    gates = []
    for hf in range(2):
        for g in range(4):
            cols = slice(g * half, (g + 1) * half)
            pre = mm(normed, w_ref[hf, :, cols]) + small_ref[hf, g : g + 1, :]
            sig = sigmoid(pre)
            act = pre * sig
            slope_ref[hf, :, cols] = sig + act * (1.0 - sig)
            if g == 0:
                gates.append(act)
            elif g == 2:
                qkv_ref[hf, 1] = (act * 0.125).astype(BF16)
            else:
                qkv_ref[hf, {1: 0, 3: 2}[g]] = act.astype(BF16)
    gate = jnp.concatenate(gates, axis=1)

    lane_pair = lax.broadcasted_iota(jnp.int32, (group, 128), 1)
    low_half = lane_pair < 64

    def split(tile):
        zero = jnp.zeros_like(tile)
        return jnp.where(low_half, tile, zero), jnp.where(low_half, zero, tile)

    turn = ((lane + row) % group == 0).astype(F32)
    rel_back = jnp.dot(
        jnp.concatenate([small_ref[0, 4:8, :], small_ref[1, 4:8, :]], axis=0),
        turn, preferred_element_type=F32, precision=lax.Precision.HIGHEST,
    )
    for hf in range(2):
        for pair in range(half // 128):
            cols = slice(pair * 128, (pair + 1) * 128)
            values = split(qkv_ref[hf, 0, :, cols])
            queries = split(qkv_ref[hf, 1, :, cols])
            keys = qkv_ref[hf, 2, :, cols]
            attended = None
            for sub in range(2):
                head_in = pair * 2 + sub
                head = hf * (half // 64) + head_in
                rel = skew(jnp.broadcast_to(rel_back[head : head + 1], (group, group)))
                table = small_ref[hf, 8 + head_in // 2 : 9 + head_in // 2, (head_in % 2) * buckets : (head_in % 2 + 1) * buckets]
                table = jnp.broadcast_to(table, (group, buckets))
                scores = mm_nt(queries[sub], keys) + rel + jnp.concatenate(
                    [
                        jnp.take_along_axis(table, time_index[:, c : c + buckets], axis=1, mode="promise_in_bounds")
                        for c in range(0, group, buckets)
                    ],
                    axis=1,
                )
                sig = sigmoid(scores)
                act = scores * sig
                weights = (act * maskscale).astype(BF16)
                w_att_ref[head] = weights
                sm_ref[head] = (sig + act * (1.0 - sig)) * maskscale
                part = mm(weights, values[sub])
                attended = part if attended is None else attended + part
            att_ref[:, hf * half + pair * 128 : hf * half + (pair + 1) * 128] = attended

    attended = att_ref[...]
    centered = attended - jnp.mean(attended, axis=1, keepdims=True)
    inv_out = lax.rsqrt(jnp.mean(centered * centered, axis=1, keepdims=True) + epsilon)
    unit_out = centered * inv_out
    gain_out = jnp.concatenate([small_ref[0, 10:11, :], small_ref[1, 10:11, :]], axis=1)
    mixed_in = (unit_out * gain_out * gate).astype(BF16)
    projected = None
    for hf in range(2):
        part = mm_nt(mixed_in[:, hf * half : (hf + 1) * half], w_ref[hf, :, 4 * half : 5 * half])
        projected = part if projected is None else projected + part
    mixed_ref[...] = (projected + bout_ref[...] + start).astype(BF16)
    cot = cot_ref[...]
    grad_mixed = jnp.concatenate([mm(cot, w_ref[hf, :, 4 * half : 5 * half]) for hf in range(2)], axis=1)
    blocks = grad_w_ref.shape[1:4]

    def put_grad_w(hf, g, value):
        grad_w_ref[hf, :, :, :, g * half : (g + 1) * half] = value.astype(BF16).reshape(blocks + (half,))

    for hf in range(2):
        put_grad_w(hf, 4, mm_tn(cot, mixed_in[:, hf * half : (hf + 1) * half]))
    grad_unit_raw = grad_mixed * unit_out
    grad_gate = grad_unit_raw * gain_out
    grad_gain_out = jnp.sum(grad_unit_raw * gate, axis=0, keepdims=True)
    grad_unit = grad_mixed * gate * gain_out
    first = jnp.mean(grad_unit, axis=1, keepdims=True)
    second = jnp.mean(grad_unit * unit_out, axis=1, keepdims=True)
    grad_att = (inv_out * (grad_unit - first - unit_out * second)).astype(BF16)
    for hf in range(2):
        cols = slice(hf * half, (hf + 1) * half)
        grad_pre_ref[hf, :, 0:half] = (grad_gate[:, cols] * slope_ref[hf, :, 0:half]).astype(BF16)
        grad_small_ref[hf, 10:11, :] = grad_gain_out[:, cols]

    for hf in range(2):
        for pair in range(half // 128):
            cols = slice(pair * 128, (pair + 1) * 128)
            values = qkv_ref[hf, 0, :, cols]
            queries = split(qkv_ref[hf, 1, :, cols])
            keys = split(qkv_ref[hf, 2, :, cols])
            grads = split(grad_att[:, hf * half + pair * 128 : hf * half + (pair + 1) * 128])
            sums = None
            for sub in range(2):
                head_in = pair * 2 + sub
                head = hf * (half // 64) + head_in
                grad_scores = (mm_nt(grads[sub], values) * sm_ref[head]).astype(BF16)
                gs_ref[:, head * group : (head + 1) * group] = grad_scores
                parts = (
                    mm_tn(w_att_ref[head], grads[sub]),
                    mm(grad_scores, keys[sub]),
                    mm_tn(grad_scores, queries[sub]),
                )
                sums = parts if sums is None else [a + b for a, b in zip(sums, parts)]
            for g, part in ((1, sums[0]), (2, sums[1] * 0.125), (3, sums[2])):
                place = slice(g * half + pair * 128, g * half + (pair + 1) * 128)
                grad_pre_ref[hf, :, place] = (part * slope_ref[hf, :, place]).astype(BF16)

    flip = (lane + row == group - 1).astype(F32)
    kept_pairs = lane + row <= group - 1
    hot_back = (times_row == group - 1 - row).astype(F32).astype(BF16)
    folded = mm(jnp.concatenate([flip.astype(BF16), hot_back], axis=0), gs_ref[...])
    rel_rows = []
    time_rows = []
    early_rows = []
    for head in range(2 * (half // 64)):
        places = slice(head * group, (head + 1) * group)
        rel_rows.append(jnp.sum(skew(folded[:group, places]), axis=0, keepdims=True))
        both = mm_nt(folded[group:, places].astype(BF16), hot_cols)
        kept = jnp.where(kept_pairs, both, 0.0)
        time_rows.append(jnp.sum(skew(kept), axis=0, keepdims=True))
        early_rows.append(jnp.sum(both - kept, axis=0, keepdims=True))
    flipped = jnp.dot(jnp.concatenate(rel_rows + time_rows, axis=0), flip, preferred_element_type=F32, precision=lax.Precision.HIGHEST)
    early = jnp.sum(jnp.concatenate(early_rows, axis=0), axis=1, keepdims=True)
    heads = 2 * (half // 64)
    first_lane = lax.broadcasted_iota(jnp.int32, (heads, buckets), 1) == 0
    last_lane = lax.broadcasted_iota(jnp.int32, (heads, buckets), 1) == buckets - 1
    times_flipped = flipped[heads:]
    late = jnp.sum(times_flipped[:, buckets:], axis=1, keepdims=True)
    time_grad = times_flipped[:, :buckets] + jnp.where(first_lane, early, 0.0) + jnp.where(last_lane, late, 0.0)
    for hf in range(2):
        for head_in in range(half // 64):
            head = hf * (half // 64) + head_in
            grad_small_ref[hf, 4 + head_in : 5 + head_in, :] = flipped[head : head + 1]
            grad_small_ref[hf, 8 + head_in // 2 : 9 + head_in // 2, (head_in % 2) * buckets : (head_in % 2 + 1) * buckets] = time_grad[head : head + 1]

    grad_normed = None
    for hf in range(2):
        grad_pre = grad_pre_ref[hf]
        part = mm_nt(grad_pre, w_ref[hf, :, 0 : 4 * half])
        grad_normed = part if grad_normed is None else grad_normed + part
    grad_unit_in = grad_normed * gain_in_ref[...]
    first = jnp.mean(grad_unit_in, axis=1, keepdims=True)
    second = jnp.mean(grad_unit_in * unit_in, axis=1, keepdims=True)
    cot32 = cot.astype(F32)
    grad_start_ref[...] = (cot32 + inv_in * (grad_unit_in - first - unit_in * second)).astype(BF16)
    gain_grad = jnp.sum(grad_normed * unit_in, axis=0, keepdims=True)
    bout_grad = jnp.sum(cot32, axis=0, keepdims=True)
    for hf in range(2):
        grad_pre = grad_pre_ref[hf]
        sums = jnp.sum(grad_pre.astype(F32), axis=0, keepdims=True)
        for g in range(4):
            grad_small_ref[hf, g : g + 1, :] = sums[:, g * half : (g + 1) * half]
            put_grad_w(hf, g, mm_tn(normed, grad_pre[:, g * half : (g + 1) * half]))
        grad_small_ref[hf, 11:12, :] = gain_grad[:, hf * half : (hf + 1) * half]
        grad_small_ref[hf, 12:13, :] = bout_grad[:, hf * half : (hf + 1) * half]
        grad_small_ref[hf, 13:16, :] = jnp.zeros((3, half), F32)


def skew(tile):
    return pltpu.roll(tile, 0, 1, stride=1, stride_axis=0)


def layer(lengths, times, emb, ctx, cot, w, small, gain_in, bout, grad_shape):
    group, width = ctx.shape
    half = width // 2
    heads = width // 64
    vmem = pl.BlockSpec(memory_space=pltpu.VMEM)
    return pl.pallas_call(
        layer_kernel,
        out_shape=(
            jax.ShapeDtypeStruct((group, width), BF16),
            jax.ShapeDtypeStruct((group, width), BF16),
            jax.ShapeDtypeStruct((2,) + grad_shape + (5 * half,), BF16),
            jax.ShapeDtypeStruct((2, 16, half), F32),
        ),
        in_specs=[pl.BlockSpec(memory_space=pltpu.SMEM)] + [vmem] * 8,
        out_specs=(vmem,) * 4,
        scratch_shapes=[
            pltpu.VMEM((2, group, 4 * half), F32),
            pltpu.VMEM((2, 3, group, half), BF16),
            pltpu.VMEM((heads, group, group), BF16),
            pltpu.VMEM((heads, group, group), F32),
            pltpu.VMEM((group, heads * group), BF16),
            pltpu.VMEM((2, group, 4 * half), BF16),
            pltpu.VMEM((group, width), F32),
        ],
        compiler_params=pltpu.CompilerParams(vmem_limit_bytes=56 * 1024 * 1024),
    )(lengths, times, emb, ctx, cot, w, small, gain_in, bout)


MESH = pl.DeviceIdType.MESH


def remote(src, dst, send_sem, recv_sem, device):
    return pltpu.make_async_remote_copy(
        src_ref=src, dst_ref=dst, send_sem=send_sem, recv_sem=recv_sem, device_id=device, device_id_type=MESH
    )


def greet(devices):
    barrier = pltpu.get_barrier_semaphore()
    for device in devices:
        pl.semaphore_signal(barrier, inc=1, device_id=device, device_id_type=MESH)
    pl.semaphore_wait(barrier, len(devices))


def back_kernel(
    place_ref, mixed_ref, grad_start_ref, grad_w_ref, grad_small_ref,
    incoming_ref, grad_rows_ref, mixed_rows_ref, grad_w_out_ref, small_out_ref,
    outgoing, stage1, core_in, hop_in_x, hop_in_y, stage2, hop_in2, stage3, z_in, small_mine, small_in,
    rows_send, rows_recv, mixed_send, mixed_recv, item_send, item_recv, pass_send, pass_recv,
    core_send, core_recv, hop_send, hop_recv, z_send, z_recv, small_send, small_recv,
):
    pbs, kas = lax.axis_size("pb"), lax.axis_size("ka")
    owners = pbs * kas
    zs = pbs // 2
    pb, ka, ha = lax.axis_index("pb"), lax.axis_index("ka"), lax.axis_index("ha")
    z, core = pb // 2, pb % 2
    me = pb * kas + ka
    stream = 2 * ka + ha
    tok = mixed_ref.shape[0] // 2
    half = mixed_ref.shape[1] // 2
    wide = grad_w_ref.shape[-1] // 2
    x_peer = (pb, ka, 1 - ha)
    y_peer = (pb, 1 - ka, ha)
    xy_peer = (pb, 1 - ka, 1 - ha)
    core_peer = (2 * z + 1 - core, ka, ha)

    def owner(index):
        return (index // kas, index % kas, ha)

    greet([owner(lax.rem(me + d, owners)) for d in range(1, owners)] + [x_peer, xy_peer])

    quads = [(y_peer, 1 - ka, ha), (x_peer, ka, 1 - ha), (xy_peer, 1 - ka, 1 - ha)]
    row_copies, mixed_copies = [], []
    for i, (device, to_ka, to_ha) in enumerate(quads):
        copy = remote(
            grad_start_ref.at[pl.ds(to_ka * tok, tok)], grad_rows_ref.at[stream], rows_send.at[i], rows_recv.at[i], device
        )
        copy.start()
        row_copies.append(copy)
    core_copies = []
    for part in range(2):
        cols = pl.ds(part * wide, wide)
        copy = remote(
            grad_w_ref.at[:, :, 1 - core, :, cols], core_in.at[part], core_send.at[part], core_recv.at[part], core_peer
        )
        copy.start()
        core_copies.append(copy)
    small_copies = [remote(grad_small_ref, small_in.at[0], small_send.at[0], small_recv.at[0], core_peer)]
    small_copies[0].start()
    for i, (device, to_ka, to_ha) in enumerate(quads):
        copy = remote(
            mixed_ref.at[pl.ds(to_ka * tok, tok), pl.ds(pl.multiple_of(to_ha * half, half), half)],
            mixed_rows_ref.at[stream], mixed_send.at[i], mixed_recv.at[i], device,
        )
        copy.start()
        mixed_copies.append(copy)
    grad_rows_ref[stream] = grad_start_ref[pl.ds(pl.multiple_of(ka * tok, tok), tok)]
    mixed_rows_ref[stream] = mixed_ref[
        pl.ds(pl.multiple_of(ka * tok, tok), tok), pl.ds(pl.multiple_of(ha * half, half), half)
    ]
    for copy in row_copies:
        copy.wait_recv()

    count = grad_rows_ref.shape[0] * tok
    share = count // owners
    slot = lax.broadcasted_iota(jnp.int32, (count, count), 1)
    hot = (place_ref[...] == slot).astype(F32).astype(BF16)
    rows = grad_rows_ref[...].reshape(count, 2 * half)
    outgoing[...] = mm_tn(hot, rows).astype(BF16).reshape(outgoing.shape)
    item_copies = []
    for d in range(1, owners):
        to = lax.rem(me + d, owners)
        copy = remote(outgoing.at[to], incoming_ref.at[ha, me], item_send.at[d], item_recv.at[d], owner(to))
        copy.start()
        item_copies.append(copy)
    incoming_ref[ha, me] = outgoing[me]
    pass_copies = []

    def hand_on(index):
        copy = remote(
            incoming_ref.at[ha, index], incoming_ref.at[ha, index],
            pass_send.at[len(pass_copies)], pass_recv.at[len(pass_copies)], x_peer,
        )
        copy.start()
        pass_copies.append(copy)

    hand_on(me)

    hop_copies = []
    for part in range(2):
        cols = slice(part * wide, (part + 1) * wide)
        core_copies[part].wait_recv()
        for h in range(2):
            total = grad_w_ref[h, :, core, :, cols].astype(F32) + core_in[part, h].astype(F32)
            stage1[part, h] = total.astype(BF16).reshape(stage1.shape[2:])
        if part == 0:
            copy = remote(stage1.at[0, 1 - ha], hop_in_x, hop_send.at[0], hop_recv.at[0], x_peer)
        else:
            copy = remote(stage1.at[1, :, :, 1 - ka], hop_in_y, hop_send.at[1], hop_recv.at[1], y_peer)
        copy.start()
        hop_copies.append(copy)
    small_copies[0].wait_recv()
    small_mine[0] = grad_small_ref[...] + small_in[0]
    small_copies.append(remote(small_mine.at[0], small_in.at[1], small_send.at[1], small_recv.at[1], x_peer))
    small_copies[1].start()

    def take(first, last):
        for d in range(first, last):
            item_copies[d - 1].wait_recv()
            hand_on(lax.rem(me - d + owners, owners))

    take(1, 6)
    hop_copies[0].wait_recv()
    stage2[0] = (stage1[0, ha].astype(F32) + hop_in_x[...].astype(F32)).astype(BF16)
    hop_copies.append(remote(stage2.at[0, :, 1 - ka], hop_in2.at[0], hop_send.at[2], hop_recv.at[2], y_peer))
    hop_copies[2].start()
    hop_copies[1].wait_recv()
    for h in range(2):
        stage2[1, :, h] = (stage1[1, h, :, ka].astype(F32) + hop_in_y[h].astype(F32)).astype(BF16)
    hop_copies.append(remote(stage2.at[1, :, 1 - ha], hop_in2.at[1], hop_send.at[3], hop_recv.at[3], x_peer))
    hop_copies[3].start()
    small_copies[1].wait_recv()
    small_mine[1] = small_mine[0] + small_in[1]
    small_copies.append(remote(small_mine.at[1], small_in.at[2], small_send.at[2], small_recv.at[2], y_peer))
    small_copies[2].start()

    take(6, 11)
    z_copies = []
    for part in range(2):
        hop_copies[2 + part].wait_recv()
        kept = stage2[0, :, ka] if part == 0 else stage2[1, :, ha]
        stage3[part] = (kept.astype(F32) + hop_in2[part].astype(F32)).astype(BF16)
    small_copies[2].wait_recv()
    small_mine[2] = small_mine[1] + small_in[2]
    for d in range(1, zs):
        to = lax.rem(z + d, zs)
        device = (2 * to + core, ka, ha)
        for part in range(2):
            i = (d - 1) * 2 + part
            copy = remote(stage3.at[part, to], z_in.at[part, d - 1], z_send.at[i], z_recv.at[i], device)
            copy.start()
            z_copies.append(copy)
        i = 2 + d
        copy = remote(small_mine.at[2], small_in.at[i], small_send.at[i], small_recv.at[i], device)
        copy.start()
        small_copies.append(copy)
    take(11, owners)
    for copy in z_copies:
        copy.wait_recv()
    for part in range(2):
        total = stage3[part, z].astype(F32)
        for d in range(zs - 1):
            total = total + z_in[part, d].astype(F32)
        grad_w_out_ref[:, part * wide : (part + 1) * wide] = total
    total = small_mine[2]
    for copy in small_copies[3:]:
        copy.wait_recv()
    for d in range(1, zs):
        total = total + small_in[2 + d]
    small_out_ref[...] = total
    for copy in mixed_copies + pass_copies:
        copy.wait_recv()
    for copies in (row_copies, mixed_copies, item_copies, pass_copies, core_copies, hop_copies, z_copies, small_copies):
        for copy in copies:
            copy.wait_send()


def back(place, mixed, grad_start, grad_w, grad_small):
    pbs, kas = lax.axis_size("pb"), lax.axis_size("ka")
    owners, zs = pbs * kas, pbs // 2
    group, width = mixed.shape
    tok, half = group // 2, width // 2
    count = MB * tok
    share = count // owners
    block = grad_w.shape[3] // 2
    wide = grad_w.shape[4] // 2
    vmem = pl.BlockSpec(memory_space=pltpu.VMEM)
    dma = pltpu.SemaphoreType.DMA
    return pl.pallas_call(
        back_kernel,
        out_shape=(
            jax.ShapeDtypeStruct((2, owners, share, width), BF16),
            jax.ShapeDtypeStruct((MB, tok, width), BF16),
            jax.ShapeDtypeStruct((MB, tok, half), BF16),
            jax.ShapeDtypeStruct((block, 2 * wide), F32),
            jax.ShapeDtypeStruct(grad_small.shape, F32),
        ),
        in_specs=[vmem] * 5,
        out_specs=(vmem,) * 5,
        scratch_shapes=[
            pltpu.VMEM((owners, share, width), BF16),
            pltpu.VMEM((2, 2, zs, 2, block, wide), BF16),
            pltpu.VMEM((2, 2, zs, 2 * block, wide), BF16),
            pltpu.VMEM((zs, 2, block, wide), BF16),
            pltpu.VMEM((2, zs, block, wide), BF16),
            pltpu.VMEM((2, zs, 2, block, wide), BF16),
            pltpu.VMEM((2, zs, block, wide), BF16),
            pltpu.VMEM((2, zs, block, wide), BF16),
            pltpu.VMEM((2, zs - 1, block, wide), BF16),
            pltpu.VMEM((3,) + grad_small.shape, F32),
            pltpu.VMEM((2 + zs,) + grad_small.shape, F32),
            dma((3,)), dma((3,)), dma((3,)), dma((3,)),
            dma((owners,)), dma((owners,)), dma((owners,)), dma((owners,)),
            dma((2,)), dma((2,)), dma((4,)), dma((4,)),
            dma((2 * (zs - 1),)), dma((2 * (zs - 1),)), dma((2 + zs,)), dma((2 + zs,)),
        ],
        compiler_params=pltpu.CompilerParams(
            collective_id=1, has_side_effects=True, vmem_limit_bytes=48 * 1024 * 1024
        ),
    )(place, mixed, grad_start, grad_w, grad_small)


def gather_kernel(ids_ref, table_ref, out_ref, total):
    step = pl.program_id(0)
    rows = table_ref.shape[0]
    lane = lax.broadcasted_iota(jnp.int32, (ids_ref.shape[0], rows), 1) + step * rows
    hot = (ids_ref[...] == lane).astype(F32).astype(BF16)
    part = mm(hot, table_ref[...])

    @pl.when(step == 0)
    def _():
        total[...] = part

    @pl.when(step > 0)
    def _():
        total[...] += part

    @pl.when(step == pl.num_programs(0) - 1)
    def _():
        out_ref[...] = total[...].astype(BF16)


def gather_rows(ids, table, tile=1024):
    count, width = ids.shape[0], table.shape[1]
    return pl.pallas_call(
        gather_kernel,
        grid=(table.shape[0] // tile,),
        out_shape=jax.ShapeDtypeStruct((count, width), BF16),
        in_specs=[
            pl.BlockSpec((count, 1), lambda i: (0, 0)),
            pl.BlockSpec((tile, width), lambda i: (i, 0)),
        ],
        out_specs=pl.BlockSpec((count, width), lambda i: (0, 0)),
        scratch_shapes=[pltpu.VMEM((count, width), F32)],
        compiler_params=pltpu.CompilerParams(vmem_limit_bytes=40 * 1024 * 1024),
    )(ids, table)


def scatter_kernel(ids_ref, rows_ref, out_ref):
    tile = out_ref.shape[0]
    row = lax.broadcasted_iota(jnp.int32, (tile, ids_ref.shape[1]), 0) + pl.program_id(0) * tile
    hot = (ids_ref[...] == row).astype(F32).astype(BF16)
    out_ref[...] = mm(hot, rows_ref[...])


def scatter_rows(ids, rows, table_rows, tile=512):
    count, width = rows.shape
    return pl.pallas_call(
        scatter_kernel,
        grid=(table_rows // tile,),
        out_shape=jax.ShapeDtypeStruct((table_rows, width), F32),
        in_specs=[
            pl.BlockSpec((1, count), lambda i: (0, 0)),
            pl.BlockSpec((count, width), lambda i: (0, 0)),
        ],
        out_specs=pl.BlockSpec((tile, width), lambda i: (i, 0)),
        compiler_params=pltpu.CompilerParams(vmem_limit_bytes=40 * 1024 * 1024),
    )(ids, rows)


def local_streams(
    context,
    item_owner,
    item_offset,
    lengths,
    times,
    table,
    cotangent,
    ln_in_gain,
    w_uvqk,
    b_uvqk,
    rel_bias,
    time_bias,
    ln_out_gain,
    w_out,
    b_out,
):
    owners = lax.axis_size(("pb", "ka"))
    pbs = lax.axis_size("pb")
    row_count, width = context.shape
    half = width // 2
    group = 2 * TOK_DEV
    capacity = max(2, 2 * row_count // owners)
    share = capacity // 2
    ka = lax.axis_index("ka")
    ha = lax.axis_index("ha")
    stream = 2 * ka + ha
    owner_ids = item_owner[:, 0]
    owner_hits = (owner_ids[:, None] == jnp.arange(owners, dtype=jnp.int32)[None, :]).astype(jnp.int32)
    earlier = jnp.sum((jnp.cumsum(owner_hits, axis=0) - owner_hits) * owner_hits, axis=1)
    slot_index = owner_ids * capacity + earlier
    requests = jnp.full((owners * capacity,), -1, jnp.int32).at[slot_index].set(item_offset)
    arrived = lax.all_to_all(
        requests.reshape(owners, capacity), ("pb", "ka"), split_axis=0, concat_axis=0, tiled=True
    )
    mine = lax.dynamic_slice_in_dim(arrived, ha * share, share, 1).reshape(owners * share, 1)
    fetched = gather_rows(mine, table).reshape(owners, share, width)
    returned = lax.all_to_all(fetched, ("pb", "ka"), split_axis=0, concat_axis=0, tiled=True)
    returned = returned.reshape(owners * share, width)
    place = earlier - ha * share
    place = jnp.where((place >= 0) & (place < share), owner_ids * share + place, -1)
    hot = (place[:, None] == jnp.arange(owners * share, dtype=jnp.int32)[None, :]).astype(BF16)
    embedded = jnp.dot(hot, returned, preferred_element_type=F32).astype(BF16)
    emb = lax.all_to_all(
        embedded.reshape(MB, TOK_DEV, width), ("ka", "ha"), split_axis=0, concat_axis=0, tiled=True
    )

    def both_halves(array):
        away = lax.dynamic_slice_in_dim(array, (2 * (1 - ka) + ha) * TOK_DEV, TOK_DEV, 0)
        own = lax.dynamic_slice_in_dim(array, stream * TOK_DEV, TOK_DEV, 0)
        other = lax.ppermute(away, "ka", [(0, 1), (1, 0)])
        first = jnp.where(ka == 0, own, other)
        second = jnp.where(ka == 0, other, own)
        return jnp.concatenate([first, second], axis=0)

    ctx = both_halves(context)
    cot = both_halves(cotangent)
    shard = jnp.concatenate([w_uvqk.reshape(w_uvqk.shape[0], 4 * half), w_out.T], axis=1)
    w_all = lax.all_gather(shard, ("ha", "pb"), axis=0, tiled=True).reshape(2, width, 5 * half)
    small = jnp.concatenate(
        [
            b_uvqk,
            rel_bias,
            time_bias.reshape(2, half),
            ln_out_gain.reshape(1, half),
        ],
        axis=0,
    )
    small = lax.all_gather(small, "ha", axis=0)
    mixed, grad_start, grad_w, grad_small = layer(
        lax.dynamic_index_in_dim(lengths[0], stream, 0, False),
        lax.dynamic_slice_in_dim(times[0], stream, 1, 0),
        emb,
        ctx,
        cot,
        w_all,
        small,
        ln_in_gain.reshape(1, width),
        b_out.reshape(1, width),
        (pbs // 2, 2, 2 * width // owners),
    )
    incoming, grad_rows, mixed_rows, grad_w, grad_small = back(
        place[:, None], mixed, grad_start, grad_w, grad_small
    )
    incoming = incoming.reshape(2 * owners * share, width)
    ids = arrived.reshape(owners, 2, share).transpose(1, 0, 2).reshape(1, 2 * owners * share)
    table_grad = scatter_rows(ids, incoming, table.shape[0])
    mine = lax.dynamic_index_in_dim(grad_small, ha, 0, False)
    return (
        mixed_rows.reshape(row_count, half),
        grad_rows.reshape(row_count, width),
        table_grad,
        grad_small[:, 11].reshape(width),
        grad_w[:, : 4 * half].reshape(-1, 4, half),
        mine[0:4],
        mine[4:8],
        mine[8:10].reshape(4, half // 2),
        mine[10],
        grad_w[:, 4 * half :].T,
        grad_small[:, 12].reshape(width),
    )


def solution(mesh):
    one_stream = mesh.shape["ka"] * mesh.shape["ha"] == MB and mesh.shape["ka"] == 2
    return jax.shard_map(
        local_streams if one_stream else local_general,
        mesh=mesh,
        in_specs=(
            P(("pb", "ka"), None),
            P(("pb", "ka"), None),
            P(("pb", "ka")),
            P("pb", None, None),
            P("pb", None, None),
            P(("pb", "ka"), None),
            P(("pb", "ka"), None),
            P(),
            P("pb", None, "ha"),
            P(None, "ha"),
            P("ha", None),
            P("ha", None),
            P("ha"),
            P("ha", "pb"),
            P(),
        ),
        out_specs=(
            P(("pb", "ka"), "ha"),
            P(("pb", "ka"), None),
            P(("pb", "ka"), None),
            P(),
            P(("pb", "ka"), None, "ha"),
            P(None, "ha"),
            P("ha", None),
            P("ha", None),
            P("ha"),
            P("ha", ("pb", "ka")),
            P(),
        ),
        check_vma=False,
    )
```

```python
import functools

import jax
import jax.numpy as jnp
from jax import lax
from jax.experimental import pallas as pl
from jax.experimental.pallas import tpu as pltpu
from jax.sharding import PartitionSpec as P

DH = 64
TOK_DEV = 128
MB = 4
SEQ_GRP = 4
F32 = jnp.float32
BF16 = jnp.bfloat16


epsilon = 1e-05


def silu_slope(values):
    sigma = jax.nn.sigmoid(values)
    return sigma * (1.0 + values * (1.0 - sigma))


def norm_rows(values, gain):
    centered = values - jnp.mean(values, axis=-1, keepdims=True)
    inverse = lax.rsqrt(jnp.mean(centered * centered, axis=-1, keepdims=True) + epsilon)
    unit_rows = centered * inverse
    return (unit_rows * gain, unit_rows, inverse)


def norm_back(grad_unit, unit_rows, inverse):
    first_mean = jnp.mean(grad_unit, axis=-1, keepdims=True)
    second_mean = jnp.mean(grad_unit * unit_rows, axis=-1, keepdims=True)
    return inverse * (grad_unit - first_mean - unit_rows * second_mean)


def stream_layout(lengths_row, group):
    places = jnp.arange(group, dtype=jnp.int32)
    ends = jnp.cumsum(lengths_row, dtype=jnp.int32)
    member = jnp.sum((ends[None, :] <= places[:, None]).astype(jnp.int32), axis=1)
    onehot = (member[:, None] == jnp.arange(SEQ_GRP, dtype=jnp.int32)[None, :]).astype(jnp.float32)
    counted = jnp.maximum(jnp.sum(onehot * lengths_row.astype(jnp.float32)[None, :], axis=1), 1.0)
    return (places, member, counted)


def diagonal_bias(rel_bias, query_first, key_first, query_len, key_len):
    heads, group = rel_bias.shape
    span = query_len + key_len - 1
    padded = jnp.concatenate([jnp.zeros((heads, group), jnp.float32), rel_bias], axis=1)
    window = lax.dynamic_slice_in_dim(
        padded, query_first - key_first - key_len + 1 + group, span, 1
    )
    flipped = jnp.concatenate([window[:, ::-1], jnp.zeros((heads, 1), jnp.float32)], axis=1)
    skewed = jnp.tile(flipped, (1, query_len))[:, : query_len * span].reshape(
        heads, query_len, span
    )
    return skewed[:, :, query_len - 1 : query_len - 1 + key_len]


def diagonal_sums(grad_scores, query_first, key_first, group):
    heads, query_len, key_len = grad_scores.shape
    span = query_len + key_len - 1
    widened = jnp.pad(grad_scores.astype(jnp.float32), ((0, 0), (0, 0), (query_len - 1, 0)))
    flat = jnp.pad(widened.reshape(heads, query_len * span), ((0, 0), (0, query_len)))
    totals = jnp.sum(flat.reshape(heads, query_len, span + 1), axis=1)
    window = totals[:, :span][:, ::-1]
    placed = lax.dynamic_update_slice_in_dim(
        jnp.zeros((heads, 2 * group), jnp.float32),
        window,
        query_first - key_first - key_len + 1 + group,
        1,
    )
    return placed[:, group:]


def bucket_lookup(time_bias, bucket_hot):
    high = time_bias.astype(jnp.bfloat16)
    rest = time_bias - high.astype(jnp.float32)
    middle = rest.astype(jnp.bfloat16)
    lowest = (rest - middle.astype(jnp.float32)).astype(jnp.bfloat16)
    pieces = jnp.einsum(
        "phb,qkb->phqk",
        jnp.stack([high, middle, lowest]),
        bucket_hot,
        preferred_element_type=jnp.float32,
    )
    return pieces[0] + pieces[1] + pieces[2]


def tile_scores(query_heads, key_heads, query_info, key_info, rel_bias, time_bias):
    query_pos, query_member, query_count, query_stamp = query_info
    key_pos, key_member, key_stamp = key_info
    distance = query_pos[:, None] - key_pos[None, :]
    time_index = jnp.clip(query_stamp[:, None] - key_stamp[None, :], 0, time_bias.shape[1] - 1)
    bucket_hot = (
        time_index[:, :, None] == jnp.arange(time_bias.shape[1], dtype=jnp.int32)[None, None, :]
    ).astype(jnp.bfloat16)
    scores = jnp.einsum(
        "qhd,khd->hqk", query_heads, key_heads, preferred_element_type=jnp.float32
    ) * DH ** (-0.5)
    scores = (
        scores
        + diagonal_bias(rel_bias, query_pos[0], key_pos[0], query_pos.shape[0], key_pos.shape[0])
        + bucket_lookup(time_bias, bucket_hot)
    )
    allowed = (
        (query_member[:, None] == key_member[None, :])
        & (query_member[:, None] < SEQ_GRP)
        & (distance >= 0)
    )[None]
    weights = (jnp.where(allowed, jax.nn.silu(scores), 0.0) / query_count[None, :, None]).astype(
        jnp.bfloat16
    )
    return (scores, allowed, weights, bucket_hot)


def score_grads(grad_weights, scores, allowed, query_count):
    return (
        jnp.where(allowed, grad_weights / query_count[None, :, None], 0.0) * silu_slope(scores)
    ).astype(jnp.bfloat16)


def local_general(
    context,
    item_owner,
    item_offset,
    lengths,
    times,
    table,
    cotangent,
    ln_in_gain,
    w_uvqk,
    b_uvqk,
    rel_bias,
    time_bias,
    ln_out_gain,
    w_out,
    b_out,
):
    owners = lax.axis_size(("pb", "ka"))
    row_count = context.shape[0]
    width = context.shape[1]
    capacity = max(2, 2 * row_count // owners)
    owner_ids = item_owner[:, 0]
    owner_hits = (owner_ids[:, None] == jnp.arange(owners, dtype=jnp.int32)[None, :]).astype(
        jnp.int32
    )
    earlier = jnp.sum((jnp.cumsum(owner_hits, axis=0) - owner_hits) * owner_hits, axis=1)
    slot_index = owner_ids * capacity + earlier
    requests = jnp.zeros((owners * capacity,), jnp.int32).at[slot_index].set(item_offset + 1)
    arrived = lax.all_to_all(
        requests.reshape(owners, capacity), ("pb", "ka"), split_axis=0, concat_axis=0, tiled=True
    ).reshape(-1)
    present = arrived > 0
    local_rows = jnp.maximum(arrived - 1, 0)
    fetched = jnp.where(present[:, None], table[local_rows], jnp.zeros((), jnp.bfloat16))
    returned = lax.all_to_all(
        fetched.reshape(owners, capacity, width),
        ("pb", "ka"),
        split_axis=0,
        concat_axis=0,
        tiled=True,
    )
    embedded = returned.reshape(owners * capacity, width)[slot_index]
    start = context.astype(jnp.float32) + embedded.astype(jnp.float32)
    group = lax.axis_size("ka") * TOK_DEV
    block_start = lax.axis_index("ka") * TOK_DEV
    half_cols = w_out.shape[0]
    heads = half_cols // DH
    full_cols = half_cols * lax.axis_size("ha")
    out_cols = width // lax.axis_size("ha")
    out_start = lax.axis_index("ha") * out_cols
    bias_half = lax.dynamic_slice_in_dim(b_out, out_start, out_cols)
    scale = DH ** (-0.5)
    grad_gain_in = jnp.zeros(ln_in_gain.shape, jnp.float32)
    grad_bias_proj = jnp.zeros(b_uvqk.shape, jnp.float32)
    grad_rel = jnp.zeros(rel_bias.shape, jnp.float32)
    grad_time = jnp.zeros(time_bias.shape, jnp.float32)
    grad_gain_out = jnp.zeros(ln_out_gain.shape, jnp.float32)
    grad_bias_out = jnp.zeros(b_out.shape, jnp.float32)
    weight_total = None
    mixed_parts = []
    grad_parts = []
    for micro in range(MB):
        w_full, w_final = (
            lax.all_gather(w_uvqk, "pb", axis=0, tiled=True),
            lax.all_gather(w_out, "pb", axis=1, tiled=True),
        )
        x_in = start[micro * TOK_DEV : (micro + 1) * TOK_DEV]
        cot_rows = cotangent[micro * TOK_DEV : (micro + 1) * TOK_DEV]
        stamps = times[0, micro]
        places, member, counted = stream_layout(lengths[0, micro], group)
        query_pos = lax.dynamic_slice_in_dim(places, block_start, TOK_DEV)
        query_member = lax.dynamic_slice_in_dim(member, block_start, TOK_DEV)
        query_count = lax.dynamic_slice_in_dim(counted, block_start, TOK_DEV)
        query_stamp = lax.dynamic_slice_in_dim(stamps, block_start, TOK_DEV)
        normed_float, unit_in, inverse_in = norm_rows(x_in, ln_in_gain)
        normed = normed_float.astype(jnp.bfloat16)
        pre_act = (
            jnp.einsum("td,dgc->tgc", normed, w_full, preferred_element_type=jnp.float32) + b_uvqk
        )
        activated = jax.nn.silu(pre_act)
        gate_part = activated[:, 0]
        values = activated[:, 1].astype(jnp.bfloat16)
        queries = activated[:, 2].astype(jnp.bfloat16)
        key_rows = activated[:, 3].astype(jnp.bfloat16)
        key_pair = lax.all_gather(jnp.stack([key_rows, values]), "ka", axis=1, tiled=True)
        all_keys = key_pair[0].reshape(group, heads, DH)
        all_values = key_pair[1].reshape(group, heads, DH)
        query_heads = queries.reshape(TOK_DEV, heads, DH)
        scores, allowed, weights, bucket_hot = tile_scores(
            query_heads,
            all_keys,
            (query_pos, query_member, query_count, query_stamp),
            (places, member, stamps),
            rel_bias,
            time_bias,
        )
        attended = jnp.einsum(
            "hqk,khd->qhd", weights, all_values, preferred_element_type=jnp.float32
        ).reshape(TOK_DEV, half_cols)
        row_total, row_square = lax.psum(
            (jnp.sum(attended, axis=1), jnp.sum(attended * attended, axis=1)), "ha"
        )
        row_mean = row_total / full_cols
        inverse_out = lax.rsqrt(row_square / full_cols - row_mean * row_mean + epsilon)[:, None]
        unit_out = (attended - row_mean[:, None]) * inverse_out
        mixed_in = (unit_out * ln_out_gain * gate_part).astype(jnp.bfloat16)
        partial_out = jnp.dot(mixed_in, w_final, preferred_element_type=jnp.float32)
        summed_out = lax.psum_scatter(partial_out, "ha", scatter_dimension=1, tiled=True)
        residual = lax.dynamic_slice_in_dim(x_in, out_start, out_cols, 1)
        mixed_parts.append((summed_out + bias_half + residual).astype(jnp.bfloat16))
        grad_final_part = jnp.einsum(
            "tc,td->cd", mixed_in, cot_rows, preferred_element_type=jnp.float32
        )
        grad_bias_out = grad_bias_out + jnp.sum(cot_rows.astype(jnp.float32), axis=0)
        grad_mixed = jnp.einsum("td,cd->tc", cot_rows, w_final, preferred_element_type=jnp.float32)
        grad_gate = grad_mixed * unit_out * ln_out_gain
        grad_gain_out = grad_gain_out + jnp.sum(grad_mixed * unit_out * gate_part, axis=0)
        grad_unit = grad_mixed * gate_part * ln_out_gain
        first_total, second_total = lax.psum(
            (jnp.sum(grad_unit, axis=1), jnp.sum(grad_unit * unit_out, axis=1)), "ha"
        )
        grad_attended = (
            inverse_out
            * (
                grad_unit
                - first_total[:, None] / full_cols
                - unit_out * second_total[:, None] / full_cols
            )
        ).astype(jnp.bfloat16)
        grad_heads = grad_attended.reshape(TOK_DEV, heads, DH)
        grad_weights = jnp.einsum(
            "qhd,khd->hqk", grad_heads, all_values, preferred_element_type=jnp.float32
        )
        grad_scores = score_grads(grad_weights, scores, allowed, query_count)
        grad_rel = grad_rel + diagonal_sums(grad_scores, query_pos[0], places[0], rel_bias.shape[1])
        grad_time = grad_time + jnp.einsum(
            "hqk,qkb->hb", grad_scores, bucket_hot, preferred_element_type=jnp.float32
        )
        grad_queries = (
            jnp.einsum("hqk,khd->qhd", grad_scores, all_keys, preferred_element_type=jnp.float32)
            * scale
        ).reshape(TOK_DEV, half_cols)
        key_part = (
            jnp.einsum("hqk,qhd->khd", grad_scores, query_heads, preferred_element_type=jnp.float32)
            * scale
        )
        value_part = jnp.einsum(
            "hqk,qhd->khd", weights, grad_heads, preferred_element_type=jnp.float32
        )
        stacked = jnp.stack(
            [key_part.reshape(group, half_cols), value_part.reshape(group, half_cols)]
        )
        owned_grads = lax.psum_scatter(stacked, "ka", scatter_dimension=1, tiled=True)
        grad_keys = owned_grads[0]
        grad_values = owned_grads[1]
        grad_act = jnp.stack([grad_gate, grad_values, grad_queries, grad_keys], axis=1)
        grad_pre = (grad_act * silu_slope(pre_act)).astype(jnp.bfloat16)
        grad_proj_part = jnp.einsum(
            "td,tgc->dgc", normed, grad_pre, preferred_element_type=jnp.float32
        )
        grad_bias_proj = grad_bias_proj + jnp.sum(grad_pre.astype(jnp.float32), axis=0)
        grad_normed = lax.psum(
            jnp.einsum("tgc,dgc->td", grad_pre, w_full, preferred_element_type=jnp.float32), "ha"
        )
        grad_gain_in = grad_gain_in + jnp.sum(grad_normed * unit_in, axis=0)
        grad_parts.append(
            cot_rows.astype(jnp.float32) + norm_back(grad_normed * ln_in_gain, unit_in, inverse_in)
        )
        local_pair = (grad_proj_part, grad_final_part)
        local_pair = (
            lax.psum_scatter(local_pair[0], ("pb", "ka"), scatter_dimension=0, tiled=True),
            lax.psum_scatter(local_pair[1], ("pb", "ka"), scatter_dimension=1, tiled=True),
        )
        weight_total = (
            local_pair if weight_total is None else jax.tree.map(jnp.add, weight_total, local_pair)
        )
    grad_start = jnp.concatenate(grad_parts, axis=0)
    outgoing = jnp.zeros((owners * capacity, width), jnp.float32).at[slot_index].set(grad_start)
    incoming = lax.all_to_all(
        outgoing.reshape(owners, capacity, width),
        ("pb", "ka"),
        split_axis=0,
        concat_axis=0,
        tiled=True,
    ).reshape(owners * capacity, width)
    table_grad = jax.ops.segment_sum(
        jnp.where(present[:, None], incoming, 0.0), local_rows, num_segments=table.shape[0]
    )
    small_total = lax.psum(
        (grad_gain_in, grad_bias_proj, grad_rel, grad_time, grad_gain_out, grad_bias_out),
        ("pb", "ka"),
    )
    mixed = jnp.concatenate(mixed_parts, axis=0)
    return (
        mixed,
        grad_start.astype(jnp.bfloat16),
        table_grad,
        small_total[0],
        weight_total[0],
        small_total[1],
        small_total[2],
        small_total[3],
        small_total[4],
        weight_total[1],
        small_total[5],
    )


MESH = pl.DeviceIdType.MESH


def remote(src, dst, send_sem, recv_sem, device):
    return pltpu.make_async_remote_copy(
        src_ref=src, dst_ref=dst, send_sem=send_sem, recv_sem=recv_sem, device_id=device, device_id_type=MESH
    )


def mm(a, b):
    return jnp.dot(a, b, preferred_element_type=F32)


def mm_nt(a, b):
    return lax.dot_general(a, b, (((1,), (1,)), ((), ())), preferred_element_type=F32)


def mm_tn(a, b):
    return lax.dot_general(a, b, (((0,), (0,)), ((), ())), preferred_element_type=F32)


def mm_exact(a, b):
    return jnp.dot(a, b, preferred_element_type=F32, precision=lax.Precision.HIGHEST)


def sigmoid(v):
    return 0.5 * jnp.tanh(0.5 * v) + 0.5


def skew(tile):
    return pltpu.roll(tile, 0, 1, stride=1, stride_axis=0)


def iota(shape, dim):
    return lax.broadcasted_iota(jnp.int32, shape, dim)


def one_hot(equal):
    return equal.astype(F32).astype(BF16)


def layer_norm(values):
    centered = values - jnp.mean(values, axis=1, keepdims=True)
    inverse = lax.rsqrt(jnp.mean(centered * centered, axis=1, keepdims=True) + epsilon)
    return centered * inverse, inverse


def layer_norm_back(grad_unit, unit, inverse):
    first = jnp.mean(grad_unit, axis=1, keepdims=True)
    second = jnp.mean(grad_unit * unit, axis=1, keepdims=True)
    return inverse * (grad_unit - first - unit * second)


class Place:
    def __init__(self):
        self.pbs, self.kas = lax.axis_size("pb"), lax.axis_size("ka")
        self.owners, self.zs = self.pbs * self.kas, self.pbs // 2
        self.pb, self.ka, self.ha = lax.axis_index("pb"), lax.axis_index("ka"), lax.axis_index("ha")
        self.z, self.core = self.pb // 2, self.pb % 2
        self.me = self.pb * self.kas + self.ka
        self.stream = 2 * self.ka + self.ha
        self.x_peer = (self.pb, self.ka, 1 - self.ha)
        self.y_peer = (self.pb, 1 - self.ka, self.ha)
        self.xy_peer = (self.pb, 1 - self.ka, 1 - self.ha)
        self.core_peer = (2 * self.z + 1 - self.core, self.ka, self.ha)
        self.quads = [
            (self.x_peer, self.ka, 1 - self.ha),
            (self.y_peer, 1 - self.ka, self.ha),
            (self.xy_peer, 1 - self.ka, 1 - self.ha),
        ]

    def owner(self, index):
        return (index // self.kas, index % self.kas, self.ha)

    def owner_to(self, d):
        return lax.rem(self.me + d, self.owners)

    def owner_from(self, d):
        return lax.rem(self.me - d + self.owners, self.owners)

    def z_to(self, d):
        return lax.rem(self.z + d, self.zs)

    def z_device(self, d):
        return (2 * self.z_to(d) + self.core, self.ka, self.ha)

    def z_from(self, d):
        return 2 * lax.rem(self.z - d + self.zs, self.zs) + self.core


class Copies:
    def __init__(self, send, recv):
        self.send, self.recv, self.copies = send, recv, []

    def start(self, src, dst, device):
        i = len(self.copies)
        copy = remote(src, dst, self.send.at[i], self.recv.at[i], device)
        copy.start()
        self.copies.append(copy)

    def arrive(self, i):
        self.copies[i].wait_recv()

    def sent(self):
        for copy in self.copies:
            copy.wait_send()


class WeightSum:
    def __init__(self, at, own, first, s, name):
        self.at, self.own, self.first = at, own, first
        self.core_in, self.stage1, self.hop1 = s[name + "core_in"], s[name + "stage1"], s[name + "hop1"]
        self.stage2, self.hop2, self.stage3, self.z_in = s[name + "stage2"], s[name + "hop2"], s[name + "stage3"], s[name + "z_in"]
        self.copies = Copies(s[name + "send"], s[name + "recv"])

    def cores(self):
        self.copies.start(self.own.at[:, :, 1 - self.at.core], self.core_in, self.at.core_peer)

    def hop_one(self):
        at = self.at
        self.copies.arrive(0)
        for h in range(2):
            total = self.own[h, :, at.core].astype(F32) + self.core_in[h].astype(F32)
            self.stage1[h] = total.astype(BF16).reshape(self.stage1.shape[1:])
        if self.first == "x":
            self.copies.start(self.stage1.at[1 - at.ha], self.hop1, at.x_peer)
        else:
            self.copies.start(self.stage1.at[:, :, 1 - at.ka], self.hop1, at.y_peer)

    def hop_two(self):
        at = self.at
        self.copies.arrive(1)
        if self.first == "x":
            self.stage2[...] = (self.stage1[at.ha].astype(F32) + self.hop1[...].astype(F32)).astype(BF16)
            self.copies.start(self.stage2.at[:, 1 - at.ka], self.hop2, at.y_peer)
        else:
            for h in range(2):
                self.stage2[h] = (self.stage1[h, :, at.ka].astype(F32) + self.hop1[h].astype(F32)).astype(BF16)
            self.copies.start(self.stage2.at[1 - at.ha], self.hop2, at.x_peer)

    def hop_z(self):
        at = self.at
        self.copies.arrive(2)
        kept = self.stage2[:, at.ka] if self.first == "x" else self.stage2[at.ha]
        self.stage3[...] = (kept.astype(F32) + self.hop2[...].astype(F32)).astype(BF16)
        for d in range(1, at.zs):
            self.copies.start(self.stage3.at[at.z_to(d)], self.z_in.at[d - 1], at.z_device(d))

    def finish(self):
        total = self.stage3[self.at.z].astype(F32)
        for d in range(1, self.at.zs):
            self.copies.arrive(2 + d)
            total = total + self.z_in[d - 1].astype(F32)
        return total


def weight_sum_scratch(name, first, zs, block, cols):
    dma = pltpu.SemaphoreType.DMA
    hop1 = (zs, 2, block, cols) if first == "x" else (2, zs, block, cols)
    return {
        name + "own": pltpu.VMEM((2, zs, 2, 2 * block, cols), BF16),
        name + "core_in": pltpu.VMEM((2, zs, 2 * block, cols), BF16),
        name + "stage1": pltpu.VMEM((2, zs, 2, block, cols), BF16),
        name + "hop1": pltpu.VMEM(hop1, BF16),
        name + "stage2": pltpu.VMEM(hop1, BF16),
        name + "hop2": pltpu.VMEM((zs, block, cols), BF16),
        name + "stage3": pltpu.VMEM((zs, block, cols), BF16),
        name + "z_in": pltpu.VMEM((zs - 1, block, cols), BF16),
        name + "send": dma((2 + zs,)),
        name + "recv": dma((2 + zs,)),
    }


def main_kernel(in_names, out_names, scratch_names, *refs):
    names = in_names + out_names + scratch_names
    s = dict(zip(names, refs, strict=True))
    at = Place()
    owners, zs, ka, ha = at.owners, at.zs, at.ka, at.ha
    count, width = s["context"].shape
    half = width // 2
    tok = count // MB
    group = 2 * tok
    share = count // owners
    capacity = 2 * share
    block = s["w_uvqk"].shape[0] // 2
    heads_half = half // 64
    heads = 2 * heads_half
    pairs = half // 128
    buckets = s["time"].shape[1]
    gates_cols = 2 * half

    table, table_buf, table_sem = s["table"], s["table_buf"], s["table_sem"]
    chunks = table_sem.shape[0]
    chunk = table.shape[0] // chunks

    def local(i, src, dst):
        copy = pltpu.make_async_copy(src, dst, s["load_sem"].at[i])
        copy.start()
        return copy

    mine = pl.ds(pl.multiple_of(at.stream * tok, tok), tok)
    away = pl.ds(pl.multiple_of((2 * (1 - ka) + ha) * tok, tok), tok)
    loads = {}
    for i, name in enumerate(
        ("owner", "offset", "w_uvqk", "w_out", "b", "rel", "time", "gain_out", "gain_in", "b_out", "lengths", "times")
    ):
        loads[name] = local(i, s[name], s[name + "_v"])
    loads["ctx"] = local(12, s["context"].at[mine], s["ctx_v"].at[ka])
    loads["cot"] = local(13, s["cot"].at[mine], s["cot_v"].at[ka])
    for i in range(chunks):
        rows = pl.ds(i * chunk, chunk)
        pltpu.make_async_copy(table.at[rows], table_buf.at[rows], table_sem.at[i]).start()
    barrier = pltpu.get_barrier_semaphore()
    partners = [at.owner(at.owner_to(d)) for d in range(1, owners)] + [at.x_peer, at.xy_peer]
    for device in partners:
        pl.semaphore_signal(barrier, inc=1, device_id=device, device_id_type=MESH)

    loads["owner"].wait()
    loads["offset"].wait()
    owner_row, offset_row = s["owner_v"][...], s["offset_v"][...]
    hits = (owner_row == iota((owners, count), 0)).astype(F32)
    earlier = mm(hits.astype(BF16), one_hot(iota((count, count), 0) < iota((count, count), 1)))
    rank = jnp.sum(hits * earlier, axis=0, keepdims=True).astype(jnp.int32)
    rank_hot = one_hot(rank == iota((128, count), 0))
    high = (offset_row // 64).astype(F32)
    low = (offset_row % 64 + 1).astype(F32)
    asked = 64.0 * mm_nt((hits * high).astype(BF16), rank_hot) + mm_nt((hits * low).astype(BF16), rank_hot) - 1.0
    asked = asked.astype(jnp.int32)
    for o in range(owners):
        s["requests"][o] = jnp.broadcast_to(asked[o : o + 1], (8, 128))
    place = rank - ha * share
    place = jnp.where((place >= 0) & (place < share), owner_row * share + place, -1)

    shard, w, small = s["shard"], s["w"], s["small"]
    loads["w_uvqk"].wait()
    for g in range(4):
        shard[:, g * half : (g + 1) * half] = s["w_uvqk_v"][:, g, :]
    loads["w_out"].wait()
    shard[:, 4 * half :] = s["w_out_v"][...]
    w[ha, at.pb] = shard[...]
    for name in ("b", "rel", "time", "gain_out"):
        loads[name].wait()
    small[ha, 0:4] = s["b_v"][...]
    small[ha, 4:8] = s["rel_v"][...]
    for i in range(2):
        for j in range(2):
            small[ha, 8 + i : 9 + i, j * buckets : (j + 1) * buckets] = s["time_v"][2 * i + j : 2 * i + j + 1]
    small[ha, 10:11] = s["gain_out_v"][...]

    pl.semaphore_wait(barrier, len(partners))

    def copies(name):
        return Copies(s[name + "_send"], s[name + "_recv"])

    requests, arrived = s["requests"], s["arrived"]
    req, item, emb_c, row_c, small_c = copies("req"), copies("item"), copies("emb"), copies("row"), copies("small")
    wz, wx, wy, wc = copies("wz"), copies("wx"), copies("wy"), copies("wc")
    for d in range(1, owners):
        to = at.owner_to(d)
        req.start(requests.at[to], arrived.at[at.me], at.owner(to))
    arrived[at.me] = requests[at.me]
    my_half = pl.ds(pl.multiple_of(ka * block, block), block)
    for d in range(1, zs):
        wz.start(shard.at[my_half], w.at[ha, at.pb, my_half], at.z_device(d))
    wx.start(shard, w.at[ha, at.pb], at.x_peer)
    small_c.start(small.at[ha], small.at[ha], at.x_peer)
    row_c.start(s["context"].at[away], s["ctx_v"].at[ka], at.y_peer)
    row_c.start(s["cot"].at[away], s["cot_v"].at[ka], at.y_peer)
    wc.start(shard, w.at[ha, at.pb], at.core_peer)

    for i in range(owners - 1):
        req.arrive(i)
    pick = iota((share, 128), 1) == iota((share, 128), 0) + ha * share
    columns = []
    for o in range(owners):
        tile = jnp.broadcast_to(arrived[o, 0:1], (share, 128)).astype(F32)
        columns.append(jnp.sum(jnp.where(pick, tile, 0.0), axis=1, keepdims=True))
    column = jnp.concatenate(columns, axis=0).astype(jnp.int32)
    low_lanes = iota((1, 128), 1) < capacity
    for i in range(owners // 2):
        first, second = arrived[2 * i, 0:1], arrived[2 * i + 1, 0:1]
        s["ids"][:, i * 128 : (i + 1) * 128] = jnp.where(low_lanes, first, pltpu.roll(second, capacity, 1))
    total = s["total"]
    total[...] = jnp.zeros_like(total)

    def look_up(i, carry):
        rows = pl.ds(pl.multiple_of(i * chunk, chunk), chunk)
        pltpu.make_async_copy(table.at[rows], table_buf.at[rows], table_sem.at[i]).wait()
        total[...] += mm(one_hot(column == iota((owners * share, chunk), 1) + i * chunk), table_buf[rows])
        return carry

    lax.fori_loop(0, chunks // 2, look_up, 0)
    for d in range(1, zs):
        wz.arrive(d - 1)
        there = w.at[ha, at.z_from(d), my_half]
        wx.start(there, there, at.x_peer)
        wy.start(there, there, at.y_peer)
    lax.fori_loop(chunks // 2, chunks, look_up, 0)
    fetched, returned, parts, emb = s["fetched"], s["returned"], s["parts"], s["emb"]
    fetched[...] = total[...].astype(BF16).reshape(fetched.shape)
    for d in range(1, owners):
        to = at.owner_to(d)
        item.start(fetched.at[to], returned.at[at.me], at.owner(to))
    returned[at.me] = fetched[at.me]
    wx.arrive(0)
    there = w.at[1 - ha, at.pb]
    wc.start(there, there, at.core_peer)
    for d in range(1, zs):
        wx.arrive(d)
        there = w.at[1 - ha, at.z_from(d), my_half]
        wy.start(there, there, at.y_peer)

    loads["lengths"].wait()
    loads["times"].wait()
    small_c.arrive(0)
    lane, row = iota((group, group), 1), iota((group, group), 0)
    lengths = s["lengths_v"][pl.ds(at.stream, 1), :]
    ends = jnp.zeros((1, 1), jnp.int32)
    member_row = jnp.zeros((group, group), jnp.int32)
    member_col = jnp.zeros((group, group), jnp.int32)
    inv_count = jnp.zeros((group, group), F32)
    for i in range(SEQ_GRP):
        length = lengths[:, i : i + 1]
        inside = (row >= ends) & (row < ends + length)
        inv_count = jnp.where(inside, 1.0 / jnp.maximum(length, 1).astype(F32), inv_count)
        ends = ends + length
        member_row = member_row + (ends <= row).astype(jnp.int32)
        member_col = member_col + (ends <= lane).astype(jnp.int32)
    allowed = (member_row == member_col) & (member_row < SEQ_GRP) & (lane <= row)
    maskscale = s["maskscale"]
    maskscale[...] = jnp.where(allowed, inv_count, 0.0)
    times_row = jnp.broadcast_to(s["times_v"][pl.ds(at.stream, 1), :], (group, group))
    times_col = jnp.sum(jnp.where(lane == row, times_row, 0).astype(F32), axis=1, keepdims=True).astype(jnp.int32)
    time_index = jnp.clip(times_col - times_row, 0, buckets - 1)
    turn = ((lane + row) % group == 0).astype(F32)
    rel_back = mm_exact(jnp.concatenate([small[0, 4:8, :], small[1, 4:8, :]], axis=0), turn)
    bias = s["bias"]
    for head in range(heads):
        hf, head_in = divmod(head, heads_half)
        begin = (head_in % 2) * buckets
        bucket_row = jnp.broadcast_to(small[hf, 8 + head_in // 2 : 9 + head_in // 2, begin : begin + buckets], (group, buckets))
        by_time = [
            jnp.take_along_axis(bucket_row, time_index[:, c : c + buckets], axis=1, mode="promise_in_bounds")
            for c in range(0, group, buckets)
        ]
        bias[head] = skew(jnp.broadcast_to(rel_back[head : head + 1], (group, group))) + jnp.concatenate(by_time, axis=1)

    for i in range(owners - 1):
        item.arrive(i)
    slot_hot = one_hot(place == iota((count, count), 0))
    parts[...] = mm_tn(slot_hot, returned[...].reshape(count, width)).astype(BF16).reshape(parts.shape)
    for device, to_ka, to_ha in at.quads:
        emb_c.start(parts.at[2 * to_ka + to_ha], emb.at[at.stream], device)
    emb[at.stream] = parts[at.stream]
    for d in range(1, zs):
        wy.arrive(d - 1)
        there = w.at[ha, at.z_from(d)]
        wc.start(there, there, at.core_peer)
    for d in range(1, zs):
        wy.arrive(zs - 2 + d)
        there = w.at[1 - ha, at.z_from(d)]
        wc.start(there, there, at.core_peer)
    for i in range(2 * zs):
        wc.arrive(i)

    def w_half(hf, cols):
        return w[hf, :, :, cols].reshape(width, cols.stop - cols.start)

    out_cols = slice(4 * half, 5 * half)
    loads["cot"].wait()
    row_c.arrive(1)
    cot = s["cot_v"][...].reshape(group, width)
    grad_mixed = jnp.concatenate([mm(cot, w_half(hf, out_cols)) for hf in range(2)], axis=1)
    loads["gain_in"].wait()
    loads["b_out"].wait()
    loads["ctx"].wait()
    row_c.arrive(0)
    for i in range(3):
        emb_c.arrive(i)

    embedded = jnp.concatenate(
        [emb[0].astype(F32) + emb[1].astype(F32), emb[2].astype(F32) + emb[3].astype(F32)], axis=0
    )
    start = s["ctx_v"][...].reshape(group, width).astype(F32) + embedded
    unit_in, inv_in = layer_norm(start)
    gain_in = s["gain_in_v"][...]
    normed = (unit_in * gain_in).astype(BF16)
    slope, qkv, w_att, sm = s["slope"], s["qkv"], s["w_att"], s["sm"]
    gates = []
    for hf in range(2):
        for g in range(4):
            cols = slice(g * half, (g + 1) * half)
            pre = mm(normed, w_half(hf, cols)) + small[hf, g : g + 1, :]
            sig = sigmoid(pre)
            act = pre * sig
            slope[hf, :, cols] = sig + act * (1.0 - sig)
            if g == 0:
                gates.append(act)
            else:
                qkv[hf, g - 1] = (act * 0.125 if g == 2 else act).astype(BF16)
    gate = jnp.concatenate(gates, axis=1)
    low_half = iota((group, 128), 1) < 64

    def split(tile):
        zero = jnp.zeros_like(tile)
        return jnp.where(low_half, tile, zero), jnp.where(low_half, zero, tile)

    attended = []
    for hf in range(2):
        for pair in range(pairs):
            cols = slice(pair * 128, (pair + 1) * 128)
            values, queries = split(qkv[hf, 0, :, cols]), split(qkv[hf, 1, :, cols])
            keys = qkv[hf, 2, :, cols]
            both = None
            for sub in range(2):
                head = hf * heads_half + pair * 2 + sub
                scores = mm_nt(queries[sub], keys) + bias[head]
                sig = sigmoid(scores)
                act = scores * sig
                weights = (act * maskscale[...]).astype(BF16)
                w_att[head] = weights
                sm[head] = (sig + act * (1.0 - sig)) * maskscale[...]
                part = mm(weights, values[sub])
                both = part if both is None else both + part
            attended.append(both)
    unit_out, inv_out = layer_norm(jnp.concatenate(attended, axis=1))
    gain_out = jnp.concatenate([small[0, 10:11, :], small[1, 10:11, :]], axis=1)
    mixed_in = (unit_out * gain_out * gate).astype(BF16)
    projected = None
    for hf in range(2):
        part = mm_nt(mixed_in[:, hf * half : (hf + 1) * half], w_half(hf, out_cols))
        projected = part if projected is None else projected + part
    mixed, mixed_rows = s["mixed"], s["mixed_rows"]
    mixed[...] = (projected + s["b_out_v"][...] + start).astype(BF16)
    mixed_c = copies("mixed")
    for device, to_ka, to_ha in at.quads:
        here = mixed.at[pl.ds(to_ka * tok, tok), pl.ds(pl.multiple_of(to_ha * half, half), half)]
        mixed_c.start(here, mixed_rows.at[at.stream], device)
    own_rows = pl.ds(pl.multiple_of(ka * tok, tok), tok)
    mixed_rows[at.stream] = mixed[own_rows, pl.ds(pl.multiple_of(ha * half, half), half)]

    grad_pre, grad_small = s["grad_pre"], s["grad_small"]
    grad_raw = grad_mixed * unit_out
    grad_gate = grad_raw * gain_out
    grad_gain_out = jnp.sum(grad_raw * gate, axis=0, keepdims=True)
    grad_att = layer_norm_back(grad_mixed * gate * gain_out, unit_out, inv_out).astype(BF16)
    sum_a = WeightSum(at, s["a_own"], "x", s, "a_")
    sums_b = [WeightSum(at, s[f"b{i}_own"], "y", s, f"b{i}_") for i in range(pairs)]

    def put(own, hf, first, value):
        cols = value.shape[1]
        own[hf, :, :, :, first : first + cols] = value.astype(BF16).reshape(own.shape[1:4] + (cols,))

    for hf in range(2):
        cols = slice(hf * half, (hf + 1) * half)
        grad_pre[hf, :, 0:half] = (grad_gate[:, cols] * slope[hf, :, 0:half]).astype(BF16)
        grad_small[hf, 10:11, :] = grad_gain_out[:, cols]
        put(s["a_own"], hf, 0, mm_tn(normed, grad_pre[hf, :, 0:half]))
        put(s["a_own"], hf, half, mm_tn(cot, mixed_in[:, cols]))
    sum_a.cores()

    gs = s["gs"]
    for pair in range(pairs):
        for hf in range(2):
            cols = slice(pair * 128, (pair + 1) * 128)
            values = qkv[hf, 0, :, cols]
            queries, keys = split(qkv[hf, 1, :, cols]), split(qkv[hf, 2, :, cols])
            grads = split(grad_att[:, hf * half + pair * 128 : hf * half + (pair + 1) * 128])
            sums = None
            for sub in range(2):
                head = hf * heads_half + pair * 2 + sub
                grad_scores = (mm_nt(grads[sub], values) * sm[head]).astype(BF16)
                gs[:, head * group : (head + 1) * group] = grad_scores
                found = (
                    mm_tn(w_att[head], grads[sub]),
                    mm(grad_scores, keys[sub]),
                    mm_tn(grad_scores, queries[sub]),
                )
                sums = found if sums is None else [a + b for a, b in zip(sums, found)]
            for g, part in ((1, sums[0]), (2, sums[1] * 0.125), (3, sums[2])):
                there = slice(g * half + pair * 128, g * half + (pair + 1) * 128)
                grad_pre[hf, :, there] = (part * slope[hf, :, there]).astype(BF16)
        if pair == 0:
            sum_a.hop_one()
        if pair < pairs - 1:
            for hf in range(2):
                for g in range(1, 4):
                    there = slice(g * half + pair * 128, g * half + (pair + 1) * 128)
                    put(s[f"b{pair}_own"], hf, (g - 1) * 128, mm_tn(normed, grad_pre[hf, :, there]))
            sums_b[pair].cores()
    grad_normed = None
    for hf in range(2):
        part = mm_nt(grad_pre[hf], w_half(hf, slice(0, 4 * half)))
        grad_normed = part if grad_normed is None else grad_normed + part
    cot32 = cot.astype(F32)
    grad_start, grad_rows = s["grad_start"], s["grad_rows"]
    grad_start[...] = (cot32 + layer_norm_back(grad_normed * gain_in, unit_in, inv_in)).astype(BF16)
    back_c = copies("back")
    for device, to_ka, to_ha in at.quads:
        back_c.start(grad_start.at[pl.ds(to_ka * tok, tok)], grad_rows.at[at.stream], device)
    grad_rows[at.stream] = grad_start[own_rows]
    for hf in range(2):
        for g in range(1, 4):
            there = slice(g * half + (pairs - 1) * 128, g * half + pairs * 128)
            put(s[f"b{pairs - 1}_own"], hf, (g - 1) * 128, mm_tn(normed, grad_pre[hf, :, there]))
    sums_b[-1].cores()
    for i in range(pairs - 1):
        sums_b[i].hop_one()
    gain_grad = jnp.sum(grad_normed * unit_in, axis=0, keepdims=True)
    bout_grad = jnp.sum(cot32, axis=0, keepdims=True)
    for hf in range(2):
        sums = jnp.sum(grad_pre[hf].astype(F32), axis=0, keepdims=True)
        for g in range(4):
            grad_small[hf, g : g + 1, :] = sums[:, g * half : (g + 1) * half]
        grad_small[hf, 11:12, :] = gain_grad[:, hf * half : (hf + 1) * half]
        grad_small[hf, 12:13, :] = bout_grad[:, hf * half : (hf + 1) * half]
        grad_small[hf, 13:16, :] = jnp.zeros((3, half), F32)
    flip = (lane + row == group - 1).astype(F32)
    kept_pairs = lane + row <= group - 1
    hot_cols = one_hot(times_row == row)
    hot_back = one_hot(times_row == group - 1 - row)
    folded = mm(jnp.concatenate([flip.astype(BF16), hot_back], axis=0), gs[...])
    rel_rows, time_rows, early_rows = [], [], []
    for head in range(heads):
        places = slice(head * group, (head + 1) * group)
        rel_rows.append(jnp.sum(skew(folded[:group, places]), axis=0, keepdims=True))
        pairs_sum = mm_nt(folded[group:, places].astype(BF16), hot_cols)
        kept = jnp.where(kept_pairs, pairs_sum, 0.0)
        time_rows.append(jnp.sum(skew(kept), axis=0, keepdims=True))
        early_rows.append(jnp.sum(pairs_sum - kept, axis=0, keepdims=True))
    flipped = mm_exact(jnp.concatenate(rel_rows + time_rows, axis=0), flip)
    early = jnp.sum(jnp.concatenate(early_rows, axis=0), axis=1, keepdims=True)
    late = jnp.sum(flipped[heads:, buckets:], axis=1, keepdims=True)
    place_in = iota((heads, buckets), 1)
    time_grad = flipped[heads:, :buckets] + jnp.where(place_in == 0, early, 0.0) + jnp.where(place_in == buckets - 1, late, 0.0)
    for head in range(heads):
        hf, head_in = divmod(head, heads_half)
        begin = (head_in % 2) * buckets
        grad_small[hf, 4 + head_in : 5 + head_in, :] = flipped[head : head + 1]
        grad_small[hf, 8 + head_in // 2 : 9 + head_in // 2, begin : begin + buckets] = time_grad[head : head + 1]
    small_in, small_mine = s["small_in"], s["small_mine"]
    sum_c = copies("sum")
    sum_c.start(grad_small, small_in.at[0], at.core_peer)
    sum_a.hop_two()

    for i in range(3):
        back_c.arrive(i)
    outgoing, incoming = s["outgoing"], s["incoming"]
    slot_hot = one_hot(place == iota((count, count), 0))
    outgoing[...] = mm(slot_hot, grad_rows[...].reshape(count, width)).astype(BF16).reshape(outgoing.shape)
    give, hand = copies("give"), copies("hand")
    for d in range(1, owners):
        to = at.owner_to(d)
        give.start(outgoing.at[to], incoming.at[at.me, ha], at.owner(to))
    incoming[at.me, ha] = outgoing[at.me]
    hand.start(incoming.at[at.me, ha], incoming.at[at.me, ha], at.x_peer)

    def take(first, last):
        for d in range(first, last):
            give.arrive(d - 1)
            there = incoming.at[at.owner_from(d), ha]
            hand.start(there, there, at.x_peer)

    third = owners // 3
    sums_b[-1].hop_one()
    sum_c.arrive(0)
    small_mine[0] = grad_small[...] + small_in[0]
    sum_c.start(small_mine.at[0], small_in.at[1], at.x_peer)
    for i in range(pairs - 1):
        sums_b[i].hop_two()
    sum_a.hop_z()
    take(1, third)
    sums_b[-1].hop_two()
    sum_c.arrive(1)
    small_mine[1] = small_mine[0] + small_in[1]
    sum_c.start(small_mine.at[1], small_in.at[2], at.y_peer)
    for i in range(pairs - 1):
        sums_b[i].hop_z()
    take(third, 2 * third)
    sum_c.arrive(2)
    small_mine[2] = small_mine[1] + small_in[2]
    for d in range(1, zs):
        sum_c.start(small_mine.at[2], small_in.at[2 + d], at.z_device(d))
    sums_b[-1].hop_z()
    take(2 * third, owners)
    grad_w = s["grad_w"]
    grad_w[:, 0:gates_cols] = sum_a.finish()
    for i in range(pairs):
        first = gates_cols + i * 384
        grad_w[:, first : first + 384] = sums_b[i].finish()
    summed = small_mine[2]
    for d in range(1, zs):
        sum_c.arrive(2 + d)
        summed = summed + small_in[2 + d]
    s["small_sum"][...] = summed
    for i in range(3):
        mixed_c.arrive(i)
    for i in range(owners):
        hand.arrive(i)
    for kind in (req, item, emb_c, row_c, small_c, wz, wx, wy, wc, mixed_c, back_c, give, hand, sum_c):
        kind.sent()
    for part in [sum_a] + sums_b:
        part.copies.sent()


def run_main(inputs):
    pbs, kas = lax.axis_size("pb"), lax.axis_size("ka")
    owners, zs = pbs * kas, pbs // 2
    count, width = inputs["context"].shape
    half, tok, share = width // 2, count // MB, count // owners
    group, heads = 2 * tok, width // 64
    shard_rows = inputs["w_uvqk"].shape[0]
    block = shard_rows // 2
    dma = pltpu.SemaphoreType.DMA
    outs = {
        "incoming": jax.ShapeDtypeStruct((owners, 2, share, width), BF16),
        "ids": jax.ShapeDtypeStruct((1, 2 * count), jnp.int32),
        "grad_rows": jax.ShapeDtypeStruct((MB, tok, width), BF16),
        "mixed_rows": jax.ShapeDtypeStruct((MB, tok, half), BF16),
        "grad_w": jax.ShapeDtypeStruct((block, 5 * half), F32),
        "small_sum": jax.ShapeDtypeStruct((2, 16, half), F32),
    }
    scratch = {
        "ctx_v": pltpu.VMEM((2, tok, width), BF16),
        "cot_v": pltpu.VMEM((2, tok, width), BF16),
        "requests": pltpu.VMEM((owners, 8, 128), jnp.int32),
        "arrived": pltpu.VMEM((owners, 8, 128), jnp.int32),
        "table_buf": pltpu.VMEM(inputs["table"].shape, BF16),
        "total": pltpu.VMEM((count, width), F32),
        "fetched": pltpu.VMEM((owners, share, width), BF16),
        "returned": pltpu.VMEM((owners, share, width), BF16),
        "parts": pltpu.VMEM((MB, tok, width), BF16),
        "emb": pltpu.VMEM((MB, tok, width), BF16),
        "shard": pltpu.VMEM((shard_rows, 5 * half), BF16),
        "w": pltpu.VMEM((2, pbs, shard_rows, 5 * half), BF16),
        "small": pltpu.VMEM((2, 16, half), F32),
        "maskscale": pltpu.VMEM((group, group), F32),
        "bias": pltpu.VMEM((heads, group, group), F32),
        "slope": pltpu.VMEM((2, group, 4 * half), F32),
        "qkv": pltpu.VMEM((2, 3, group, half), BF16),
        "w_att": pltpu.VMEM((heads, group, group), BF16),
        "sm": pltpu.VMEM((heads, group, group), F32),
        "gs": pltpu.VMEM((group, heads * group), BF16),
        "grad_pre": pltpu.VMEM((2, group, 4 * half), BF16),
        "mixed": pltpu.VMEM((group, width), BF16),
        "grad_start": pltpu.VMEM((group, width), BF16),
        "grad_small": pltpu.VMEM((2, 16, half), F32),
        "outgoing": pltpu.VMEM((owners, share, width), BF16),
        "small_mine": pltpu.VMEM((3, 2, 16, half), F32),
        "small_in": pltpu.VMEM((2 + zs, 2, 16, half), F32),
        "load_sem": dma((14,)),
        "table_sem": dma((8,)),
    }
    for name in ("owner", "offset", "w_uvqk", "w_out", "b", "rel", "time", "gain_out", "gain_in", "b_out", "lengths", "times"):
        scratch[name + "_v"] = pltpu.VMEM(inputs[name].shape, inputs[name].dtype)
    for name, number in (
        ("req", owners - 1), ("item", owners - 1), ("emb", 3), ("row", 2), ("small", 1), ("wz", zs - 1), ("wx", zs),
        ("wy", 2 * zs - 2), ("wc", 2 * zs), ("mixed", 3), ("back", 3), ("give", owners - 1), ("hand", owners), ("sum", 2 + zs),
    ):
        scratch[name + "_send"] = dma((number,))
        scratch[name + "_recv"] = dma((number,))
    scratch |= weight_sum_scratch("a_", "x", zs, block, 2 * half)
    for i in range(half // 128):
        scratch |= weight_sum_scratch(f"b{i}_", "y", zs, block, 384)
    vmem = pl.BlockSpec(memory_space=pltpu.VMEM)
    found = pl.pallas_call(
        functools.partial(main_kernel, tuple(inputs), tuple(outs), tuple(scratch)),
        out_shape=tuple(outs.values()),
        in_specs=[pl.BlockSpec(memory_space=pltpu.HBM)] * len(inputs),
        out_specs=(vmem,) * len(outs),
        scratch_shapes=list(scratch.values()),
        compiler_params=pltpu.CompilerParams(
            collective_id=1, has_side_effects=True, vmem_limit_bytes=58 * 1024 * 1024
        ),
    )(*inputs.values())
    return dict(zip(outs, found, strict=True))


def scatter_kernel(ids_ref, rows_ref, grad_w_ref, small_ref, out_ref, w_ref, w_out_ref, b_ref, rel_ref, time_ref, gain_in_ref, gain_out_ref, b_out_ref):
    tile = out_ref.shape[0]
    row = iota((tile, ids_ref.shape[1]), 0) + pl.program_id(0) * tile
    out_ref[...] = mm(one_hot(ids_ref[...] == row), rows_ref[...])

    @pl.when(pl.program_id(0) == 0)
    def _():
        half = w_ref.shape[2]
        buckets = time_ref.shape[1]
        w_ref[:, 0, :] = grad_w_ref[:, 0:half]
        w_out_ref[...] = grad_w_ref[:, half : 2 * half]
        for pair in range(half // 128):
            for g in range(1, 4):
                first = 2 * half + pair * 384 + (g - 1) * 128
                w_ref[:, g, pair * 128 : (pair + 1) * 128] = grad_w_ref[:, first : first + 128]
        ha = lax.axis_index("ha")
        b_ref[...] = small_ref[ha, 0:4, :]
        rel_ref[...] = small_ref[ha, 4:8, :]
        for i in range(2):
            for j in range(2):
                time_ref[2 * i + j : 2 * i + j + 1, :] = small_ref[ha, 8 + i : 9 + i, j * buckets : (j + 1) * buckets]
        gain_out_ref[...] = small_ref[ha, 10:11, :]
        for hf in range(2):
            gain_in_ref[:, hf * half : (hf + 1) * half] = small_ref[hf, 11:12, :]
            b_out_ref[:, hf * half : (hf + 1) * half] = small_ref[hf, 12:13, :]


def scatter_rows(ids, rows, grad_w, small, table_rows, buckets, tile=512):
    count, width = rows.shape
    half, block = width // 2, grad_w.shape[0]

    def whole(shape):
        return pl.BlockSpec(shape, lambda i: (0,) * len(shape))

    shapes = [(block, 4, half), (block, half), (4, half), (4, half), (4, buckets), (1, width), (1, half), (1, width)]
    return pl.pallas_call(
        scatter_kernel,
        grid=(table_rows // tile,),
        out_shape=[jax.ShapeDtypeStruct(shape, F32) for shape in [(table_rows, width)] + shapes],
        in_specs=[whole((1, count)), whole((count, width)), whole(grad_w.shape), whole(small.shape)],
        out_specs=[pl.BlockSpec((tile, width), lambda i: (i, 0))] + [whole(shape) for shape in shapes],
        compiler_params=pltpu.CompilerParams(vmem_limit_bytes=40 * 1024 * 1024),
    )(ids, rows, grad_w, small)


def local_streams(
    context,
    item_owner,
    item_offset,
    lengths,
    times,
    table,
    cotangent,
    ln_in_gain,
    w_uvqk,
    b_uvqk,
    rel_bias,
    time_bias,
    ln_out_gain,
    w_out,
    b_out,
):
    row_count, width = context.shape
    half = width // 2
    found = run_main(
        {
            "owner": item_owner.reshape(1, row_count),
            "offset": item_offset.reshape(1, row_count),
            "context": context,
            "cot": cotangent,
            "table": table,
            "w_uvqk": w_uvqk,
            "w_out": w_out.T,
            "b": b_uvqk,
            "rel": rel_bias,
            "time": time_bias,
            "gain_out": ln_out_gain.reshape(1, half),
            "gain_in": ln_in_gain.reshape(1, width),
            "b_out": b_out.reshape(1, width),
            "lengths": lengths[0],
            "times": times[0],
        }
    )
    table_grad, grad_w, grad_w_out, grad_b, grad_rel, grad_time, grad_gain_in, grad_gain_out, grad_b_out = scatter_rows(
        found["ids"],
        found["incoming"].reshape(2 * row_count, width),
        found["grad_w"],
        found["small_sum"],
        table.shape[0],
        time_bias.shape[1],
    )
    return (
        found["mixed_rows"].reshape(row_count, half),
        found["grad_rows"].reshape(row_count, width),
        table_grad,
        grad_gain_in.reshape(width),
        grad_w,
        grad_b,
        grad_rel,
        grad_time,
        grad_gain_out.reshape(half),
        grad_w_out.T,
        grad_b_out.reshape(width),
    )


def solution(mesh):
    one_stream = mesh.shape["ka"] * mesh.shape["ha"] == MB and mesh.shape["ka"] == 2
    return jax.shard_map(
        local_streams if one_stream else local_general,
        mesh=mesh,
        in_specs=(
            P(("pb", "ka"), None),
            P(("pb", "ka"), None),
            P(("pb", "ka")),
            P("pb", None, None),
            P("pb", None, None),
            P(("pb", "ka"), None),
            P(("pb", "ka"), None),
            P(),
            P("pb", None, "ha"),
            P(None, "ha"),
            P("ha", None),
            P("ha", None),
            P("ha"),
            P("ha", "pb"),
            P(),
        ),
        out_specs=(
            P(("pb", "ka"), "ha"),
            P(("pb", "ka"), None),
            P(("pb", "ka"), None),
            P(),
            P(("pb", "ka"), None, "ha"),
            P(None, "ha"),
            P("ha", None),
            P("ha", None),
            P("ha"),
            P("ha", ("pb", "ka")),
            P(),
        ),
        check_vma=False,
    )
```

```python
import functools

import jax
import jax.numpy as jnp
from jax import lax
from jax.experimental import pallas as pl
from jax.experimental.pallas import tpu as pltpu
from jax.sharding import PartitionSpec as P

DH = 64
TOK_DEV = 128
MB = 4
SEQ_GRP = 4
F32 = jnp.float32
BF16 = jnp.bfloat16


epsilon = 1e-05


def silu_slope(values):
    sigma = jax.nn.sigmoid(values)
    return sigma * (1.0 + values * (1.0 - sigma))


def norm_rows(values, gain):
    centered = values - jnp.mean(values, axis=-1, keepdims=True)
    inverse = lax.rsqrt(jnp.mean(centered * centered, axis=-1, keepdims=True) + epsilon)
    unit_rows = centered * inverse
    return (unit_rows * gain, unit_rows, inverse)


def norm_back(grad_unit, unit_rows, inverse):
    first_mean = jnp.mean(grad_unit, axis=-1, keepdims=True)
    second_mean = jnp.mean(grad_unit * unit_rows, axis=-1, keepdims=True)
    return inverse * (grad_unit - first_mean - unit_rows * second_mean)


def stream_layout(lengths_row, group):
    places = jnp.arange(group, dtype=jnp.int32)
    ends = jnp.cumsum(lengths_row, dtype=jnp.int32)
    member = jnp.sum((ends[None, :] <= places[:, None]).astype(jnp.int32), axis=1)
    onehot = (member[:, None] == jnp.arange(SEQ_GRP, dtype=jnp.int32)[None, :]).astype(jnp.float32)
    counted = jnp.maximum(jnp.sum(onehot * lengths_row.astype(jnp.float32)[None, :], axis=1), 1.0)
    return (places, member, counted)


def diagonal_bias(rel_bias, query_first, key_first, query_len, key_len):
    heads, group = rel_bias.shape
    span = query_len + key_len - 1
    padded = jnp.concatenate([jnp.zeros((heads, group), jnp.float32), rel_bias], axis=1)
    window = lax.dynamic_slice_in_dim(
        padded, query_first - key_first - key_len + 1 + group, span, 1
    )
    flipped = jnp.concatenate([window[:, ::-1], jnp.zeros((heads, 1), jnp.float32)], axis=1)
    skewed = jnp.tile(flipped, (1, query_len))[:, : query_len * span].reshape(
        heads, query_len, span
    )
    return skewed[:, :, query_len - 1 : query_len - 1 + key_len]


def diagonal_sums(grad_scores, query_first, key_first, group):
    heads, query_len, key_len = grad_scores.shape
    span = query_len + key_len - 1
    widened = jnp.pad(grad_scores.astype(jnp.float32), ((0, 0), (0, 0), (query_len - 1, 0)))
    flat = jnp.pad(widened.reshape(heads, query_len * span), ((0, 0), (0, query_len)))
    totals = jnp.sum(flat.reshape(heads, query_len, span + 1), axis=1)
    window = totals[:, :span][:, ::-1]
    placed = lax.dynamic_update_slice_in_dim(
        jnp.zeros((heads, 2 * group), jnp.float32),
        window,
        query_first - key_first - key_len + 1 + group,
        1,
    )
    return placed[:, group:]


def bucket_lookup(time_bias, bucket_hot):
    high = time_bias.astype(jnp.bfloat16)
    rest = time_bias - high.astype(jnp.float32)
    middle = rest.astype(jnp.bfloat16)
    lowest = (rest - middle.astype(jnp.float32)).astype(jnp.bfloat16)
    pieces = jnp.einsum(
        "phb,qkb->phqk",
        jnp.stack([high, middle, lowest]),
        bucket_hot,
        preferred_element_type=jnp.float32,
    )
    return pieces[0] + pieces[1] + pieces[2]


def tile_scores(query_heads, key_heads, query_info, key_info, rel_bias, time_bias):
    query_pos, query_member, query_count, query_stamp = query_info
    key_pos, key_member, key_stamp = key_info
    distance = query_pos[:, None] - key_pos[None, :]
    time_index = jnp.clip(query_stamp[:, None] - key_stamp[None, :], 0, time_bias.shape[1] - 1)
    bucket_hot = (
        time_index[:, :, None] == jnp.arange(time_bias.shape[1], dtype=jnp.int32)[None, None, :]
    ).astype(jnp.bfloat16)
    scores = jnp.einsum(
        "qhd,khd->hqk", query_heads, key_heads, preferred_element_type=jnp.float32
    ) * DH ** (-0.5)
    scores = (
        scores
        + diagonal_bias(rel_bias, query_pos[0], key_pos[0], query_pos.shape[0], key_pos.shape[0])
        + bucket_lookup(time_bias, bucket_hot)
    )
    allowed = (
        (query_member[:, None] == key_member[None, :])
        & (query_member[:, None] < SEQ_GRP)
        & (distance >= 0)
    )[None]
    weights = (jnp.where(allowed, jax.nn.silu(scores), 0.0) / query_count[None, :, None]).astype(
        jnp.bfloat16
    )
    return (scores, allowed, weights, bucket_hot)


def score_grads(grad_weights, scores, allowed, query_count):
    return (
        jnp.where(allowed, grad_weights / query_count[None, :, None], 0.0) * silu_slope(scores)
    ).astype(jnp.bfloat16)


def local_general(
    context,
    item_owner,
    item_offset,
    lengths,
    times,
    table,
    cotangent,
    ln_in_gain,
    w_uvqk,
    b_uvqk,
    rel_bias,
    time_bias,
    ln_out_gain,
    w_out,
    b_out,
):
    owners = lax.axis_size(("pb", "ka"))
    row_count = context.shape[0]
    width = context.shape[1]
    capacity = max(2, 2 * row_count // owners)
    owner_ids = item_owner[:, 0]
    owner_hits = (owner_ids[:, None] == jnp.arange(owners, dtype=jnp.int32)[None, :]).astype(
        jnp.int32
    )
    earlier = jnp.sum((jnp.cumsum(owner_hits, axis=0) - owner_hits) * owner_hits, axis=1)
    slot_index = owner_ids * capacity + earlier
    requests = jnp.zeros((owners * capacity,), jnp.int32).at[slot_index].set(item_offset + 1)
    arrived = lax.all_to_all(
        requests.reshape(owners, capacity), ("pb", "ka"), split_axis=0, concat_axis=0, tiled=True
    ).reshape(-1)
    present = arrived > 0
    local_rows = jnp.maximum(arrived - 1, 0)
    fetched = jnp.where(present[:, None], table[local_rows], jnp.zeros((), jnp.bfloat16))
    returned = lax.all_to_all(
        fetched.reshape(owners, capacity, width),
        ("pb", "ka"),
        split_axis=0,
        concat_axis=0,
        tiled=True,
    )
    embedded = returned.reshape(owners * capacity, width)[slot_index]
    start = context.astype(jnp.float32) + embedded.astype(jnp.float32)
    group = lax.axis_size("ka") * TOK_DEV
    block_start = lax.axis_index("ka") * TOK_DEV
    half_cols = w_out.shape[0]
    heads = half_cols // DH
    full_cols = half_cols * lax.axis_size("ha")
    out_cols = width // lax.axis_size("ha")
    out_start = lax.axis_index("ha") * out_cols
    bias_half = lax.dynamic_slice_in_dim(b_out, out_start, out_cols)
    scale = DH ** (-0.5)
    grad_gain_in = jnp.zeros(ln_in_gain.shape, jnp.float32)
    grad_bias_proj = jnp.zeros(b_uvqk.shape, jnp.float32)
    grad_rel = jnp.zeros(rel_bias.shape, jnp.float32)
    grad_time = jnp.zeros(time_bias.shape, jnp.float32)
    grad_gain_out = jnp.zeros(ln_out_gain.shape, jnp.float32)
    grad_bias_out = jnp.zeros(b_out.shape, jnp.float32)
    weight_total = None
    mixed_parts = []
    grad_parts = []
    for micro in range(MB):
        w_full, w_final = (
            lax.all_gather(w_uvqk, "pb", axis=0, tiled=True),
            lax.all_gather(w_out, "pb", axis=1, tiled=True),
        )
        x_in = start[micro * TOK_DEV : (micro + 1) * TOK_DEV]
        cot_rows = cotangent[micro * TOK_DEV : (micro + 1) * TOK_DEV]
        stamps = times[0, micro]
        places, member, counted = stream_layout(lengths[0, micro], group)
        query_pos = lax.dynamic_slice_in_dim(places, block_start, TOK_DEV)
        query_member = lax.dynamic_slice_in_dim(member, block_start, TOK_DEV)
        query_count = lax.dynamic_slice_in_dim(counted, block_start, TOK_DEV)
        query_stamp = lax.dynamic_slice_in_dim(stamps, block_start, TOK_DEV)
        normed_float, unit_in, inverse_in = norm_rows(x_in, ln_in_gain)
        normed = normed_float.astype(jnp.bfloat16)
        pre_act = (
            jnp.einsum("td,dgc->tgc", normed, w_full, preferred_element_type=jnp.float32) + b_uvqk
        )
        activated = jax.nn.silu(pre_act)
        gate_part = activated[:, 0]
        values = activated[:, 1].astype(jnp.bfloat16)
        queries = activated[:, 2].astype(jnp.bfloat16)
        key_rows = activated[:, 3].astype(jnp.bfloat16)
        key_pair = lax.all_gather(jnp.stack([key_rows, values]), "ka", axis=1, tiled=True)
        all_keys = key_pair[0].reshape(group, heads, DH)
        all_values = key_pair[1].reshape(group, heads, DH)
        query_heads = queries.reshape(TOK_DEV, heads, DH)
        scores, allowed, weights, bucket_hot = tile_scores(
            query_heads,
            all_keys,
            (query_pos, query_member, query_count, query_stamp),
            (places, member, stamps),
            rel_bias,
            time_bias,
        )
        attended = jnp.einsum(
            "hqk,khd->qhd", weights, all_values, preferred_element_type=jnp.float32
        ).reshape(TOK_DEV, half_cols)
        row_total, row_square = lax.psum(
            (jnp.sum(attended, axis=1), jnp.sum(attended * attended, axis=1)), "ha"
        )
        row_mean = row_total / full_cols
        inverse_out = lax.rsqrt(row_square / full_cols - row_mean * row_mean + epsilon)[:, None]
        unit_out = (attended - row_mean[:, None]) * inverse_out
        mixed_in = (unit_out * ln_out_gain * gate_part).astype(jnp.bfloat16)
        partial_out = jnp.dot(mixed_in, w_final, preferred_element_type=jnp.float32)
        summed_out = lax.psum_scatter(partial_out, "ha", scatter_dimension=1, tiled=True)
        residual = lax.dynamic_slice_in_dim(x_in, out_start, out_cols, 1)
        mixed_parts.append((summed_out + bias_half + residual).astype(jnp.bfloat16))
        grad_final_part = jnp.einsum(
            "tc,td->cd", mixed_in, cot_rows, preferred_element_type=jnp.float32
        )
        grad_bias_out = grad_bias_out + jnp.sum(cot_rows.astype(jnp.float32), axis=0)
        grad_mixed = jnp.einsum("td,cd->tc", cot_rows, w_final, preferred_element_type=jnp.float32)
        grad_gate = grad_mixed * unit_out * ln_out_gain
        grad_gain_out = grad_gain_out + jnp.sum(grad_mixed * unit_out * gate_part, axis=0)
        grad_unit = grad_mixed * gate_part * ln_out_gain
        first_total, second_total = lax.psum(
            (jnp.sum(grad_unit, axis=1), jnp.sum(grad_unit * unit_out, axis=1)), "ha"
        )
        grad_attended = (
            inverse_out
            * (
                grad_unit
                - first_total[:, None] / full_cols
                - unit_out * second_total[:, None] / full_cols
            )
        ).astype(jnp.bfloat16)
        grad_heads = grad_attended.reshape(TOK_DEV, heads, DH)
        grad_weights = jnp.einsum(
            "qhd,khd->hqk", grad_heads, all_values, preferred_element_type=jnp.float32
        )
        grad_scores = score_grads(grad_weights, scores, allowed, query_count)
        grad_rel = grad_rel + diagonal_sums(grad_scores, query_pos[0], places[0], rel_bias.shape[1])
        grad_time = grad_time + jnp.einsum(
            "hqk,qkb->hb", grad_scores, bucket_hot, preferred_element_type=jnp.float32
        )
        grad_queries = (
            jnp.einsum("hqk,khd->qhd", grad_scores, all_keys, preferred_element_type=jnp.float32)
            * scale
        ).reshape(TOK_DEV, half_cols)
        key_part = (
            jnp.einsum("hqk,qhd->khd", grad_scores, query_heads, preferred_element_type=jnp.float32)
            * scale
        )
        value_part = jnp.einsum(
            "hqk,qhd->khd", weights, grad_heads, preferred_element_type=jnp.float32
        )
        stacked = jnp.stack(
            [key_part.reshape(group, half_cols), value_part.reshape(group, half_cols)]
        )
        owned_grads = lax.psum_scatter(stacked, "ka", scatter_dimension=1, tiled=True)
        grad_keys = owned_grads[0]
        grad_values = owned_grads[1]
        grad_act = jnp.stack([grad_gate, grad_values, grad_queries, grad_keys], axis=1)
        grad_pre = (grad_act * silu_slope(pre_act)).astype(jnp.bfloat16)
        grad_proj_part = jnp.einsum(
            "td,tgc->dgc", normed, grad_pre, preferred_element_type=jnp.float32
        )
        grad_bias_proj = grad_bias_proj + jnp.sum(grad_pre.astype(jnp.float32), axis=0)
        grad_normed = lax.psum(
            jnp.einsum("tgc,dgc->td", grad_pre, w_full, preferred_element_type=jnp.float32), "ha"
        )
        grad_gain_in = grad_gain_in + jnp.sum(grad_normed * unit_in, axis=0)
        grad_parts.append(
            cot_rows.astype(jnp.float32) + norm_back(grad_normed * ln_in_gain, unit_in, inverse_in)
        )
        local_pair = (grad_proj_part, grad_final_part)
        local_pair = (
            lax.psum_scatter(local_pair[0], ("pb", "ka"), scatter_dimension=0, tiled=True),
            lax.psum_scatter(local_pair[1], ("pb", "ka"), scatter_dimension=1, tiled=True),
        )
        weight_total = (
            local_pair if weight_total is None else jax.tree.map(jnp.add, weight_total, local_pair)
        )
    grad_start = jnp.concatenate(grad_parts, axis=0)
    outgoing = jnp.zeros((owners * capacity, width), jnp.float32).at[slot_index].set(grad_start)
    incoming = lax.all_to_all(
        outgoing.reshape(owners, capacity, width),
        ("pb", "ka"),
        split_axis=0,
        concat_axis=0,
        tiled=True,
    ).reshape(owners * capacity, width)
    table_grad = jax.ops.segment_sum(
        jnp.where(present[:, None], incoming, 0.0), local_rows, num_segments=table.shape[0]
    )
    small_total = lax.psum(
        (grad_gain_in, grad_bias_proj, grad_rel, grad_time, grad_gain_out, grad_bias_out),
        ("pb", "ka"),
    )
    mixed = jnp.concatenate(mixed_parts, axis=0)
    return (
        mixed,
        grad_start.astype(jnp.bfloat16),
        table_grad,
        small_total[0],
        weight_total[0],
        small_total[1],
        small_total[2],
        small_total[3],
        small_total[4],
        weight_total[1],
        small_total[5],
    )


MESH = pl.DeviceIdType.MESH


def remote(src, dst, send_sem, recv_sem, device):
    return pltpu.make_async_remote_copy(
        src_ref=src, dst_ref=dst, send_sem=send_sem, recv_sem=recv_sem, device_id=device, device_id_type=MESH
    )


def mm(a, b):
    return jnp.dot(a, b, preferred_element_type=F32)


def mm_nt(a, b):
    return lax.dot_general(a, b, (((1,), (1,)), ((), ())), preferred_element_type=F32)


def mm_tn(a, b):
    return lax.dot_general(a, b, (((0,), (0,)), ((), ())), preferred_element_type=F32)


def mm_exact(a, b):
    return jnp.dot(a, b, preferred_element_type=F32, precision=lax.Precision.HIGHEST)


def sigmoid(v):
    return 0.5 * jnp.tanh(0.5 * v) + 0.5


def skew(tile):
    return pltpu.roll(tile, 0, 1, stride=1, stride_axis=0)


def iota(shape, dim):
    return lax.broadcasted_iota(jnp.int32, shape, dim)


def one_hot(equal):
    return equal.astype(F32).astype(BF16)


def layer_norm(values):
    centered = values - jnp.mean(values, axis=1, keepdims=True)
    inverse = lax.rsqrt(jnp.mean(centered * centered, axis=1, keepdims=True) + epsilon)
    return centered * inverse, inverse


def layer_norm_back(grad_unit, unit, inverse):
    first = jnp.mean(grad_unit, axis=1, keepdims=True)
    second = jnp.mean(grad_unit * unit, axis=1, keepdims=True)
    return inverse * (grad_unit - first - unit * second)


class Place:
    def __init__(self):
        self.pbs, self.kas = lax.axis_size("pb"), lax.axis_size("ka")
        self.owners, self.zs = self.pbs * self.kas, self.pbs // 2
        self.pb, self.ka, self.ha = lax.axis_index("pb"), lax.axis_index("ka"), lax.axis_index("ha")
        self.z, self.core = self.pb // 2, self.pb % 2
        self.me = self.pb * self.kas + self.ka
        self.stream = 2 * self.ka + self.ha
        self.x_peer = (self.pb, self.ka, 1 - self.ha)
        self.y_peer = (self.pb, 1 - self.ka, self.ha)
        self.xy_peer = (self.pb, 1 - self.ka, 1 - self.ha)
        self.core_peer = (2 * self.z + 1 - self.core, self.ka, self.ha)
        self.quads = [
            (self.x_peer, self.ka, 1 - self.ha),
            (self.y_peer, 1 - self.ka, self.ha),
            (self.xy_peer, 1 - self.ka, 1 - self.ha),
        ]

    def owner(self, index):
        return (index // self.kas, index % self.kas, self.ha)

    def owner_to(self, d):
        return lax.rem(self.me + d, self.owners)

    def owner_from(self, d):
        return lax.rem(self.me - d + self.owners, self.owners)

    def z_to(self, d):
        return lax.rem(self.z + d, self.zs)

    def z_device(self, d):
        return (2 * self.z_to(d) + self.core, self.ka, self.ha)

    def z_from(self, d):
        return 2 * lax.rem(self.z - d + self.zs, self.zs) + self.core


class Copies:
    def __init__(self, send, recv):
        self.send, self.recv, self.copies = send, recv, []

    def start(self, src, dst, device):
        i = len(self.copies)
        copy = remote(src, dst, self.send.at[i], self.recv.at[i], device)
        copy.start()
        self.copies.append(copy)

    def arrive(self, i):
        self.copies[i].wait_recv()

    def sent(self):
        for copy in self.copies:
            copy.wait_send()


class WeightSum:
    def __init__(self, at, order, s, name):
        self.at, self.order = at, order
        self.own, self.core_in = s[name + "own"], s[name + "core_in"]
        self.mine = [s[f"{name}mine{i}"] for i in range(3)]
        self.other = [s[f"{name}other{i}"] for i in range(3)]
        self.copies = Copies(s[name + "send"], s[name + "recv"])
        self.begun = [0]

    def pick(self, ref, axis, index):
        left = [a for a in "xzy" if a not in self.order[: self.order.index(axis)]]
        return ref.at[(slice(None),) * left.index(axis) + (index,)]

    def peers(self, axis):
        at = self.at
        if axis == "x":
            return [(at.x_peer, 1 - at.ha)]
        if axis == "y":
            return [(at.y_peer, 1 - at.ka)]
        return [(at.z_device(d), at.z_to(d)) for d in range(1, at.zs)]

    def own_index(self, axis):
        return {"x": self.at.ha, "y": self.at.ka, "z": self.at.z}[axis]

    def cores(self):
        self.copies.start(self.own.at[:, :, 1 - self.at.core], self.core_in, self.at.core_peer)

    def send(self, i):
        axis = self.order[i]
        self.begun.append(len(self.copies.copies))
        for k, (device, index) in enumerate(self.peers(axis)):
            self.copies.start(self.pick(self.mine[i], axis, index), self.other[i].at[k], device)

    def received(self, i):
        axis = self.order[i]
        total = self.pick(self.mine[i], axis, self.own_index(axis))[...].astype(F32)
        for k in range(len(self.peers(axis))):
            self.copies.arrive(self.begun[i + 1] + k)
            total = total + self.other[i][k].astype(F32)
        return total

    def hop(self, i):
        if i == 0:
            self.copies.arrive(0)
            for h in range(2):
                total = self.own[h, :, self.at.core].astype(F32) + self.core_in[h].astype(F32)
                self.mine[0][h] = total.astype(BF16).reshape(self.mine[0].shape[1:])
        else:
            self.mine[i][...] = self.received(i - 1).astype(BF16)
        self.send(i)

    def finish(self):
        return self.received(2)


def weight_sum_scratch(name, order, zs, block, cols):
    dma = pltpu.SemaphoreType.DMA
    sizes = {"x": 2, "z": zs, "y": 2}
    found = {
        name + "own": pltpu.VMEM((2, zs, 2, 2 * block, cols), BF16),
        name + "core_in": pltpu.VMEM((2, zs, 2 * block, cols), BF16),
    }
    for i, axis in enumerate(order):
        before = [sizes[a] for a in "xzy" if a not in order[:i]]
        after = [sizes[a] for a in "xzy" if a not in order[: i + 1]]
        found[f"{name}mine{i}"] = pltpu.VMEM((*before, block, cols), BF16)
        found[f"{name}other{i}"] = pltpu.VMEM((sizes[axis] - 1, *after, block, cols), BF16)
    found[name + "send"] = dma((2 + zs,))
    found[name + "recv"] = dma((2 + zs,))
    return found


def main_kernel(in_names, out_names, scratch_names, *refs):
    names = in_names + out_names + scratch_names
    s = dict(zip(names, refs, strict=True))
    s["limit_rows"] = 256
    at = Place()
    owners, zs, ka, ha = at.owners, at.zs, at.ka, at.ha
    count, width = s["context"].shape
    half = width // 2
    tok = count // MB
    group = 2 * tok
    share = count // owners
    capacity = 2 * share
    block = s["w_uvqk"].shape[0] // 2
    heads_half = half // 64
    heads = 2 * heads_half
    pairs = half // 128
    buckets = s["time"].shape[1]
    gates_cols = 2 * half

    table, table_buf, table_sem = s["table"], s["table_buf"], s["table_sem"]
    chunks = table_sem.shape[0]
    chunk = table.shape[0] // chunks

    def local(i, src, dst):
        copy = pltpu.make_async_copy(src, dst, s["load_sem"].at[i])
        copy.start()
        return copy

    mine = pl.ds(pl.multiple_of(at.stream * tok, tok), tok)
    away = pl.ds(pl.multiple_of((2 * (1 - ka) + ha) * tok, tok), tok)
    loads = {}
    for i, name in enumerate(
        ("owner", "offset", "w_uvqk", "w_out", "b", "rel", "time", "gain_out", "gain_in", "b_out", "lengths", "times")
    ):
        loads[name] = local(i, s[name], s[name + "_v"])
    loads["ctx"] = local(12, s["context"].at[mine], s["ctx_v"].at[ka])
    loads["cot"] = local(13, s["cot"].at[mine], s["cot_v"].at[ka])
    for i in range(chunks):
        rows = pl.ds(i * chunk, chunk)
        pltpu.make_async_copy(table.at[rows], table_buf.at[rows], table_sem.at[i]).start()
    barrier = pltpu.get_barrier_semaphore()
    partners = [at.owner(at.owner_to(d)) for d in range(1, owners)] + [at.x_peer, at.xy_peer]
    for device in partners:
        pl.semaphore_signal(barrier, inc=1, device_id=device, device_id_type=MESH)

    loads["owner"].wait()
    loads["offset"].wait()
    owner_row, offset_row = s["owner_v"][...], s["offset_v"][...]
    hits = (owner_row == iota((owners, count), 0)).astype(F32)
    earlier = mm(hits.astype(BF16), one_hot(iota((count, count), 0) < iota((count, count), 1)))
    rank = jnp.sum(hits * earlier, axis=0, keepdims=True).astype(jnp.int32)
    rank_hot = one_hot(rank == iota((128, count), 0))
    high = (offset_row // 64).astype(F32)
    low = (offset_row % 64 + 1).astype(F32)
    asked = 64.0 * mm_nt((hits * high).astype(BF16), rank_hot) + mm_nt((hits * low).astype(BF16), rank_hot) - 1.0
    asked = asked.astype(jnp.int32)
    for o in range(owners):
        s["requests"][o] = jnp.broadcast_to(asked[o : o + 1], (8, 128))
    place = rank - ha * share
    place = jnp.where((place >= 0) & (place < share), owner_row * share + place, -1)

    shard, w, small = s["shard"], s["w"], s["small"]
    loads["w_uvqk"].wait()
    for g in range(4):
        shard[:, g * half : (g + 1) * half] = s["w_uvqk_v"][:, g, :]
    loads["w_out"].wait()
    shard[:, 4 * half :] = s["w_out_v"][...]
    w[ha, at.pb] = shard[...]
    for name in ("b", "rel", "time", "gain_out"):
        loads[name].wait()
    small[ha, 0:4] = s["b_v"][...]
    small[ha, 4:8] = s["rel_v"][...]
    for i in range(2):
        for j in range(2):
            small[ha, 8 + i : 9 + i, j * buckets : (j + 1) * buckets] = s["time_v"][2 * i + j : 2 * i + j + 1]
    small[ha, 10:11] = s["gain_out_v"][...]

    pl.semaphore_wait(barrier, len(partners))

    def copies(name):
        return Copies(s[name + "_send"], s[name + "_recv"])

    requests, arrived = s["requests"], s["arrived"]
    req, item, emb_c, row_c, small_c = copies("req"), copies("item"), copies("emb"), copies("row"), copies("small")
    wz, wx, wy, wc = copies("wz"), copies("wx"), copies("wy"), copies("wc")
    for d in range(1, owners):
        to = at.owner_to(d)
        req.start(requests.at[to], arrived.at[at.me], at.owner(to))
    arrived[at.me] = requests[at.me]
    my_half = pl.ds(pl.multiple_of(ka * block, block), block)
    for d in range(1, zs):
        wz.start(shard.at[my_half], w.at[ha, at.pb, my_half], at.z_device(d))
    wx.start(shard, w.at[ha, at.pb], at.x_peer)
    small_c.start(small.at[ha], small.at[ha], at.x_peer)
    row_c.start(s["context"].at[away], s["ctx_v"].at[ka], at.y_peer)
    row_c.start(s["cot"].at[away], s["cot_v"].at[ka], at.y_peer)
    wc.start(shard, w.at[ha, at.pb], at.core_peer)

    for i in range(owners - 1):
        req.arrive(i)
    def column_of(source, first):
        tile = jnp.broadcast_to(arrived[source, 0:1], (share, 128)).astype(F32)
        there = iota((share, 128), 1) == iota((share, 128), 0) + first
        return jnp.sum(jnp.where(there, tile, 0.0), axis=1, keepdims=True)

    fetched, returned, parts, emb = s["fetched"], s["returned"], s["parts"], s["emb"]
    total = s["total"]
    askers = owners // 2

    def look_up(part):
        wanted = [column_of(at.owner_to(part * askers + d + 1), ha * share) for d in range(askers)]
        column = jnp.concatenate(wanted, axis=0).astype(jnp.int32)
        total[...] = jnp.zeros_like(total)

        def step(i, carry):
            rows = pl.ds(pl.multiple_of(i * chunk, chunk), chunk)
            if part == 0:
                pltpu.make_async_copy(table.at[rows], table_buf.at[rows], table_sem.at[i]).wait()
            total[...] += mm(one_hot(column == iota((askers * share, chunk), 1) + i * chunk), table_buf[rows])
            return carry

        lax.fori_loop(0, chunks, step, 0)
        fetched[part] = total[...].astype(BF16).reshape(fetched.shape[1:])
        for d in range(askers):
            to = at.owner_to(part * askers + d + 1)
            if part * askers + d + 1 < owners:
                item.start(fetched.at[part, d], returned.at[at.me], at.owner(to))
            else:
                returned[at.me] = fetched[part, d]

    look_up(0)
    for d in range(1, zs):
        wz.arrive(d - 1)
        there = w.at[ha, at.z_from(d), my_half]
        wx.start(there, there, at.x_peer)
        wy.start(there, there, at.y_peer)
    look_up(1)
    wx.arrive(0)
    there = w.at[1 - ha, at.pb]
    wc.start(there, there, at.core_peer)
    for d in range(1, zs):
        wx.arrive(d)
        there = w.at[1 - ha, at.z_from(d), my_half]
        wy.start(there, there, at.y_peer)

    loads["lengths"].wait()
    loads["times"].wait()
    small_c.arrive(0)
    lane, row = iota((group, group), 1), iota((group, group), 0)
    lengths = s["lengths_v"][pl.ds(at.stream, 1), :]
    ends = jnp.zeros((1, 1), jnp.int32)
    member_row = jnp.zeros((group, group), jnp.int32)
    member_col = jnp.zeros((group, group), jnp.int32)
    inv_count = jnp.zeros((group, group), F32)
    for i in range(SEQ_GRP):
        length = lengths[:, i : i + 1]
        inside = (row >= ends) & (row < ends + length)
        inv_count = jnp.where(inside, 1.0 / jnp.maximum(length, 1).astype(F32), inv_count)
        ends = ends + length
        member_row = member_row + (ends <= row).astype(jnp.int32)
        member_col = member_col + (ends <= lane).astype(jnp.int32)
    allowed = (member_row == member_col) & (member_row < SEQ_GRP) & (lane <= row)
    maskscale = s["maskscale"]
    maskscale[...] = jnp.where(allowed, inv_count, 0.0)
    times_row = jnp.broadcast_to(s["times_v"][pl.ds(at.stream, 1), :], (group, group))
    times_col = jnp.sum(jnp.where(lane == row, times_row, 0).astype(F32), axis=1, keepdims=True).astype(jnp.int32)
    time_index = jnp.clip(times_col - times_row, 0, buckets - 1)
    turn = ((lane + row) % group == 0).astype(F32)
    rel_back = mm_exact(jnp.concatenate([small[0, 4:8, :], small[1, 4:8, :]], axis=0), turn)
    bias = s["bias"]
    for head in range(heads):
        hf, head_in = divmod(head, heads_half)
        begin = (head_in % 2) * buckets
        bucket_row = jnp.broadcast_to(small[hf, 8 + head_in // 2 : 9 + head_in // 2, begin : begin + buckets], (group, buckets))
        by_time = [
            jnp.take_along_axis(bucket_row, time_index[:, c : c + buckets], axis=1, mode="promise_in_bounds")
            for c in range(0, group, buckets)
        ]
        bias[head] = skew(jnp.broadcast_to(rel_back[head : head + 1], (group, group))) + jnp.concatenate(by_time, axis=1)

    slots = 2 * count
    ids = []
    for h in range(2):
        for block_at in range(owners * share // 128):
            piece = jnp.zeros((1, 128), jnp.int32)
            for k in range(128 // share):
                turned = pltpu.roll(arrived[block_at * (128 // share) + k, 0:1], (k - h) * share % 128, 1)
                piece = jnp.where(iota((1, 128), 1) // share == k, turned, piece)
            ids.append(piece)
    ids_row = jnp.concatenate(ids, axis=1)
    ids_col = jnp.concatenate([column_of(o, h * share) for h in range(2) for o in range(owners)], axis=0).astype(jnp.int32)
    last = table.shape[0]
    ids_row = jnp.where(ids_row < 0, last, ids_row)
    ids_col = jnp.where(ids_col < 0, last, ids_col)
    keys_row, keys_col = ids_row * slots + iota((1, slots), 1), ids_col * slots + iota((slots, 1), 0)
    order = jnp.sum((keys_col < keys_row).astype(F32), axis=0, keepdims=True).astype(jnp.int32)
    s["turn"][...] = one_hot(order == iota((slots, slots), 0))
    digits = jnp.concatenate([ids_row // 64, ids_row % 64] + [jnp.zeros((1, slots), jnp.int32)] * 6, axis=0)
    found = mm_nt(digits.astype(F32).astype(BF16), s["turn"][...])
    s["sorted_v"][...] = (64.0 * found[0:1] + found[1:2]).astype(jnp.int32)
    limits = iota((slots, 128), 1) * s["limit_rows"]
    s["limits_v"][...] = jnp.sum((ids_col < jnp.minimum(limits, last)).astype(F32), axis=0, keepdims=True).astype(jnp.int32)
    out_copies = [local(14, s["sorted_v"], s["sorted"]), local(15, s["limits_v"], s["limits"])]
    for i in range(owners - 1):
        item.arrive(i)
    slot_hot = one_hot(place == iota((count, count), 0))
    parts[...] = mm_tn(slot_hot, returned[...].reshape(count, width)).astype(BF16).reshape(parts.shape)
    for device, to_ka, to_ha in at.quads:
        emb_c.start(parts.at[2 * to_ka + to_ha], emb.at[at.stream], device)
    emb[at.stream] = parts[at.stream]
    for d in range(1, zs):
        wy.arrive(d - 1)
        there = w.at[ha, at.z_from(d)]
        wc.start(there, there, at.core_peer)
    for d in range(1, zs):
        wy.arrive(zs - 2 + d)
        there = w.at[1 - ha, at.z_from(d)]
        wc.start(there, there, at.core_peer)
    for i in range(2 * zs):
        wc.arrive(i)

    def w_half(hf, cols):
        return w[hf, :, :, cols].reshape(width, cols.stop - cols.start)

    out_cols = slice(4 * half, 5 * half)
    loads["cot"].wait()
    row_c.arrive(1)
    cot = s["cot_v"][...].reshape(group, width)
    grad_mixed = jnp.concatenate([mm(cot, w_half(hf, out_cols)) for hf in range(2)], axis=1)
    loads["gain_in"].wait()
    loads["b_out"].wait()
    loads["ctx"].wait()
    row_c.arrive(0)
    for i in range(3):
        emb_c.arrive(i)

    embedded = jnp.concatenate(
        [emb[0].astype(F32) + emb[1].astype(F32), emb[2].astype(F32) + emb[3].astype(F32)], axis=0
    )
    start = s["ctx_v"][...].reshape(group, width).astype(F32) + embedded
    unit_in, inv_in = layer_norm(start)
    gain_in = s["gain_in_v"][...]
    normed = (unit_in * gain_in).astype(BF16)
    slope, qkv, w_att, sm = s["slope"], s["qkv"], s["w_att"], s["sm"]
    gates = []
    for hf in range(2):
        for g in range(4):
            cols = slice(g * half, (g + 1) * half)
            pre = mm(normed, w_half(hf, cols)) + small[hf, g : g + 1, :]
            sig = sigmoid(pre)
            act = pre * sig
            slope[hf, :, cols] = sig + act * (1.0 - sig)
            if g == 0:
                gates.append(act)
            else:
                qkv[hf, g - 1] = (act * 0.125 if g == 2 else act).astype(BF16)
    gate = jnp.concatenate(gates, axis=1)
    low_half = iota((group, 128), 1) < 64

    def split(tile):
        zero = jnp.zeros_like(tile)
        return jnp.where(low_half, tile, zero), jnp.where(low_half, zero, tile)

    attended = []
    for hf in range(2):
        for pair in range(pairs):
            cols = slice(pair * 128, (pair + 1) * 128)
            values, queries = split(qkv[hf, 0, :, cols]), split(qkv[hf, 1, :, cols])
            keys = qkv[hf, 2, :, cols]
            both = None
            for sub in range(2):
                head = hf * heads_half + pair * 2 + sub
                scores = mm_nt(queries[sub], keys) + bias[head]
                sig = sigmoid(scores)
                act = scores * sig
                weights = (act * maskscale[...]).astype(BF16)
                w_att[head] = weights
                sm[head] = (sig + act * (1.0 - sig)) * maskscale[...]
                part = mm(weights, values[sub])
                both = part if both is None else both + part
            attended.append(both)
    unit_out, inv_out = layer_norm(jnp.concatenate(attended, axis=1))
    gain_out = jnp.concatenate([small[0, 10:11, :], small[1, 10:11, :]], axis=1)
    mixed_in = (unit_out * gain_out * gate).astype(BF16)
    projected = None
    for hf in range(2):
        part = mm_nt(mixed_in[:, hf * half : (hf + 1) * half], w_half(hf, out_cols))
        projected = part if projected is None else projected + part
    mixed, mixed_rows = s["mixed"], s["mixed_v"]
    mixed[...] = (projected + s["b_out_v"][...] + start).astype(BF16)
    mixed_c = copies("mixed")
    for device, to_ka, to_ha in at.quads:
        here = mixed.at[pl.ds(to_ka * tok, tok), pl.ds(pl.multiple_of(to_ha * half, half), half)]
        mixed_c.start(here, mixed_rows.at[at.stream], device)
    own_rows = pl.ds(pl.multiple_of(ka * tok, tok), tok)
    mixed_rows[at.stream] = mixed[own_rows, pl.ds(pl.multiple_of(ha * half, half), half)]

    grad_pre, grad_small = s["grad_pre"], s["grad_small"]
    grad_raw = grad_mixed * unit_out
    grad_gate = grad_raw * gain_out
    grad_gain_out = jnp.sum(grad_raw * gate, axis=0, keepdims=True)
    grad_att = layer_norm_back(grad_mixed * gate * gain_out, unit_out, inv_out).astype(BF16)
    sum_a = WeightSum(at, "zxy", s, "a_")
    sums_b = [WeightSum(at, "yxz", s, f"b{i}_") for i in range(pairs)]

    def put(own, hf, first, value):
        cols = value.shape[1]
        own[hf, :, :, :, first : first + cols] = value.astype(BF16).reshape(own.shape[1:4] + (cols,))

    for hf in range(2):
        cols = slice(hf * half, (hf + 1) * half)
        grad_pre[hf, :, 0:half] = (grad_gate[:, cols] * slope[hf, :, 0:half]).astype(BF16)
        grad_small[hf, 10:11, :] = grad_gain_out[:, cols]
        put(s["a_own"], hf, 0, mm_tn(normed, grad_pre[hf, :, 0:half]))
        put(s["a_own"], hf, half, mm_tn(cot, mixed_in[:, cols]))
    sum_a.cores()

    gs = s["gs"]
    for pair in range(pairs):
        for hf in range(2):
            cols = slice(pair * 128, (pair + 1) * 128)
            values = qkv[hf, 0, :, cols]
            queries, keys = split(qkv[hf, 1, :, cols]), split(qkv[hf, 2, :, cols])
            grads = split(grad_att[:, hf * half + pair * 128 : hf * half + (pair + 1) * 128])
            sums = None
            for sub in range(2):
                head = hf * heads_half + pair * 2 + sub
                grad_scores = (mm_nt(grads[sub], values) * sm[head]).astype(BF16)
                gs[:, head * group : (head + 1) * group] = grad_scores
                found = (
                    mm_tn(w_att[head], grads[sub]),
                    mm(grad_scores, keys[sub]),
                    mm_tn(grad_scores, queries[sub]),
                )
                sums = found if sums is None else [a + b for a, b in zip(sums, found)]
            for g, part in ((1, sums[0]), (2, sums[1] * 0.125), (3, sums[2])):
                there = slice(g * half + pair * 128, g * half + (pair + 1) * 128)
                grad_pre[hf, :, there] = (part * slope[hf, :, there]).astype(BF16)
        if pair == 0:
            sum_a.hop(0)
        if pair < pairs - 1:
            for hf in range(2):
                for g in range(1, 4):
                    there = slice(g * half + pair * 128, g * half + (pair + 1) * 128)
                    put(s[f"b{pair}_own"], hf, (g - 1) * 128, mm_tn(normed, grad_pre[hf, :, there]))
            sums_b[pair].cores()
    grad_normed = None
    for hf in range(2):
        part = mm_nt(grad_pre[hf], w_half(hf, slice(0, 4 * half)))
        grad_normed = part if grad_normed is None else grad_normed + part
    cot32 = cot.astype(F32)
    grad_start, grad_rows = s["grad_start"], s["grad_rows_v"]
    grad_start[...] = (cot32 + layer_norm_back(grad_normed * gain_in, unit_in, inv_in)).astype(BF16)
    back_c = copies("back")
    for device, to_ka, to_ha in at.quads:
        back_c.start(grad_start.at[pl.ds(to_ka * tok, tok)], grad_rows.at[at.stream], device)
    grad_rows[at.stream] = grad_start[own_rows]
    for hf in range(2):
        for g in range(1, 4):
            there = slice(g * half + (pairs - 1) * 128, g * half + pairs * 128)
            put(s[f"b{pairs - 1}_own"], hf, (g - 1) * 128, mm_tn(normed, grad_pre[hf, :, there]))
    sums_b[-1].cores()
    for i in range(pairs - 1):
        sums_b[i].hop(0)
    gain_grad = jnp.sum(grad_normed * unit_in, axis=0, keepdims=True)
    bout_grad = jnp.sum(cot32, axis=0, keepdims=True)
    for hf in range(2):
        sums = jnp.sum(grad_pre[hf].astype(F32), axis=0, keepdims=True)
        for g in range(4):
            grad_small[hf, g : g + 1, :] = sums[:, g * half : (g + 1) * half]
        grad_small[hf, 11:12, :] = gain_grad[:, hf * half : (hf + 1) * half]
        grad_small[hf, 12:13, :] = bout_grad[:, hf * half : (hf + 1) * half]
        grad_small[hf, 13:16, :] = jnp.zeros((3, half), F32)
    flip = (lane + row == group - 1).astype(F32)
    kept_pairs = lane + row <= group - 1
    hot_cols = one_hot(times_row == row)
    hot_back = one_hot(times_row == group - 1 - row)
    folded = mm(jnp.concatenate([flip.astype(BF16), hot_back], axis=0), gs[...])
    rel_rows, time_rows, early_rows = [], [], []
    for head in range(heads):
        places = slice(head * group, (head + 1) * group)
        rel_rows.append(jnp.sum(skew(folded[:group, places]), axis=0, keepdims=True))
        pairs_sum = mm_nt(folded[group:, places].astype(BF16), hot_cols)
        kept = jnp.where(kept_pairs, pairs_sum, 0.0)
        time_rows.append(jnp.sum(skew(kept), axis=0, keepdims=True))
        early_rows.append(jnp.sum(pairs_sum - kept, axis=0, keepdims=True))
    flipped = mm_exact(jnp.concatenate(rel_rows + time_rows, axis=0), flip)
    early = jnp.sum(jnp.concatenate(early_rows, axis=0), axis=1, keepdims=True)
    late = jnp.sum(flipped[heads:, buckets:], axis=1, keepdims=True)
    place_in = iota((heads, buckets), 1)
    time_grad = flipped[heads:, :buckets] + jnp.where(place_in == 0, early, 0.0) + jnp.where(place_in == buckets - 1, late, 0.0)
    for head in range(heads):
        hf, head_in = divmod(head, heads_half)
        begin = (head_in % 2) * buckets
        grad_small[hf, 4 + head_in : 5 + head_in, :] = flipped[head : head + 1]
        grad_small[hf, 8 + head_in // 2 : 9 + head_in // 2, begin : begin + buckets] = time_grad[head : head + 1]
    small_in, small_mine = s["small_in"], s["small_mine"]
    sum_c = copies("sum")
    sum_c.start(grad_small, small_in.at[0], at.core_peer)
    sum_a.hop(1)

    for i in range(3):
        back_c.arrive(i)
    out_copies.append(local(16, grad_rows, s["grad_rows"]))
    outgoing, incoming = s["outgoing"], s["incoming"]
    slot_hot = one_hot(place == iota((count, count), 0))
    outgoing[...] = mm(slot_hot, grad_rows[...].reshape(count, width)).astype(BF16).reshape(outgoing.shape)
    give, hand = copies("give"), copies("hand")
    for d in range(1, owners):
        to = at.owner_to(d)
        give.start(outgoing.at[to], incoming.at[ha, at.me], at.owner(to))
    incoming[ha, at.me] = outgoing[at.me]
    hand.start(incoming.at[ha, at.me], incoming.at[ha, at.me], at.x_peer)

    def take(first, last):
        for d in range(first, last):
            give.arrive(d - 1)
            there = incoming.at[ha, at.owner_from(d)]
            hand.start(there, there, at.x_peer)

    third = owners // 3
    sums_b[-1].hop(0)
    sum_c.arrive(0)
    small_mine[0] = grad_small[...] + small_in[0]
    sum_c.start(small_mine.at[0], small_in.at[1], at.x_peer)
    for i in range(pairs - 1):
        sums_b[i].hop(1)
    sum_a.hop(2)
    take(1, third)
    sums_b[-1].hop(1)
    sum_c.arrive(1)
    small_mine[1] = small_mine[0] + small_in[1]
    sum_c.start(small_mine.at[1], small_in.at[2], at.y_peer)
    for i in range(pairs - 1):
        sums_b[i].hop(2)
    take(third, 2 * third)
    sum_c.arrive(2)
    small_mine[2] = small_mine[1] + small_in[2]
    for d in range(1, zs):
        sum_c.start(small_mine.at[2], small_in.at[2 + d], at.z_device(d))
    sums_b[-1].hop(2)
    take(2 * third, owners)
    ordered = s["ordered"]

    def in_order(h):
        cols = pl.ds(pl.multiple_of(h * count, count), count)
        return mm(s["turn"][:, cols], incoming[h].reshape(count, width))

    ordered[...] = in_order(ha)
    for i in range(3):
        mixed_c.arrive(i)
    out_copies.append(local(17, mixed_rows, s["mixed_rows"]))
    grad_w = s["grad_w_v"]
    grad_w[:, 0:gates_cols] = sum_a.finish()
    for i in range(pairs):
        first = gates_cols + i * 384
        grad_w[:, first : first + 384] = sums_b[i].finish()
    summed = small_mine[2]
    for d in range(1, zs):
        sum_c.arrive(2 + d)
        summed = summed + small_in[2 + d]
    s["small_v"][...] = summed
    out_copies += [local(18, grad_w, s["grad_w"]), local(19, s["small_v"], s["small_sum"])]
    for i in range(owners):
        hand.arrive(i)
    s["rows_v"][...] = (ordered[...] + in_order(1 - ha)).astype(BF16)
    out_copies.append(local(20, s["rows_v"], s["rows"]))
    for copy in out_copies:
        copy.wait()
    for kind in (req, item, emb_c, row_c, small_c, wz, wx, wy, wc, mixed_c, back_c, give, hand, sum_c):
        kind.sent()
    for part in [sum_a] + sums_b:
        part.copies.sent()


def run_main(inputs):
    pbs, kas = lax.axis_size("pb"), lax.axis_size("ka")
    owners, zs = pbs * kas, pbs // 2
    count, width = inputs["context"].shape
    half, tok, share = width // 2, count // MB, count // owners
    group, heads = 2 * tok, width // 64
    shard_rows = inputs["w_uvqk"].shape[0]
    block = shard_rows // 2
    dma = pltpu.SemaphoreType.DMA
    outs = {
        "rows": jax.ShapeDtypeStruct((2 * count, width), BF16),
        "sorted": jax.ShapeDtypeStruct((1, 2 * count), jnp.int32),
        "limits": jax.ShapeDtypeStruct((1, 128), jnp.int32),
        "grad_rows": jax.ShapeDtypeStruct((MB, tok, width), BF16),
        "mixed_rows": jax.ShapeDtypeStruct((MB, tok, half), BF16),
        "grad_w": jax.ShapeDtypeStruct((block, 5 * half), F32),
        "small_sum": jax.ShapeDtypeStruct((2, 16, half), F32),
    }
    scratch = {
        "ctx_v": pltpu.VMEM((2, tok, width), BF16),
        "cot_v": pltpu.VMEM((2, tok, width), BF16),
        "requests": pltpu.VMEM((owners, 8, 128), jnp.int32),
        "arrived": pltpu.VMEM((owners, 8, 128), jnp.int32),
        "table_buf": pltpu.VMEM(inputs["table"].shape, BF16),
        "total": pltpu.VMEM((count // 2, width), F32),
        "fetched": pltpu.VMEM((2, owners // 2, share, width), BF16),
        "returned": pltpu.VMEM((owners, share, width), BF16),
        "parts": pltpu.VMEM((MB, tok, width), BF16),
        "emb": pltpu.VMEM((MB, tok, width), BF16),
        "shard": pltpu.VMEM((shard_rows, 5 * half), BF16),
        "w": pltpu.VMEM((2, pbs, shard_rows, 5 * half), BF16),
        "small": pltpu.VMEM((2, 16, half), F32),
        "maskscale": pltpu.VMEM((group, group), F32),
        "bias": pltpu.VMEM((heads, group, group), F32),
        "slope": pltpu.VMEM((2, group, 4 * half), F32),
        "qkv": pltpu.VMEM((2, 3, group, half), BF16),
        "w_att": pltpu.VMEM((heads, group, group), BF16),
        "sm": pltpu.VMEM((heads, group, group), F32),
        "gs": pltpu.VMEM((group, heads * group), BF16),
        "grad_pre": pltpu.VMEM((2, group, 4 * half), BF16),
        "mixed": pltpu.VMEM((group, width), BF16),
        "grad_start": pltpu.VMEM((group, width), BF16),
        "grad_small": pltpu.VMEM((2, 16, half), F32),
        "outgoing": pltpu.VMEM((owners, share, width), BF16),
        "small_mine": pltpu.VMEM((3, 2, 16, half), F32),
        "small_in": pltpu.VMEM((2 + zs, 2, 16, half), F32),
        "incoming": pltpu.VMEM((2, owners, share, width), BF16),
        "rows_v": pltpu.VMEM((2 * count, width), BF16),
        "ordered": pltpu.VMEM((2 * count, width), F32),
        "turn": pltpu.VMEM((2 * count, 2 * count), BF16),
        "sorted_v": pltpu.VMEM((1, 2 * count), jnp.int32),
        "limits_v": pltpu.VMEM((1, 128), jnp.int32),
        "grad_rows_v": pltpu.VMEM((MB, tok, width), BF16),
        "mixed_v": pltpu.VMEM((MB, tok, half), BF16),
        "grad_w_v": pltpu.VMEM((block, 5 * half), F32),
        "small_v": pltpu.VMEM((2, 16, half), F32),
        "load_sem": dma((21,)),
        "table_sem": dma((8,)),
    }
    for name in ("owner", "offset", "w_uvqk", "w_out", "b", "rel", "time", "gain_out", "gain_in", "b_out", "lengths", "times"):
        scratch[name + "_v"] = pltpu.VMEM(inputs[name].shape, inputs[name].dtype)
    for name, number in (
        ("req", owners - 1), ("item", owners - 1), ("emb", 3), ("row", 2), ("small", 1), ("wz", zs - 1), ("wx", zs),
        ("wy", 2 * zs - 2), ("wc", 2 * zs), ("mixed", 3), ("back", 3), ("give", owners - 1), ("hand", owners), ("sum", 2 + zs),
    ):
        scratch[name + "_send"] = dma((number,))
        scratch[name + "_recv"] = dma((number,))
    scratch |= weight_sum_scratch("a_", "zxy", zs, block, 2 * half)
    for i in range(half // 128):
        scratch |= weight_sum_scratch(f"b{i}_", "yxz", zs, block, 384)
    hbm = pl.BlockSpec(memory_space=pltpu.HBM)
    found = pl.pallas_call(
        functools.partial(main_kernel, tuple(inputs), tuple(outs), tuple(scratch)),
        out_shape=tuple(outs.values()),
        in_specs=[hbm] * len(inputs),
        out_specs=(hbm,) * len(outs),
        scratch_shapes=list(scratch.values()),
        compiler_params=pltpu.CompilerParams(
            collective_id=1, has_side_effects=True, vmem_limit_bytes=58 * 1024 * 1024
        ),
    )(*inputs.values())
    return dict(zip(outs, found, strict=True))


def scatter_kernel(
    limits_in, sorted_in, rows_in, grad_w_in, small_in, mixed_in, grad_rows_in,
    out_ref, w_ref, w_out_ref, b_ref, rel_ref, time_ref, gain_in_ref, gain_out_ref, b_out_ref, mixed_out, grad_rows_out,
    limits, ids, rows, grad_w_ref, small_ref, mixed, grad_rows, tiles, load_sem, tile_sem, pass_sem,
):
    pairs_in = [
        (limits_in, limits), (sorted_in, ids), (rows_in, rows), (grad_w_in, grad_w_ref), (small_in, small_ref),
        (mixed_in, mixed), (grad_rows_in, grad_rows),
    ]
    loads = [pltpu.make_async_copy(src, dst, load_sem.at[i]) for i, (src, dst) in enumerate(pairs_in)]
    for load in loads:
        load.start()
    for load in loads[:3]:
        load.wait()
    slots, tile = tiles.shape[0], tiles.shape[1]
    count = out_ref.shape[0] // tile
    per_tile = tile // 256
    depth = 256

    def write(i, slot):
        there = pl.ds(pl.multiple_of(i * tile, tile), tile)
        return pltpu.make_async_copy(tiles.at[slot], out_ref.at[there], tile_sem.at[slot])

    def step(i, carry):
        slot = lax.rem(i, slots)

        @pl.when(i >= slots)
        def _():
            write(i - slots, slot).wait()

        first = limits[0, i * per_tile] // depth
        end = (limits[0, (i + 1) * per_tile] + depth - 1) // depth

        def product(j):
            here = pl.ds(pl.multiple_of(j * depth, depth), depth)
            return mm(one_hot(ids[:, here] == iota((tile, depth), 0) + i * tile), rows[here, :])

        tiles[slot] = product(jnp.minimum(first, rows.shape[0] // depth - 1))

        def more(j, carry):
            tiles[slot] += product(j)
            return carry

        lax.fori_loop(first + 1, end, more, 0)
        write(i, slot).start()
        return carry

    lax.fori_loop(0, 2, step, 0)
    for load in loads[3:]:
        load.wait()
    passed = [
        pltpu.make_async_copy(mixed, mixed_out, pass_sem.at[0]),
        pltpu.make_async_copy(grad_rows, grad_rows_out, pass_sem.at[1]),
    ]
    for copy in passed:
        copy.start()
    lax.fori_loop(2, count, step, 0)
    half = w_ref.shape[2]
    buckets = time_ref.shape[1]
    w_ref[:, 0, :] = grad_w_ref[:, 0:half]
    w_out_ref[...] = grad_w_ref[:, half : 2 * half]
    for pair in range(half // 128):
        for g in range(1, 4):
            first = 2 * half + pair * 384 + (g - 1) * 128
            w_ref[:, g, pair * 128 : (pair + 1) * 128] = grad_w_ref[:, first : first + 128]
    ha = lax.axis_index("ha")
    b_ref[...] = small_ref[ha, 0:4, :]
    rel_ref[...] = small_ref[ha, 4:8, :]
    for i in range(2):
        for j in range(2):
            time_ref[2 * i + j : 2 * i + j + 1, :] = small_ref[ha, 8 + i : 9 + i, j * buckets : (j + 1) * buckets]
    gain_out_ref[...] = small_ref[ha, 10:11, :]
    for hf in range(2):
        gain_in_ref[:, hf * half : (hf + 1) * half] = small_ref[hf, 11:12, :]
        b_out_ref[:, hf * half : (hf + 1) * half] = small_ref[hf, 12:13, :]
    for k in range(slots):
        write(count - slots + k, (count - slots + k) % slots).wait()
    for copy in passed:
        copy.wait()


def scatter_rows(found, table_rows, buckets, tile=512, slots=4):
    rows, grad_w = found["rows"], found["grad_w"]
    width = rows.shape[1]
    half, block = width // 2, grad_w.shape[0]
    names = ("limits", "sorted", "rows", "grad_w", "small_sum", "mixed_rows", "grad_rows")
    shapes = [(block, 4, half), (block, half), (4, half), (4, half), (4, buckets), (1, width), (1, half), (1, width)]
    hbm, vmem = pl.BlockSpec(memory_space=pltpu.HBM), pl.BlockSpec(memory_space=pltpu.VMEM)
    outs = [jax.ShapeDtypeStruct(shape, F32) for shape in [(table_rows, width)] + shapes]
    outs += [jax.ShapeDtypeStruct(found[name].shape, BF16) for name in ("mixed_rows", "grad_rows")]
    return pl.pallas_call(
        scatter_kernel,
        out_shape=outs,
        in_specs=[hbm] * len(names),
        out_specs=[hbm] + [vmem] * len(shapes) + [hbm] * 2,
        scratch_shapes=[
            pltpu.SMEM(found["limits"].shape, jnp.int32),
            pltpu.VMEM(found["sorted"].shape, jnp.int32),
            pltpu.VMEM(rows.shape, BF16),
            pltpu.VMEM(grad_w.shape, F32),
            pltpu.VMEM(found["small_sum"].shape, F32),
            pltpu.VMEM(found["mixed_rows"].shape, BF16),
            pltpu.VMEM(found["grad_rows"].shape, BF16),
            pltpu.VMEM((slots, tile, width), F32),
            pltpu.SemaphoreType.DMA((len(names),)),
            pltpu.SemaphoreType.DMA((slots,)),
            pltpu.SemaphoreType.DMA((2,)),
        ],
        compiler_params=pltpu.CompilerParams(vmem_limit_bytes=58 * 1024 * 1024),
    )(*(found[name] for name in names))


def local_streams(
    context,
    item_owner,
    item_offset,
    lengths,
    times,
    table,
    cotangent,
    ln_in_gain,
    w_uvqk,
    b_uvqk,
    rel_bias,
    time_bias,
    ln_out_gain,
    w_out,
    b_out,
):
    row_count, width = context.shape
    half = width // 2
    found = run_main(
        {
            "owner": item_owner.reshape(1, row_count),
            "offset": item_offset.reshape(1, row_count),
            "context": context,
            "cot": cotangent,
            "table": table,
            "w_uvqk": w_uvqk,
            "w_out": w_out.T,
            "b": b_uvqk,
            "rel": rel_bias,
            "time": time_bias,
            "gain_out": ln_out_gain.reshape(1, half),
            "gain_in": ln_in_gain.reshape(1, width),
            "b_out": b_out.reshape(1, width),
            "lengths": lengths[0],
            "times": times[0],
        }
    )
    (
        table_grad, grad_w, grad_w_out, grad_b, grad_rel, grad_time, grad_gain_in, grad_gain_out, grad_b_out, mixed, grad_rows,
    ) = scatter_rows(found, table.shape[0], time_bias.shape[1])
    return (
        mixed.reshape(row_count, half),
        grad_rows.reshape(row_count, width),
        table_grad,
        grad_gain_in.reshape(width),
        grad_w,
        grad_b,
        grad_rel,
        grad_time,
        grad_gain_out.reshape(half),
        grad_w_out.T,
        grad_b_out.reshape(width),
    )


def solution(mesh):
    one_stream = mesh.shape["ka"] * mesh.shape["ha"] == MB and mesh.shape["ka"] == 2
    return jax.shard_map(
        local_streams if one_stream else local_general,
        mesh=mesh,
        in_specs=(
            P(("pb", "ka"), None),
            P(("pb", "ka"), None),
            P(("pb", "ka")),
            P("pb", None, None),
            P("pb", None, None),
            P(("pb", "ka"), None),
            P(("pb", "ka"), None),
            P(),
            P("pb", None, "ha"),
            P(None, "ha"),
            P("ha", None),
            P("ha", None),
            P("ha"),
            P("ha", "pb"),
            P(),
        ),
        out_specs=(
            P(("pb", "ka"), "ha"),
            P(("pb", "ka"), None),
            P(("pb", "ka"), None),
            P(),
            P(("pb", "ka"), None, "ha"),
            P(None, "ha"),
            P("ha", None),
            P("ha", None),
            P("ha"),
            P("ha", ("pb", "ka")),
            P(),
        ),
        check_vma=False,
    )
```

```python
import functools

import jax
import jax.numpy as jnp
from jax import lax
from jax.experimental import pallas as pl
from jax.experimental.pallas import tpu as pltpu
from jax.sharding import PartitionSpec as P

DH = 64
TOK_DEV = 128
MB = 4
SEQ_GRP = 4
F32 = jnp.float32
BF16 = jnp.bfloat16


epsilon = 1e-05


def silu_slope(values):
    sigma = jax.nn.sigmoid(values)
    return sigma * (1.0 + values * (1.0 - sigma))


def norm_rows(values, gain):
    centered = values - jnp.mean(values, axis=-1, keepdims=True)
    inverse = lax.rsqrt(jnp.mean(centered * centered, axis=-1, keepdims=True) + epsilon)
    unit_rows = centered * inverse
    return (unit_rows * gain, unit_rows, inverse)


def norm_back(grad_unit, unit_rows, inverse):
    first_mean = jnp.mean(grad_unit, axis=-1, keepdims=True)
    second_mean = jnp.mean(grad_unit * unit_rows, axis=-1, keepdims=True)
    return inverse * (grad_unit - first_mean - unit_rows * second_mean)


def stream_layout(lengths_row, group):
    places = jnp.arange(group, dtype=jnp.int32)
    ends = jnp.cumsum(lengths_row, dtype=jnp.int32)
    member = jnp.sum((ends[None, :] <= places[:, None]).astype(jnp.int32), axis=1)
    onehot = (member[:, None] == jnp.arange(SEQ_GRP, dtype=jnp.int32)[None, :]).astype(jnp.float32)
    counted = jnp.maximum(jnp.sum(onehot * lengths_row.astype(jnp.float32)[None, :], axis=1), 1.0)
    return (places, member, counted)


def diagonal_bias(rel_bias, query_first, key_first, query_len, key_len):
    heads, group = rel_bias.shape
    span = query_len + key_len - 1
    padded = jnp.concatenate([jnp.zeros((heads, group), jnp.float32), rel_bias], axis=1)
    window = lax.dynamic_slice_in_dim(
        padded, query_first - key_first - key_len + 1 + group, span, 1
    )
    flipped = jnp.concatenate([window[:, ::-1], jnp.zeros((heads, 1), jnp.float32)], axis=1)
    skewed = jnp.tile(flipped, (1, query_len))[:, : query_len * span].reshape(
        heads, query_len, span
    )
    return skewed[:, :, query_len - 1 : query_len - 1 + key_len]


def diagonal_sums(grad_scores, query_first, key_first, group):
    heads, query_len, key_len = grad_scores.shape
    span = query_len + key_len - 1
    widened = jnp.pad(grad_scores.astype(jnp.float32), ((0, 0), (0, 0), (query_len - 1, 0)))
    flat = jnp.pad(widened.reshape(heads, query_len * span), ((0, 0), (0, query_len)))
    totals = jnp.sum(flat.reshape(heads, query_len, span + 1), axis=1)
    window = totals[:, :span][:, ::-1]
    placed = lax.dynamic_update_slice_in_dim(
        jnp.zeros((heads, 2 * group), jnp.float32),
        window,
        query_first - key_first - key_len + 1 + group,
        1,
    )
    return placed[:, group:]


def bucket_lookup(time_bias, bucket_hot):
    high = time_bias.astype(jnp.bfloat16)
    rest = time_bias - high.astype(jnp.float32)
    middle = rest.astype(jnp.bfloat16)
    lowest = (rest - middle.astype(jnp.float32)).astype(jnp.bfloat16)
    pieces = jnp.einsum(
        "phb,qkb->phqk",
        jnp.stack([high, middle, lowest]),
        bucket_hot,
        preferred_element_type=jnp.float32,
    )
    return pieces[0] + pieces[1] + pieces[2]


def tile_scores(query_heads, key_heads, query_info, key_info, rel_bias, time_bias):
    query_pos, query_member, query_count, query_stamp = query_info
    key_pos, key_member, key_stamp = key_info
    distance = query_pos[:, None] - key_pos[None, :]
    time_index = jnp.clip(query_stamp[:, None] - key_stamp[None, :], 0, time_bias.shape[1] - 1)
    bucket_hot = (
        time_index[:, :, None] == jnp.arange(time_bias.shape[1], dtype=jnp.int32)[None, None, :]
    ).astype(jnp.bfloat16)
    scores = jnp.einsum(
        "qhd,khd->hqk", query_heads, key_heads, preferred_element_type=jnp.float32
    ) * DH ** (-0.5)
    scores = (
        scores
        + diagonal_bias(rel_bias, query_pos[0], key_pos[0], query_pos.shape[0], key_pos.shape[0])
        + bucket_lookup(time_bias, bucket_hot)
    )
    allowed = (
        (query_member[:, None] == key_member[None, :])
        & (query_member[:, None] < SEQ_GRP)
        & (distance >= 0)
    )[None]
    weights = (jnp.where(allowed, jax.nn.silu(scores), 0.0) / query_count[None, :, None]).astype(
        jnp.bfloat16
    )
    return (scores, allowed, weights, bucket_hot)


def score_grads(grad_weights, scores, allowed, query_count):
    return (
        jnp.where(allowed, grad_weights / query_count[None, :, None], 0.0) * silu_slope(scores)
    ).astype(jnp.bfloat16)


def local_general(
    context,
    item_owner,
    item_offset,
    lengths,
    times,
    table,
    cotangent,
    ln_in_gain,
    w_uvqk,
    b_uvqk,
    rel_bias,
    time_bias,
    ln_out_gain,
    w_out,
    b_out,
):
    owners = lax.axis_size(("pb", "ka"))
    row_count = context.shape[0]
    width = context.shape[1]
    capacity = max(2, 2 * row_count // owners)
    owner_ids = item_owner[:, 0]
    owner_hits = (owner_ids[:, None] == jnp.arange(owners, dtype=jnp.int32)[None, :]).astype(
        jnp.int32
    )
    earlier = jnp.sum((jnp.cumsum(owner_hits, axis=0) - owner_hits) * owner_hits, axis=1)
    slot_index = owner_ids * capacity + earlier
    requests = jnp.zeros((owners * capacity,), jnp.int32).at[slot_index].set(item_offset + 1)
    arrived = lax.all_to_all(
        requests.reshape(owners, capacity), ("pb", "ka"), split_axis=0, concat_axis=0, tiled=True
    ).reshape(-1)
    present = arrived > 0
    local_rows = jnp.maximum(arrived - 1, 0)
    fetched = jnp.where(present[:, None], table[local_rows], jnp.zeros((), jnp.bfloat16))
    returned = lax.all_to_all(
        fetched.reshape(owners, capacity, width),
        ("pb", "ka"),
        split_axis=0,
        concat_axis=0,
        tiled=True,
    )
    embedded = returned.reshape(owners * capacity, width)[slot_index]
    start = context.astype(jnp.float32) + embedded.astype(jnp.float32)
    group = lax.axis_size("ka") * TOK_DEV
    block_start = lax.axis_index("ka") * TOK_DEV
    half_cols = w_out.shape[0]
    heads = half_cols // DH
    full_cols = half_cols * lax.axis_size("ha")
    out_cols = width // lax.axis_size("ha")
    out_start = lax.axis_index("ha") * out_cols
    bias_half = lax.dynamic_slice_in_dim(b_out, out_start, out_cols)
    scale = DH ** (-0.5)
    grad_gain_in = jnp.zeros(ln_in_gain.shape, jnp.float32)
    grad_bias_proj = jnp.zeros(b_uvqk.shape, jnp.float32)
    grad_rel = jnp.zeros(rel_bias.shape, jnp.float32)
    grad_time = jnp.zeros(time_bias.shape, jnp.float32)
    grad_gain_out = jnp.zeros(ln_out_gain.shape, jnp.float32)
    grad_bias_out = jnp.zeros(b_out.shape, jnp.float32)
    weight_total = None
    mixed_parts = []
    grad_parts = []
    for micro in range(MB):
        w_full, w_final = (
            lax.all_gather(w_uvqk, "pb", axis=0, tiled=True),
            lax.all_gather(w_out, "pb", axis=1, tiled=True),
        )
        x_in = start[micro * TOK_DEV : (micro + 1) * TOK_DEV]
        cot_rows = cotangent[micro * TOK_DEV : (micro + 1) * TOK_DEV]
        stamps = times[0, micro]
        places, member, counted = stream_layout(lengths[0, micro], group)
        query_pos = lax.dynamic_slice_in_dim(places, block_start, TOK_DEV)
        query_member = lax.dynamic_slice_in_dim(member, block_start, TOK_DEV)
        query_count = lax.dynamic_slice_in_dim(counted, block_start, TOK_DEV)
        query_stamp = lax.dynamic_slice_in_dim(stamps, block_start, TOK_DEV)
        normed_float, unit_in, inverse_in = norm_rows(x_in, ln_in_gain)
        normed = normed_float.astype(jnp.bfloat16)
        pre_act = (
            jnp.einsum("td,dgc->tgc", normed, w_full, preferred_element_type=jnp.float32) + b_uvqk
        )
        activated = jax.nn.silu(pre_act)
        gate_part = activated[:, 0]
        values = activated[:, 1].astype(jnp.bfloat16)
        queries = activated[:, 2].astype(jnp.bfloat16)
        key_rows = activated[:, 3].astype(jnp.bfloat16)
        key_pair = lax.all_gather(jnp.stack([key_rows, values]), "ka", axis=1, tiled=True)
        all_keys = key_pair[0].reshape(group, heads, DH)
        all_values = key_pair[1].reshape(group, heads, DH)
        query_heads = queries.reshape(TOK_DEV, heads, DH)
        scores, allowed, weights, bucket_hot = tile_scores(
            query_heads,
            all_keys,
            (query_pos, query_member, query_count, query_stamp),
            (places, member, stamps),
            rel_bias,
            time_bias,
        )
        attended = jnp.einsum(
            "hqk,khd->qhd", weights, all_values, preferred_element_type=jnp.float32
        ).reshape(TOK_DEV, half_cols)
        row_total, row_square = lax.psum(
            (jnp.sum(attended, axis=1), jnp.sum(attended * attended, axis=1)), "ha"
        )
        row_mean = row_total / full_cols
        inverse_out = lax.rsqrt(row_square / full_cols - row_mean * row_mean + epsilon)[:, None]
        unit_out = (attended - row_mean[:, None]) * inverse_out
        mixed_in = (unit_out * ln_out_gain * gate_part).astype(jnp.bfloat16)
        partial_out = jnp.dot(mixed_in, w_final, preferred_element_type=jnp.float32)
        summed_out = lax.psum_scatter(partial_out, "ha", scatter_dimension=1, tiled=True)
        residual = lax.dynamic_slice_in_dim(x_in, out_start, out_cols, 1)
        mixed_parts.append((summed_out + bias_half + residual).astype(jnp.bfloat16))
        grad_final_part = jnp.einsum(
            "tc,td->cd", mixed_in, cot_rows, preferred_element_type=jnp.float32
        )
        grad_bias_out = grad_bias_out + jnp.sum(cot_rows.astype(jnp.float32), axis=0)
        grad_mixed = jnp.einsum("td,cd->tc", cot_rows, w_final, preferred_element_type=jnp.float32)
        grad_gate = grad_mixed * unit_out * ln_out_gain
        grad_gain_out = grad_gain_out + jnp.sum(grad_mixed * unit_out * gate_part, axis=0)
        grad_unit = grad_mixed * gate_part * ln_out_gain
        first_total, second_total = lax.psum(
            (jnp.sum(grad_unit, axis=1), jnp.sum(grad_unit * unit_out, axis=1)), "ha"
        )
        grad_attended = (
            inverse_out
            * (
                grad_unit
                - first_total[:, None] / full_cols
                - unit_out * second_total[:, None] / full_cols
            )
        ).astype(jnp.bfloat16)
        grad_heads = grad_attended.reshape(TOK_DEV, heads, DH)
        grad_weights = jnp.einsum(
            "qhd,khd->hqk", grad_heads, all_values, preferred_element_type=jnp.float32
        )
        grad_scores = score_grads(grad_weights, scores, allowed, query_count)
        grad_rel = grad_rel + diagonal_sums(grad_scores, query_pos[0], places[0], rel_bias.shape[1])
        grad_time = grad_time + jnp.einsum(
            "hqk,qkb->hb", grad_scores, bucket_hot, preferred_element_type=jnp.float32
        )
        grad_queries = (
            jnp.einsum("hqk,khd->qhd", grad_scores, all_keys, preferred_element_type=jnp.float32)
            * scale
        ).reshape(TOK_DEV, half_cols)
        key_part = (
            jnp.einsum("hqk,qhd->khd", grad_scores, query_heads, preferred_element_type=jnp.float32)
            * scale
        )
        value_part = jnp.einsum(
            "hqk,qhd->khd", weights, grad_heads, preferred_element_type=jnp.float32
        )
        stacked = jnp.stack(
            [key_part.reshape(group, half_cols), value_part.reshape(group, half_cols)]
        )
        owned_grads = lax.psum_scatter(stacked, "ka", scatter_dimension=1, tiled=True)
        grad_keys = owned_grads[0]
        grad_values = owned_grads[1]
        grad_act = jnp.stack([grad_gate, grad_values, grad_queries, grad_keys], axis=1)
        grad_pre = (grad_act * silu_slope(pre_act)).astype(jnp.bfloat16)
        grad_proj_part = jnp.einsum(
            "td,tgc->dgc", normed, grad_pre, preferred_element_type=jnp.float32
        )
        grad_bias_proj = grad_bias_proj + jnp.sum(grad_pre.astype(jnp.float32), axis=0)
        grad_normed = lax.psum(
            jnp.einsum("tgc,dgc->td", grad_pre, w_full, preferred_element_type=jnp.float32), "ha"
        )
        grad_gain_in = grad_gain_in + jnp.sum(grad_normed * unit_in, axis=0)
        grad_parts.append(
            cot_rows.astype(jnp.float32) + norm_back(grad_normed * ln_in_gain, unit_in, inverse_in)
        )
        local_pair = (grad_proj_part, grad_final_part)
        local_pair = (
            lax.psum_scatter(local_pair[0], ("pb", "ka"), scatter_dimension=0, tiled=True),
            lax.psum_scatter(local_pair[1], ("pb", "ka"), scatter_dimension=1, tiled=True),
        )
        weight_total = (
            local_pair if weight_total is None else jax.tree.map(jnp.add, weight_total, local_pair)
        )
    grad_start = jnp.concatenate(grad_parts, axis=0)
    outgoing = jnp.zeros((owners * capacity, width), jnp.float32).at[slot_index].set(grad_start)
    incoming = lax.all_to_all(
        outgoing.reshape(owners, capacity, width),
        ("pb", "ka"),
        split_axis=0,
        concat_axis=0,
        tiled=True,
    ).reshape(owners * capacity, width)
    table_grad = jax.ops.segment_sum(
        jnp.where(present[:, None], incoming, 0.0), local_rows, num_segments=table.shape[0]
    )
    small_total = lax.psum(
        (grad_gain_in, grad_bias_proj, grad_rel, grad_time, grad_gain_out, grad_bias_out),
        ("pb", "ka"),
    )
    mixed = jnp.concatenate(mixed_parts, axis=0)
    return (
        mixed,
        grad_start.astype(jnp.bfloat16),
        table_grad,
        small_total[0],
        weight_total[0],
        small_total[1],
        small_total[2],
        small_total[3],
        small_total[4],
        weight_total[1],
        small_total[5],
    )


MESH = pl.DeviceIdType.MESH


def remote(src, dst, send_sem, recv_sem, device):
    return pltpu.make_async_remote_copy(
        src_ref=src, dst_ref=dst, send_sem=send_sem, recv_sem=recv_sem, device_id=device, device_id_type=MESH
    )


def mm(a, b):
    return jnp.dot(a, b, preferred_element_type=F32)


def mm_nt(a, b):
    return lax.dot_general(a, b, (((1,), (1,)), ((), ())), preferred_element_type=F32)


def mm_tn(a, b):
    return lax.dot_general(a, b, (((0,), (0,)), ((), ())), preferred_element_type=F32)


def mm_exact(a, b):
    return jnp.dot(a, b, preferred_element_type=F32, precision=lax.Precision.HIGHEST)


def sigmoid(v):
    return 0.5 * jnp.tanh(0.5 * v) + 0.5


def skew(tile):
    return pltpu.roll(tile, 0, 1, stride=1, stride_axis=0)


def iota(shape, dim):
    return lax.broadcasted_iota(jnp.int32, shape, dim)


def one_hot(equal):
    return equal.astype(F32).astype(BF16)


def layer_norm(values):
    centered = values - jnp.mean(values, axis=1, keepdims=True)
    inverse = lax.rsqrt(jnp.mean(centered * centered, axis=1, keepdims=True) + epsilon)
    return centered * inverse, inverse


def layer_norm_back(grad_unit, unit, inverse):
    first = jnp.mean(grad_unit, axis=1, keepdims=True)
    second = jnp.mean(grad_unit * unit, axis=1, keepdims=True)
    return inverse * (grad_unit - first - unit * second)


class Place:
    def __init__(self):
        self.pbs, self.kas = lax.axis_size("pb"), lax.axis_size("ka")
        self.owners, self.zs = self.pbs * self.kas, self.pbs // 2
        self.pb, self.ka, self.ha = lax.axis_index("pb"), lax.axis_index("ka"), lax.axis_index("ha")
        self.z, self.core = self.pb // 2, self.pb % 2
        self.me = self.pb * self.kas + self.ka
        self.stream = 2 * self.ka + self.ha
        self.x_peer = (self.pb, self.ka, 1 - self.ha)
        self.y_peer = (self.pb, 1 - self.ka, self.ha)
        self.xy_peer = (self.pb, 1 - self.ka, 1 - self.ha)
        self.core_peer = (2 * self.z + 1 - self.core, self.ka, self.ha)
        self.quads = [
            (self.xy_peer, 1 - self.ka, 1 - self.ha),
            (self.x_peer, self.ka, 1 - self.ha),
            (self.y_peer, 1 - self.ka, self.ha),
        ]

    def partner(self, k):
        dz, dc, dk = k // 4, k // 2 % 2, k % 2
        z = [self.z, self.z + 1 - 2 * (self.z % 2), (self.z + 2) % 4, 3 - self.z][dz]
        core = 1 - self.core if dc else self.core
        ka = 1 - self.ka if dk else self.ka
        return (2 * z + core) * 2 + ka, (2 * z + core, ka, self.ha)

    def owner_to(self, d):
        index = lax.rem(self.me + d, self.owners)
        return index, (index // self.kas, index % self.kas, self.ha)

    def z_to(self, d):
        return lax.rem(self.z + d, self.zs)

    def z_device(self, d):
        return (2 * self.z_to(d) + self.core, self.ka, self.ha)

    def z_from(self, d):
        return 2 * lax.rem(self.z - d + self.zs, self.zs) + self.core


class Copies:
    def __init__(self, send, recv):
        self.send, self.recv, self.copies = send, recv, []

    def start(self, src, dst, device):
        i = len(self.copies)
        copy = remote(src, dst, self.send.at[i], self.recv.at[i], device)
        copy.start()
        self.copies.append(copy)

    def arrive(self, i):
        self.copies[i].wait_recv()

    def sent(self):
        for copy in self.copies:
            copy.wait_send()


class WeightSum:
    def __init__(self, at, order, s, name):
        self.at, self.order = at, order
        self.own, self.core_in = s[name + "own"], s[name + "core_in"]
        self.mine = [s[f"{name}mine{i}"] for i in range(len(order))]
        self.other = [s[f"{name}other{i}"] for i in range(len(order))]
        self.copies = Copies(s[name + "send"], s[name + "recv"])
        self.begun = [0]

    def pick(self, ref, step, index):
        done = "".join(self.order[: self.order.index(step)])
        left = [a for a in "xzy" if a not in done]
        at_axis = dict(zip(step, index))
        return ref.at[tuple(at_axis.get(a, slice(None)) for a in left)]

    def peers(self, step):
        at = self.at
        if step == "z":
            return [(at.z_device(d), (at.z_to(d),)) for d in range(1, at.zs)]
        if step == "x":
            return [(at.x_peer, (1 - at.ha,))]
        if step == "y":
            return [(at.y_peer, (1 - at.ka,))]
        return [(device, (to_ha, to_ka)) for device, to_ka, to_ha in at.quads]

    def own_index(self, step):
        return tuple({"x": self.at.ha, "y": self.at.ka, "z": self.at.z}[axis] for axis in step)

    def cores(self):
        self.copies.start(self.own.at[:, :, 1 - self.at.core], self.core_in, self.at.core_peer)

    def send(self, i):
        step = self.order[i]
        self.begun.append(len(self.copies.copies))
        for k, (device, index) in enumerate(self.peers(step)):
            self.copies.start(self.pick(self.mine[i], step, index), self.other[i].at[k], device)

    def received(self, i):
        step = self.order[i]
        total = self.pick(self.mine[i], step, self.own_index(step))[...].astype(F32)
        for k in range(len(self.peers(step))):
            self.copies.arrive(self.begun[i + 1] + k)
            total = total + self.other[i][k].astype(F32)
        return total

    def hop(self):
        i = len(self.begun) - 1
        if i == 0:
            self.copies.arrive(0)
            for h in range(2):
                total = self.own[h, :, self.at.core].astype(F32) + self.core_in[h].astype(F32)
                self.mine[0][h] = total.astype(BF16).reshape(self.mine[0].shape[1:])
        else:
            self.mine[i][...] = self.received(i - 1).astype(BF16)
        self.send(i)

    def finish(self):
        return self.received(len(self.order) - 1)


def weight_sum_scratch(name, order, zs, block, cols):
    dma = pltpu.SemaphoreType.DMA
    sizes = {"x": 2, "z": zs, "y": 2}
    found = {
        name + "own": pltpu.VMEM((2, zs, 2, 2 * block, cols), BF16),
        name + "core_in": pltpu.VMEM((2, zs, 2 * block, cols), BF16),
    }
    for i, step in enumerate(order):
        before = [sizes[a] for a in "xzy" if a not in "".join(order[:i])]
        after = [sizes[a] for a in "xzy" if a not in "".join(order[: i + 1])]
        found[f"{name}mine{i}"] = pltpu.VMEM((*before, block, cols), BF16)
        found[f"{name}other{i}"] = pltpu.VMEM(({"xy": 3, "z": zs - 1}.get(step, 1), *after, block, cols), BF16)
    found[name + "send"] = dma((1 + 3 + zs,))
    found[name + "recv"] = dma((1 + 3 + zs,))
    return found


ORDERS = {"a_": ("z", "xy"), "b0_": ("xy", "z"), "b1_": ("xy", "z")}
STEPS = {
    "pair 0": ("a_",),
    "rows sent": (),
    "tables": (),
    "given": ("b0_", "b1_", "a_"),
    "take 1": (),
    "take 2": ("b0_",),
    "take 3": (),
    "take 4": ("b1_",),
    "take 5": (),
}


def main_kernel(in_names, out_names, scratch_names, *refs):
    names = in_names + out_names + scratch_names
    s = dict(zip(names, refs, strict=True))
    s["limit_rows"] = 256
    at = Place()
    owners, zs, ka, ha = at.owners, at.zs, at.ka, at.ha
    count, width = s["context"].shape
    half = width // 2
    tok = count // MB
    group = 2 * tok
    capacity = 2 * count // owners
    block = s["w_uvqk"].shape[0] // 2
    heads_half = half // 64
    heads = 2 * heads_half
    pairs = half // 128
    buckets = s["time"].shape[1]
    gates_cols = 2 * half

    table, table_buf, table_sem = s["table"], s["table_buf"], s["table_sem"]
    chunks = table_sem.shape[0]
    chunk = table.shape[0] // chunks

    def local(i, src, dst):
        copy = pltpu.make_async_copy(src, dst, s["load_sem"].at[i])
        copy.start()
        return copy

    mine = pl.ds(pl.multiple_of(at.stream * tok, tok), tok)
    away = pl.ds(pl.multiple_of((2 * (1 - ka) + ha) * tok, tok), tok)
    loads = {}
    for i, name in enumerate(
        ("owner", "offset", "w_uvqk", "w_out", "b", "rel", "time", "gain_out", "gain_in", "b_out", "lengths", "times")
    ):
        loads[name] = local(i, s[name], s[name + "_v"])
    loads["ctx"] = local(12, s["context"].at[mine], s["ctx_v"].at[ka])
    loads["cot"] = local(13, s["cot"].at[mine], s["cot_v"].at[ka])
    own_cols = pl.ds(pl.multiple_of(ha * half, half), half)

    def table_copy(i):
        rows = pl.ds(pl.multiple_of(i * chunk, chunk), chunk)
        return pltpu.make_async_copy(table.at[rows, own_cols], table_buf.at[rows], table_sem.at[i])

    for i in range(chunks):
        table_copy(i).start()
    barrier = pltpu.get_barrier_semaphore()
    far, near = list(range(owners // 2, owners)), list(range(1, owners // 2))
    partners = [at.partner(k)[1] for k in far + near] + [at.x_peer, at.xy_peer]
    for device in partners:
        pl.semaphore_signal(barrier, inc=1, device_id=device, device_id_type=MESH)

    loads["owner"].wait()
    loads["offset"].wait()
    owner_row, offset_row = s["owner_v"][...], s["offset_v"][...]
    hits = (owner_row == iota((owners, count), 0)).astype(F32)
    earlier = mm(hits.astype(BF16), one_hot(iota((count, count), 0) < iota((count, count), 1)))
    rank = jnp.sum(hits * earlier, axis=0, keepdims=True).astype(jnp.int32)
    rank_hot = one_hot(rank == iota((128, count), 0))
    high = (offset_row // 64).astype(F32)
    low = (offset_row % 64 + 1).astype(F32)
    asked = 64.0 * mm_nt((hits * high).astype(BF16), rank_hot) + mm_nt((hits * low).astype(BF16), rank_hot) - 1.0
    asked = asked.astype(jnp.int32)
    for o in range(owners):
        s["requests"][o] = jnp.broadcast_to(asked[o : o + 1], (8, 128))
    place = owner_row * capacity + rank

    shard, w, small = s["shard"], s["w"], s["small"]
    loads["w_uvqk"].wait()
    for g in range(4):
        shard[:, g * half : (g + 1) * half] = s["w_uvqk_v"][:, g, :]
    loads["w_out"].wait()
    shard[:, 4 * half :] = s["w_out_v"][...]
    w[ha, at.pb] = shard[...]
    for name in ("b", "rel", "time", "gain_out"):
        loads[name].wait()
    small[ha, 0:4] = s["b_v"][...]
    small[ha, 4:8] = s["rel_v"][...]
    for i in range(2):
        for j in range(2):
            small[ha, 8 + i : 9 + i, j * buckets : (j + 1) * buckets] = s["time_v"][2 * i + j : 2 * i + j + 1]
    small[ha, 10:11] = s["gain_out_v"][...]

    pl.semaphore_wait(barrier, len(partners))

    def copies(name):
        return Copies(s[name + "_send"], s[name + "_recv"])

    requests, arrived = s["requests"], s["arrived"]
    req, item, emb_c, row_c, small_c = copies("req"), copies("item"), copies("emb"), copies("row"), copies("small")
    wz, wx, wy, wc = copies("wz"), copies("wx"), copies("wy"), copies("wc")
    for k in far + near:
        to, device = at.partner(k)
        req.start(requests.at[to], arrived.at[at.me], device)
    arrived[at.me] = requests[at.me]
    my_half = pl.ds(pl.multiple_of(ka * block, block), block)
    for d in range(1, zs):
        wz.start(shard.at[my_half], w.at[ha, at.pb, my_half], at.z_device(d))
    wx.start(shard, w.at[ha, at.pb], at.x_peer)
    small_c.start(small.at[ha], small.at[ha], at.x_peer)
    row_c.start(s["context"].at[away], s["ctx_v"].at[ka], at.y_peer)
    row_c.start(s["cot"].at[away], s["cot_v"].at[ka], at.y_peer)
    wc.start(shard, w.at[ha, at.pb], at.core_peer)

    for i in range(owners - 1):
        req.arrive(i)
    wide_pick = iota((capacity, 128), 1) == iota((capacity, 128), 0)

    def column_of(source):
        tile = jnp.broadcast_to(arrived[source, 0:1], (capacity, 128)).astype(F32)
        return jnp.sum(jnp.where(wide_pick, tile, 0.0), axis=1, keepdims=True)

    fetched, returned, parts, emb = s["fetched"], s["returned"], s["parts"], s["emb"]
    total = s["total"]
    askers = owners // 2

    def look_up(part):
        rounds = [(part * askers + d + 1) % owners for d in range(askers)]
        wanted = [column_of(at.owner_to(d)[0]) for d in rounds]
        column = jnp.concatenate(wanted, axis=0).astype(jnp.int32)
        total[...] = jnp.zeros_like(total)

        def step(i, carry):
            if part == 0:
                table_copy(i).wait()
            rows = pl.ds(pl.multiple_of(i * chunk, chunk), chunk)
            total[...] += mm(one_hot(column == iota((askers * capacity, chunk), 1) + i * chunk), table_buf[rows])
            return carry

        lax.fori_loop(0, chunks, step, 0)
        fetched[part] = total[...].astype(BF16).reshape(fetched.shape[1:])
        for i, d in enumerate(rounds):
            if d:
                item.start(fetched.at[part, i], returned.at[at.me], at.owner_to(d)[1])
            else:
                returned[at.me] = fetched[part, i]

    look_up(0)
    for d in range(1, zs):
        wz.arrive(d - 1)
        there = w.at[ha, at.z_from(d), my_half]
        wx.start(there, there, at.x_peer)
        wy.start(there, there, at.y_peer)
    look_up(1)
    wx.arrive(0)
    there = w.at[1 - ha, at.pb]
    wc.start(there, there, at.core_peer)
    for d in range(1, zs):
        wx.arrive(d)
        there = w.at[1 - ha, at.z_from(d), my_half]
        wy.start(there, there, at.y_peer)

    loads["lengths"].wait()
    loads["times"].wait()
    small_c.arrive(0)
    lane, row = iota((group, group), 1), iota((group, group), 0)
    lengths = s["lengths_v"][pl.ds(at.stream, 1), :]
    ends = jnp.zeros((1, 1), jnp.int32)
    member_row = jnp.zeros((group, group), jnp.int32)
    member_col = jnp.zeros((group, group), jnp.int32)
    inv_count = jnp.zeros((group, group), F32)
    for i in range(SEQ_GRP):
        length = lengths[:, i : i + 1]
        inside = (row >= ends) & (row < ends + length)
        inv_count = jnp.where(inside, 1.0 / jnp.maximum(length, 1).astype(F32), inv_count)
        ends = ends + length
        member_row = member_row + (ends <= row).astype(jnp.int32)
        member_col = member_col + (ends <= lane).astype(jnp.int32)
    allowed = (member_row == member_col) & (member_row < SEQ_GRP) & (lane <= row)
    maskscale = s["maskscale"]
    maskscale[...] = jnp.where(allowed, inv_count, 0.0)
    times_row = jnp.broadcast_to(s["times_v"][pl.ds(at.stream, 1), :], (group, group))
    times_col = jnp.sum(jnp.where(lane == row, times_row, 0).astype(F32), axis=1, keepdims=True).astype(jnp.int32)
    time_index = jnp.clip(times_col - times_row, 0, buckets - 1)
    turn = ((lane + row) % group == 0).astype(F32)
    rel_back = mm_exact(jnp.concatenate([small[0, 4:8, :], small[1, 4:8, :]], axis=0), turn)
    bias = s["bias"]
    for head in range(heads):
        hf, head_in = divmod(head, heads_half)
        begin = (head_in % 2) * buckets
        bucket_row = jnp.broadcast_to(small[hf, 8 + head_in // 2 : 9 + head_in // 2, begin : begin + buckets], (group, buckets))
        by_time = [
            jnp.take_along_axis(bucket_row, time_index[:, c : c + buckets], axis=1, mode="promise_in_bounds")
            for c in range(0, group, buckets)
        ]
        bias[head] = skew(jnp.broadcast_to(rel_back[head : head + 1], (group, group))) + jnp.concatenate(by_time, axis=1)

    for i in range(owners - 1):
        item.arrive(i)
    slot_hot = one_hot(place == iota((2 * count, count), 0))
    parts[...] = mm_tn(slot_hot, returned[...].reshape(2 * count, half)).astype(BF16).reshape(parts.shape)
    for device, to_ka, to_ha in at.quads:
        emb_c.start(parts.at[2 * to_ka + to_ha], emb.at[at.stream], device)
    emb[at.stream] = parts[at.stream]
    for d in range(1, zs):
        wy.arrive(d - 1)
        there = w.at[ha, at.z_from(d)]
        wc.start(there, there, at.core_peer)
    for d in range(1, zs):
        wy.arrive(zs - 2 + d)
        there = w.at[1 - ha, at.z_from(d)]
        wc.start(there, there, at.core_peer)
    slots = 2 * count
    low_lanes = iota((1, 128), 1) < capacity
    ids = []
    for i in range(owners // 2):
        ids.append(jnp.where(low_lanes, arrived[2 * i, 0:1], pltpu.roll(arrived[2 * i + 1, 0:1], capacity, 1)))
    ids_row = jnp.concatenate(ids, axis=1)
    ids_col = jnp.concatenate([column_of(o) for o in range(owners)], axis=0).astype(jnp.int32)
    last = table.shape[0]
    ids_row = jnp.where(ids_row < 0, last, ids_row)
    ids_col = jnp.where(ids_col < 0, last, ids_col)
    keys_row, keys_col = ids_row * slots + iota((1, slots), 1), ids_col * slots + iota((slots, 1), 0)
    order = jnp.sum((keys_col < keys_row).astype(F32), axis=0, keepdims=True).astype(jnp.int32)
    s["turn"][...] = one_hot(order == iota((slots, slots), 0))
    digits = jnp.concatenate([ids_row // 64, ids_row % 64] + [jnp.zeros((1, slots), jnp.int32)] * 6, axis=0)
    found = mm_nt(digits.astype(F32).astype(BF16), s["turn"][...])
    s["sorted_v"][...] = (64.0 * found[0:1] + found[1:2]).astype(jnp.int32)
    limits = iota((slots, 128), 1) * s["limit_rows"]
    s["limits_v"][...] = jnp.sum((ids_col < jnp.minimum(limits, last)).astype(F32), axis=0, keepdims=True).astype(jnp.int32)
    out_copies = [local(14, s["sorted_v"], s["sorted"]), local(15, s["limits_v"], s["limits"])]
    for i in range(2 * zs):
        wc.arrive(i)

    def w_half(hf, cols):
        return w[hf, :, :, cols].reshape(width, cols.stop - cols.start)

    out_cols = slice(4 * half, 5 * half)
    loads["cot"].wait()
    row_c.arrive(1)
    cot = s["cot_v"][...].reshape(group, width)
    grad_mixed = jnp.concatenate([mm(cot, w_half(hf, out_cols)) for hf in range(2)], axis=1)
    loads["gain_in"].wait()
    loads["b_out"].wait()
    loads["ctx"].wait()
    row_c.arrive(0)
    for i in range(3):
        emb_c.arrive(i)

    embedded = jnp.concatenate(
        [jnp.concatenate([emb[2 * i], emb[2 * i + 1]], axis=1).astype(F32) for i in range(2)], axis=0
    )
    start = s["ctx_v"][...].reshape(group, width).astype(F32) + embedded
    unit_in, inv_in = layer_norm(start)
    gain_in = s["gain_in_v"][...]
    normed = (unit_in * gain_in).astype(BF16)
    slope, qkv, w_att, sm = s["slope"], s["qkv"], s["w_att"], s["sm"]
    gates = []
    for hf in range(2):
        for g in range(4):
            cols = slice(g * half, (g + 1) * half)
            pre = mm(normed, w_half(hf, cols)) + small[hf, g : g + 1, :]
            sig = sigmoid(pre)
            act = pre * sig
            slope[hf, :, cols] = sig + act * (1.0 - sig)
            if g == 0:
                gates.append(act)
            else:
                qkv[hf, g - 1] = (act * 0.125 if g == 2 else act).astype(BF16)
    gate = jnp.concatenate(gates, axis=1)
    low_half = iota((group, 128), 1) < 64

    def split(tile):
        zero = jnp.zeros_like(tile)
        return jnp.where(low_half, tile, zero), jnp.where(low_half, zero, tile)

    attended = []
    for hf in range(2):
        for pair in range(pairs):
            cols = slice(pair * 128, (pair + 1) * 128)
            values, queries = split(qkv[hf, 0, :, cols]), split(qkv[hf, 1, :, cols])
            keys = qkv[hf, 2, :, cols]
            both = None
            for sub in range(2):
                head = hf * heads_half + pair * 2 + sub
                scores = mm_nt(queries[sub], keys) + bias[head]
                sig = sigmoid(scores)
                act = scores * sig
                weights = (act * maskscale[...]).astype(BF16)
                w_att[head] = weights
                sm[head] = (sig + act * (1.0 - sig)) * maskscale[...]
                part = mm(weights, values[sub])
                both = part if both is None else both + part
            attended.append(both)
    unit_out, inv_out = layer_norm(jnp.concatenate(attended, axis=1))
    gain_out = jnp.concatenate([small[0, 10:11, :], small[1, 10:11, :]], axis=1)
    mixed_in = (unit_out * gain_out * gate).astype(BF16)
    projected = None
    for hf in range(2):
        part = mm_nt(mixed_in[:, hf * half : (hf + 1) * half], w_half(hf, out_cols))
        projected = part if projected is None else projected + part
    mixed, mixed_rows = s["mixed"], s["mixed_v"]
    mixed[...] = (projected + s["b_out_v"][...] + start).astype(BF16)
    mixed_c = copies("mixed")
    for device, to_ka, to_ha in at.quads:
        here = mixed.at[pl.ds(to_ka * tok, tok), pl.ds(pl.multiple_of(to_ha * half, half), half)]
        mixed_c.start(here, mixed_rows.at[at.stream], device)
    own_rows = pl.ds(pl.multiple_of(ka * tok, tok), tok)
    mixed_rows[at.stream] = mixed[own_rows, pl.ds(pl.multiple_of(ha * half, half), half)]

    grad_pre, grad_small = s["grad_pre"], s["grad_small"]
    grad_raw = grad_mixed * unit_out
    grad_gate = grad_raw * gain_out
    grad_gain_out = jnp.sum(grad_raw * gate, axis=0, keepdims=True)
    grad_att = layer_norm_back(grad_mixed * gate * gain_out, unit_out, inv_out).astype(BF16)
    sum_a = WeightSum(at, ORDERS["a_"], s, "a_")
    sums_b = [WeightSum(at, ORDERS[f"b{i}_"], s, f"b{i}_") for i in range(pairs)]

    hops = {"a_": sum_a} | {f"b{i}_": part for i, part in enumerate(sums_b)}

    def steps_at(point):
        for name in STEPS[point]:
            hops[name].hop()

    def put(own, hf, first, value):
        cols = value.shape[1]
        own[hf, :, :, :, first : first + cols] = value.astype(BF16).reshape(own.shape[1:4] + (cols,))

    for hf in range(2):
        cols = slice(hf * half, (hf + 1) * half)
        grad_pre[hf, :, 0:half] = (grad_gate[:, cols] * slope[hf, :, 0:half]).astype(BF16)
        grad_small[hf, 10:11, :] = grad_gain_out[:, cols]
        put(s["a_own"], hf, 0, mm_tn(normed, grad_pre[hf, :, 0:half]))
        put(s["a_own"], hf, half, mm_tn(cot, mixed_in[:, cols]))
    sum_a.cores()

    gs = s["gs"]
    for pair in range(pairs):
        for hf in range(2):
            cols = slice(pair * 128, (pair + 1) * 128)
            values = qkv[hf, 0, :, cols]
            queries, keys = split(qkv[hf, 1, :, cols]), split(qkv[hf, 2, :, cols])
            grads = split(grad_att[:, hf * half + pair * 128 : hf * half + (pair + 1) * 128])
            sums = None
            for sub in range(2):
                head = hf * heads_half + pair * 2 + sub
                grad_scores = (mm_nt(grads[sub], values) * sm[head]).astype(BF16)
                gs[:, head * group : (head + 1) * group] = grad_scores
                found = (
                    mm_tn(w_att[head], grads[sub]),
                    mm(grad_scores, keys[sub]),
                    mm_tn(grad_scores, queries[sub]),
                )
                sums = found if sums is None else [a + b for a, b in zip(sums, found)]
            for g, part in ((1, sums[0]), (2, sums[1] * 0.125), (3, sums[2])):
                there = slice(g * half + pair * 128, g * half + (pair + 1) * 128)
                grad_pre[hf, :, there] = (part * slope[hf, :, there]).astype(BF16)
        if pair == 0:
            steps_at("pair 0")
        if pair < pairs - 1:
            for hf in range(2):
                for g in range(1, 4):
                    there = slice(g * half + pair * 128, g * half + (pair + 1) * 128)
                    put(s[f"b{pair}_own"], hf, (g - 1) * 128, mm_tn(normed, grad_pre[hf, :, there]))
            sums_b[pair].cores()
    grad_normed = None
    for hf in range(2):
        part = mm_nt(grad_pre[hf], w_half(hf, slice(0, 4 * half)))
        grad_normed = part if grad_normed is None else grad_normed + part
    cot32 = cot.astype(F32)
    grad_start, grad_rows = s["grad_start"], s["grad_rows_v"]
    grad_start[...] = (cot32 + layer_norm_back(grad_normed * gain_in, unit_in, inv_in)).astype(BF16)
    back_c = copies("back")
    for first in (True, False):
        for device, to_ka, to_ha in at.quads:
            h = to_ha if first else 1 - to_ha
            cols = pl.ds(pl.multiple_of(h * half, half), half)
            here = grad_start.at[pl.ds(pl.multiple_of(to_ka * tok, tok), tok), cols]
            back_c.start(here, grad_rows.at[at.stream, :, cols], device)
    grad_rows[at.stream] = grad_start[own_rows]
    for hf in range(2):
        for g in range(1, 4):
            there = slice(g * half + (pairs - 1) * 128, g * half + pairs * 128)
            put(s[f"b{pairs - 1}_own"], hf, (g - 1) * 128, mm_tn(normed, grad_pre[hf, :, there]))
    sums_b[-1].cores()
    steps_at("rows sent")
    gain_grad = jnp.sum(grad_normed * unit_in, axis=0, keepdims=True)
    bout_grad = jnp.sum(cot32, axis=0, keepdims=True)
    for hf in range(2):
        sums = jnp.sum(grad_pre[hf].astype(F32), axis=0, keepdims=True)
        for g in range(4):
            grad_small[hf, g : g + 1, :] = sums[:, g * half : (g + 1) * half]
        grad_small[hf, 11:12, :] = gain_grad[:, hf * half : (hf + 1) * half]
        grad_small[hf, 12:13, :] = bout_grad[:, hf * half : (hf + 1) * half]
        grad_small[hf, 13:16, :] = jnp.zeros((3, half), F32)
    flip = (lane + row == group - 1).astype(F32)
    kept_pairs = lane + row <= group - 1
    hot_cols = one_hot(times_row == row)
    hot_back = one_hot(times_row == group - 1 - row)
    folded = mm(jnp.concatenate([flip.astype(BF16), hot_back], axis=0), gs[...])
    rel_rows, time_rows, early_rows = [], [], []
    for head in range(heads):
        places = slice(head * group, (head + 1) * group)
        rel_rows.append(jnp.sum(skew(folded[:group, places]), axis=0, keepdims=True))
        pairs_sum = mm_nt(folded[group:, places].astype(BF16), hot_cols)
        kept = jnp.where(kept_pairs, pairs_sum, 0.0)
        time_rows.append(jnp.sum(skew(kept), axis=0, keepdims=True))
        early_rows.append(jnp.sum(pairs_sum - kept, axis=0, keepdims=True))
    flipped = mm_exact(jnp.concatenate(rel_rows + time_rows, axis=0), flip)
    early = jnp.sum(jnp.concatenate(early_rows, axis=0), axis=1, keepdims=True)
    late = jnp.sum(flipped[heads:, buckets:], axis=1, keepdims=True)
    place_in = iota((heads, buckets), 1)
    time_grad = flipped[heads:, :buckets] + jnp.where(place_in == 0, early, 0.0) + jnp.where(place_in == buckets - 1, late, 0.0)
    for head in range(heads):
        hf, head_in = divmod(head, heads_half)
        begin = (head_in % 2) * buckets
        grad_small[hf, 4 + head_in : 5 + head_in, :] = flipped[head : head + 1]
        grad_small[hf, 8 + head_in // 2 : 9 + head_in // 2, begin : begin + buckets] = time_grad[head : head + 1]
    small_in, small_mine = s["small_in"], s["small_mine"]
    sum_c = copies("sum")
    sum_c.start(grad_small, small_in.at[0], at.core_peer)

    steps_at("tables")
    for i in range(3):
        back_c.arrive(i)
    outgoing, incoming = s["outgoing"], s["incoming"]
    slot_hot = one_hot(place == iota((2 * count, count), 0))
    outgoing[...] = mm(slot_hot, grad_rows[:, :, own_cols].reshape(count, half)).astype(BF16).reshape(outgoing.shape)
    give, hand = copies("give"), copies("hand")
    given = {}

    def start_give(*rounds):
        for k in rounds:
            to, device = at.partner(k)
            given[k] = len(give.copies)
            give.start(outgoing.at[to], incoming.at[ha, at.me], device)

    start_give(8, 9, 10, 11, 1, 2, 3, 4, 5, 6, 7)
    incoming[ha, at.me] = outgoing[at.me]
    hand.start(incoming.at[ha, at.me], incoming.at[ha, at.me], at.x_peer)

    def take(*rounds):
        for k in rounds:
            give.arrive(given[k])
            there = incoming.at[ha, at.partner(k)[0]]
            hand.start(there, there, at.x_peer)

    steps_at("given")
    take(1, 2, 3)
    sum_c.arrive(0)
    small_mine[0] = grad_small[...] + small_in[0]
    for i, (device, _, _) in enumerate(at.quads):
        sum_c.start(small_mine.at[0], small_in.at[1 + i], device)
    steps_at("take 1")
    take(8, 9)
    start_give(12, 13)
    steps_at("take 2")
    take(4, 5, 6, 7)
    steps_at("take 3")
    take(10, 11)
    start_give(14, 15)
    summed = small_mine[0]
    for i in range(1, 4):
        sum_c.arrive(i)
        summed = summed + small_in[i]
    small_mine[1] = summed
    for d in range(1, zs):
        sum_c.start(small_mine.at[1], small_in.at[3 + d], at.z_device(d))
    steps_at("take 4")
    take(12, 13)
    steps_at("take 5")
    take(14, 15)
    def in_order(h):
        cols = pl.ds(pl.multiple_of(h * half, half), half)
        s["rows_v"][:, cols] = mm(s["turn"][...], incoming[h].reshape(slots, half)).astype(BF16)

    in_order(ha)
    for i in range(3, 6):
        back_c.arrive(i)
    out_copies.append(local(16, grad_rows, s["grad_rows"]))
    for i in range(3):
        mixed_c.arrive(i)
    out_copies.append(local(17, mixed_rows, s["mixed_rows"]))
    grad_w = s["grad_w_v"]
    grad_w[:, 0:gates_cols] = sum_a.finish()
    for i in range(pairs):
        first = gates_cols + i * 384
        grad_w[:, first : first + 384] = sums_b[i].finish()
    summed = small_mine[1]
    for d in range(1, zs):
        sum_c.arrive(3 + d)
        summed = summed + small_in[3 + d]
    s["small_v"][...] = summed
    out_copies += [local(18, grad_w, s["grad_w"]), local(19, s["small_v"], s["small_sum"])]
    for i in range(owners):
        hand.arrive(i)
    in_order(1 - ha)
    out_copies.append(local(20, s["rows_v"], s["rows"]))
    for copy in out_copies:
        copy.wait()
    for kind in (req, item, emb_c, row_c, small_c, wz, wx, wy, wc, mixed_c, back_c, give, hand, sum_c):
        kind.sent()
    for part in [sum_a] + sums_b:
        part.copies.sent()


def run_main(inputs):
    pbs, kas = lax.axis_size("pb"), lax.axis_size("ka")
    owners, zs = pbs * kas, pbs // 2
    count, width = inputs["context"].shape
    half, tok, capacity = width // 2, count // MB, 2 * count // owners
    group, heads = 2 * tok, width // 64
    shard_rows = inputs["w_uvqk"].shape[0]
    block = shard_rows // 2
    dma = pltpu.SemaphoreType.DMA
    outs = {
        "rows": jax.ShapeDtypeStruct((2 * count, width), BF16),
        "sorted": jax.ShapeDtypeStruct((1, 2 * count), jnp.int32),
        "limits": jax.ShapeDtypeStruct((1, 128), jnp.int32),
        "grad_rows": jax.ShapeDtypeStruct((MB, tok, width), BF16),
        "mixed_rows": jax.ShapeDtypeStruct((MB, tok, half), BF16),
        "grad_w": jax.ShapeDtypeStruct((block, 5 * half), F32),
        "small_sum": jax.ShapeDtypeStruct((2, 16, half), F32),
    }
    scratch = {
        "ctx_v": pltpu.VMEM((2, tok, width), BF16),
        "cot_v": pltpu.VMEM((2, tok, width), BF16),
        "requests": pltpu.VMEM((owners, 8, 128), jnp.int32),
        "arrived": pltpu.VMEM((owners, 8, 128), jnp.int32),
        "table_buf": pltpu.VMEM((inputs["table"].shape[0], half), BF16),
        "total": pltpu.VMEM((count, half), F32),
        "fetched": pltpu.VMEM((2, owners // 2, capacity, half), BF16),
        "returned": pltpu.VMEM((owners, capacity, half), BF16),
        "parts": pltpu.VMEM((MB, tok, half), BF16),
        "emb": pltpu.VMEM((MB, tok, half), BF16),
        "shard": pltpu.VMEM((shard_rows, 5 * half), BF16),
        "w": pltpu.VMEM((2, pbs, shard_rows, 5 * half), BF16),
        "small": pltpu.VMEM((2, 16, half), F32),
        "maskscale": pltpu.VMEM((group, group), F32),
        "bias": pltpu.VMEM((heads, group, group), F32),
        "slope": pltpu.VMEM((2, group, 4 * half), F32),
        "qkv": pltpu.VMEM((2, 3, group, half), BF16),
        "w_att": pltpu.VMEM((heads, group, group), BF16),
        "sm": pltpu.VMEM((heads, group, group), F32),
        "gs": pltpu.VMEM((group, heads * group), BF16),
        "grad_pre": pltpu.VMEM((2, group, 4 * half), BF16),
        "mixed": pltpu.VMEM((group, width), BF16),
        "grad_start": pltpu.VMEM((group, width), BF16),
        "grad_small": pltpu.VMEM((2, 16, half), F32),
        "outgoing": pltpu.VMEM((owners, capacity, half), BF16),
        "small_mine": pltpu.VMEM((2, 2, 16, half), F32),
        "small_in": pltpu.VMEM((3 + zs, 2, 16, half), F32),
        "incoming": pltpu.VMEM((2, owners, capacity, half), BF16),
        "rows_v": pltpu.VMEM((2 * count, width), BF16),
        "turn": pltpu.VMEM((2 * count, 2 * count), BF16),
        "sorted_v": pltpu.VMEM((1, 2 * count), jnp.int32),
        "limits_v": pltpu.VMEM((1, 128), jnp.int32),
        "grad_rows_v": pltpu.VMEM((MB, tok, width), BF16),
        "mixed_v": pltpu.VMEM((MB, tok, half), BF16),
        "grad_w_v": pltpu.VMEM((block, 5 * half), F32),
        "small_v": pltpu.VMEM((2, 16, half), F32),
        "load_sem": dma((21,)),
        "table_sem": dma((4,)),
    }
    for name in ("owner", "offset", "w_uvqk", "w_out", "b", "rel", "time", "gain_out", "gain_in", "b_out", "lengths", "times"):
        scratch[name + "_v"] = pltpu.VMEM(inputs[name].shape, inputs[name].dtype)
    for name, number in (
        ("req", owners - 1), ("item", owners - 1), ("emb", 3), ("row", 2), ("small", 1), ("wz", zs - 1), ("wx", zs),
        ("wy", 2 * zs - 2), ("wc", 2 * zs), ("mixed", 3), ("back", 6), ("give", owners - 1), ("hand", owners), ("sum", 3 + zs),
    ):
        scratch[name + "_send"] = dma((number,))
        scratch[name + "_recv"] = dma((number,))
    scratch |= weight_sum_scratch("a_", ORDERS["a_"], zs, block, 2 * half)
    for i in range(half // 128):
        scratch |= weight_sum_scratch(f"b{i}_", ORDERS[f"b{i}_"], zs, block, 384)
    hbm = pl.BlockSpec(memory_space=pltpu.HBM)
    found = pl.pallas_call(
        functools.partial(main_kernel, tuple(inputs), tuple(outs), tuple(scratch)),
        out_shape=tuple(outs.values()),
        in_specs=[hbm] * len(inputs),
        out_specs=(hbm,) * len(outs),
        scratch_shapes=list(scratch.values()),
        compiler_params=pltpu.CompilerParams(
            collective_id=1, has_side_effects=True, vmem_limit_bytes=58 * 1024 * 1024
        ),
    )(*inputs.values())
    return dict(zip(outs, found, strict=True))


def scatter_kernel(
    limits_in, sorted_in, rows_in, grad_w_in, small_in, mixed_in, grad_rows_in,
    out_ref, w_ref, w_out_ref, b_ref, rel_ref, time_ref, gain_in_ref, gain_out_ref, b_out_ref, mixed_out, grad_rows_out,
    limits, ids, rows, grad_w_ref, small_ref, mixed, grad_rows, tiles, load_sem, tile_sem, pass_sem,
):
    pairs_in = [
        (limits_in, limits), (sorted_in, ids), (rows_in, rows), (grad_w_in, grad_w_ref), (small_in, small_ref),
        (mixed_in, mixed), (grad_rows_in, grad_rows),
    ]
    loads = [pltpu.make_async_copy(src, dst, load_sem.at[i]) for i, (src, dst) in enumerate(pairs_in)]
    for load in loads:
        load.start()
    for load in loads[:3]:
        load.wait()
    slots, tile = tiles.shape[0], tiles.shape[1]
    count = out_ref.shape[0] // tile
    per_tile = tile // 256
    depth = 256

    def write(i, slot):
        there = pl.ds(pl.multiple_of(i * tile, tile), tile)
        return pltpu.make_async_copy(tiles.at[slot], out_ref.at[there], tile_sem.at[slot])

    def step(i, carry):
        slot = lax.rem(i, slots)

        @pl.when(i >= slots)
        def _():
            write(i - slots, slot).wait()

        first = limits[0, i * per_tile] // depth
        end = (limits[0, (i + 1) * per_tile] + depth - 1) // depth

        def product(j):
            here = pl.ds(pl.multiple_of(j * depth, depth), depth)
            return mm(one_hot(ids[:, here] == iota((tile, depth), 0) + i * tile), rows[here, :])

        tiles[slot] = product(jnp.minimum(first, rows.shape[0] // depth - 1))

        def more(j, carry):
            tiles[slot] += product(j)
            return carry

        lax.fori_loop(first + 1, end, more, 0)
        write(i, slot).start()
        return carry

    lax.fori_loop(0, 2, step, 0)
    for load in loads[3:]:
        load.wait()
    passed = [
        pltpu.make_async_copy(mixed, mixed_out, pass_sem.at[0]),
        pltpu.make_async_copy(grad_rows, grad_rows_out, pass_sem.at[1]),
    ]
    for copy in passed:
        copy.start()
    lax.fori_loop(2, count, step, 0)
    half = w_ref.shape[2]
    buckets = time_ref.shape[1]
    w_ref[:, 0, :] = grad_w_ref[:, 0:half]
    w_out_ref[...] = grad_w_ref[:, half : 2 * half]
    for pair in range(half // 128):
        for g in range(1, 4):
            first = 2 * half + pair * 384 + (g - 1) * 128
            w_ref[:, g, pair * 128 : (pair + 1) * 128] = grad_w_ref[:, first : first + 128]
    ha = lax.axis_index("ha")
    b_ref[...] = small_ref[ha, 0:4, :]
    rel_ref[...] = small_ref[ha, 4:8, :]
    for i in range(2):
        for j in range(2):
            time_ref[2 * i + j : 2 * i + j + 1, :] = small_ref[ha, 8 + i : 9 + i, j * buckets : (j + 1) * buckets]
    gain_out_ref[...] = small_ref[ha, 10:11, :]
    for hf in range(2):
        gain_in_ref[:, hf * half : (hf + 1) * half] = small_ref[hf, 11:12, :]
        b_out_ref[:, hf * half : (hf + 1) * half] = small_ref[hf, 12:13, :]
    for k in range(slots):
        write(count - slots + k, (count - slots + k) % slots).wait()
    for copy in passed:
        copy.wait()


def scatter_rows(found, table_rows, buckets, tile=512, slots=4):
    rows, grad_w = found["rows"], found["grad_w"]
    width = rows.shape[1]
    half, block = width // 2, grad_w.shape[0]
    names = ("limits", "sorted", "rows", "grad_w", "small_sum", "mixed_rows", "grad_rows")
    shapes = [(block, 4, half), (block, half), (4, half), (4, half), (4, buckets), (1, width), (1, half), (1, width)]
    hbm, vmem = pl.BlockSpec(memory_space=pltpu.HBM), pl.BlockSpec(memory_space=pltpu.VMEM)
    outs = [jax.ShapeDtypeStruct(shape, F32) for shape in [(table_rows, width)] + shapes]
    outs += [jax.ShapeDtypeStruct(found[name].shape, BF16) for name in ("mixed_rows", "grad_rows")]
    return pl.pallas_call(
        scatter_kernel,
        out_shape=outs,
        in_specs=[hbm] * len(names),
        out_specs=[hbm] + [vmem] * len(shapes) + [hbm] * 2,
        scratch_shapes=[
            pltpu.SMEM(found["limits"].shape, jnp.int32),
            pltpu.VMEM(found["sorted"].shape, jnp.int32),
            pltpu.VMEM(rows.shape, BF16),
            pltpu.VMEM(grad_w.shape, F32),
            pltpu.VMEM(found["small_sum"].shape, F32),
            pltpu.VMEM(found["mixed_rows"].shape, BF16),
            pltpu.VMEM(found["grad_rows"].shape, BF16),
            pltpu.VMEM((slots, tile, width), F32),
            pltpu.SemaphoreType.DMA((len(names),)),
            pltpu.SemaphoreType.DMA((slots,)),
            pltpu.SemaphoreType.DMA((2,)),
        ],
        compiler_params=pltpu.CompilerParams(vmem_limit_bytes=58 * 1024 * 1024),
    )(*(found[name] for name in names))


def local_streams(
    context,
    item_owner,
    item_offset,
    lengths,
    times,
    table,
    cotangent,
    ln_in_gain,
    w_uvqk,
    b_uvqk,
    rel_bias,
    time_bias,
    ln_out_gain,
    w_out,
    b_out,
):
    row_count, width = context.shape
    half = width // 2
    found = run_main(
        {
            "owner": item_owner.reshape(1, row_count),
            "offset": item_offset.reshape(1, row_count),
            "context": context,
            "cot": cotangent,
            "table": table,
            "w_uvqk": w_uvqk,
            "w_out": w_out.T,
            "b": b_uvqk,
            "rel": rel_bias,
            "time": time_bias,
            "gain_out": ln_out_gain.reshape(1, half),
            "gain_in": ln_in_gain.reshape(1, width),
            "b_out": b_out.reshape(1, width),
            "lengths": lengths[0],
            "times": times[0],
        }
    )
    (
        table_grad, grad_w, grad_w_out, grad_b, grad_rel, grad_time, grad_gain_in, grad_gain_out, grad_b_out, mixed, grad_rows,
    ) = scatter_rows(found, table.shape[0], time_bias.shape[1])
    return (
        mixed.reshape(row_count, half),
        grad_rows.reshape(row_count, width),
        table_grad,
        grad_gain_in.reshape(width),
        grad_w,
        grad_b,
        grad_rel,
        grad_time,
        grad_gain_out.reshape(half),
        grad_w_out.T,
        grad_b_out.reshape(width),
    )


def solution(mesh):
    one_stream = mesh.shape["ka"] * mesh.shape["ha"] == MB and mesh.shape["ka"] == 2 and mesh.shape["pb"] == 8
    return jax.shard_map(
        local_streams if one_stream else local_general,
        mesh=mesh,
        in_specs=(
            P(("pb", "ka"), None),
            P(("pb", "ka"), None),
            P(("pb", "ka")),
            P("pb", None, None),
            P("pb", None, None),
            P(("pb", "ka"), None),
            P(("pb", "ka"), None),
            P(),
            P("pb", None, "ha"),
            P(None, "ha"),
            P("ha", None),
            P("ha", None),
            P("ha"),
            P("ha", "pb"),
            P(),
        ),
        out_specs=(
            P(("pb", "ka"), "ha"),
            P(("pb", "ka"), None),
            P(("pb", "ka"), None),
            P(),
            P(("pb", "ka"), None, "ha"),
            P(None, "ha"),
            P("ha", None),
            P("ha", None),
            P("ha"),
            P("ha", ("pb", "ka")),
            P(),
        ),
        check_vma=False,
    )
```

```python
import functools

import jax
import jax.numpy as jnp
from jax import lax
from jax.experimental import pallas as pl
from jax.experimental.pallas import tpu as pltpu
from jax.sharding import PartitionSpec as P

DH = 64
TOK_DEV = 128
MB = 4
SEQ_GRP = 4
F32 = jnp.float32
BF16 = jnp.bfloat16


epsilon = 1e-05


def silu_slope(values):
    sigma = jax.nn.sigmoid(values)
    return sigma * (1.0 + values * (1.0 - sigma))


def norm_rows(values, gain):
    centered = values - jnp.mean(values, axis=-1, keepdims=True)
    inverse = lax.rsqrt(jnp.mean(centered * centered, axis=-1, keepdims=True) + epsilon)
    unit_rows = centered * inverse
    return (unit_rows * gain, unit_rows, inverse)


def norm_back(grad_unit, unit_rows, inverse):
    first_mean = jnp.mean(grad_unit, axis=-1, keepdims=True)
    second_mean = jnp.mean(grad_unit * unit_rows, axis=-1, keepdims=True)
    return inverse * (grad_unit - first_mean - unit_rows * second_mean)


def stream_layout(lengths_row, group):
    places = jnp.arange(group, dtype=jnp.int32)
    ends = jnp.cumsum(lengths_row, dtype=jnp.int32)
    member = jnp.sum((ends[None, :] <= places[:, None]).astype(jnp.int32), axis=1)
    onehot = (member[:, None] == jnp.arange(SEQ_GRP, dtype=jnp.int32)[None, :]).astype(jnp.float32)
    counted = jnp.maximum(jnp.sum(onehot * lengths_row.astype(jnp.float32)[None, :], axis=1), 1.0)
    return (places, member, counted)


def diagonal_bias(rel_bias, query_first, key_first, query_len, key_len):
    heads, group = rel_bias.shape
    span = query_len + key_len - 1
    padded = jnp.concatenate([jnp.zeros((heads, group), jnp.float32), rel_bias], axis=1)
    window = lax.dynamic_slice_in_dim(
        padded, query_first - key_first - key_len + 1 + group, span, 1
    )
    flipped = jnp.concatenate([window[:, ::-1], jnp.zeros((heads, 1), jnp.float32)], axis=1)
    skewed = jnp.tile(flipped, (1, query_len))[:, : query_len * span].reshape(
        heads, query_len, span
    )
    return skewed[:, :, query_len - 1 : query_len - 1 + key_len]


def diagonal_sums(grad_scores, query_first, key_first, group):
    heads, query_len, key_len = grad_scores.shape
    span = query_len + key_len - 1
    widened = jnp.pad(grad_scores.astype(jnp.float32), ((0, 0), (0, 0), (query_len - 1, 0)))
    flat = jnp.pad(widened.reshape(heads, query_len * span), ((0, 0), (0, query_len)))
    totals = jnp.sum(flat.reshape(heads, query_len, span + 1), axis=1)
    window = totals[:, :span][:, ::-1]
    placed = lax.dynamic_update_slice_in_dim(
        jnp.zeros((heads, 2 * group), jnp.float32),
        window,
        query_first - key_first - key_len + 1 + group,
        1,
    )
    return placed[:, group:]


def bucket_lookup(time_bias, bucket_hot):
    high = time_bias.astype(jnp.bfloat16)
    rest = time_bias - high.astype(jnp.float32)
    middle = rest.astype(jnp.bfloat16)
    lowest = (rest - middle.astype(jnp.float32)).astype(jnp.bfloat16)
    pieces = jnp.einsum(
        "phb,qkb->phqk",
        jnp.stack([high, middle, lowest]),
        bucket_hot,
        preferred_element_type=jnp.float32,
    )
    return pieces[0] + pieces[1] + pieces[2]


def tile_scores(query_heads, key_heads, query_info, key_info, rel_bias, time_bias):
    query_pos, query_member, query_count, query_stamp = query_info
    key_pos, key_member, key_stamp = key_info
    distance = query_pos[:, None] - key_pos[None, :]
    time_index = jnp.clip(query_stamp[:, None] - key_stamp[None, :], 0, time_bias.shape[1] - 1)
    bucket_hot = (
        time_index[:, :, None] == jnp.arange(time_bias.shape[1], dtype=jnp.int32)[None, None, :]
    ).astype(jnp.bfloat16)
    scores = jnp.einsum(
        "qhd,khd->hqk", query_heads, key_heads, preferred_element_type=jnp.float32
    ) * DH ** (-0.5)
    scores = (
        scores
        + diagonal_bias(rel_bias, query_pos[0], key_pos[0], query_pos.shape[0], key_pos.shape[0])
        + bucket_lookup(time_bias, bucket_hot)
    )
    allowed = (
        (query_member[:, None] == key_member[None, :])
        & (query_member[:, None] < SEQ_GRP)
        & (distance >= 0)
    )[None]
    weights = (jnp.where(allowed, jax.nn.silu(scores), 0.0) / query_count[None, :, None]).astype(
        jnp.bfloat16
    )
    return (scores, allowed, weights, bucket_hot)


def score_grads(grad_weights, scores, allowed, query_count):
    return (
        jnp.where(allowed, grad_weights / query_count[None, :, None], 0.0) * silu_slope(scores)
    ).astype(jnp.bfloat16)


def local_general(
    context,
    item_owner,
    item_offset,
    lengths,
    times,
    table,
    cotangent,
    ln_in_gain,
    w_uvqk,
    b_uvqk,
    rel_bias,
    time_bias,
    ln_out_gain,
    w_out,
    b_out,
):
    owners = lax.axis_size(("pb", "ka"))
    row_count = context.shape[0]
    width = context.shape[1]
    capacity = max(2, 2 * row_count // owners)
    owner_ids = item_owner[:, 0]
    owner_hits = (owner_ids[:, None] == jnp.arange(owners, dtype=jnp.int32)[None, :]).astype(
        jnp.int32
    )
    earlier = jnp.sum((jnp.cumsum(owner_hits, axis=0) - owner_hits) * owner_hits, axis=1)
    slot_index = owner_ids * capacity + earlier
    requests = jnp.zeros((owners * capacity,), jnp.int32).at[slot_index].set(item_offset + 1)
    arrived = lax.all_to_all(
        requests.reshape(owners, capacity), ("pb", "ka"), split_axis=0, concat_axis=0, tiled=True
    ).reshape(-1)
    present = arrived > 0
    local_rows = jnp.maximum(arrived - 1, 0)
    fetched = jnp.where(present[:, None], table[local_rows], jnp.zeros((), jnp.bfloat16))
    returned = lax.all_to_all(
        fetched.reshape(owners, capacity, width),
        ("pb", "ka"),
        split_axis=0,
        concat_axis=0,
        tiled=True,
    )
    embedded = returned.reshape(owners * capacity, width)[slot_index]
    start = context.astype(jnp.float32) + embedded.astype(jnp.float32)
    group = lax.axis_size("ka") * TOK_DEV
    block_start = lax.axis_index("ka") * TOK_DEV
    half_cols = w_out.shape[0]
    heads = half_cols // DH
    full_cols = half_cols * lax.axis_size("ha")
    out_cols = width // lax.axis_size("ha")
    out_start = lax.axis_index("ha") * out_cols
    bias_half = lax.dynamic_slice_in_dim(b_out, out_start, out_cols)
    scale = DH ** (-0.5)
    grad_gain_in = jnp.zeros(ln_in_gain.shape, jnp.float32)
    grad_bias_proj = jnp.zeros(b_uvqk.shape, jnp.float32)
    grad_rel = jnp.zeros(rel_bias.shape, jnp.float32)
    grad_time = jnp.zeros(time_bias.shape, jnp.float32)
    grad_gain_out = jnp.zeros(ln_out_gain.shape, jnp.float32)
    grad_bias_out = jnp.zeros(b_out.shape, jnp.float32)
    weight_total = None
    mixed_parts = []
    grad_parts = []
    for micro in range(MB):
        w_full, w_final = (
            lax.all_gather(w_uvqk, "pb", axis=0, tiled=True),
            lax.all_gather(w_out, "pb", axis=1, tiled=True),
        )
        x_in = start[micro * TOK_DEV : (micro + 1) * TOK_DEV]
        cot_rows = cotangent[micro * TOK_DEV : (micro + 1) * TOK_DEV]
        stamps = times[0, micro]
        places, member, counted = stream_layout(lengths[0, micro], group)
        query_pos = lax.dynamic_slice_in_dim(places, block_start, TOK_DEV)
        query_member = lax.dynamic_slice_in_dim(member, block_start, TOK_DEV)
        query_count = lax.dynamic_slice_in_dim(counted, block_start, TOK_DEV)
        query_stamp = lax.dynamic_slice_in_dim(stamps, block_start, TOK_DEV)
        normed_float, unit_in, inverse_in = norm_rows(x_in, ln_in_gain)
        normed = normed_float.astype(jnp.bfloat16)
        pre_act = (
            jnp.einsum("td,dgc->tgc", normed, w_full, preferred_element_type=jnp.float32) + b_uvqk
        )
        activated = jax.nn.silu(pre_act)
        gate_part = activated[:, 0]
        values = activated[:, 1].astype(jnp.bfloat16)
        queries = activated[:, 2].astype(jnp.bfloat16)
        key_rows = activated[:, 3].astype(jnp.bfloat16)
        key_pair = lax.all_gather(jnp.stack([key_rows, values]), "ka", axis=1, tiled=True)
        all_keys = key_pair[0].reshape(group, heads, DH)
        all_values = key_pair[1].reshape(group, heads, DH)
        query_heads = queries.reshape(TOK_DEV, heads, DH)
        scores, allowed, weights, bucket_hot = tile_scores(
            query_heads,
            all_keys,
            (query_pos, query_member, query_count, query_stamp),
            (places, member, stamps),
            rel_bias,
            time_bias,
        )
        attended = jnp.einsum(
            "hqk,khd->qhd", weights, all_values, preferred_element_type=jnp.float32
        ).reshape(TOK_DEV, half_cols)
        row_total, row_square = lax.psum(
            (jnp.sum(attended, axis=1), jnp.sum(attended * attended, axis=1)), "ha"
        )
        row_mean = row_total / full_cols
        inverse_out = lax.rsqrt(row_square / full_cols - row_mean * row_mean + epsilon)[:, None]
        unit_out = (attended - row_mean[:, None]) * inverse_out
        mixed_in = (unit_out * ln_out_gain * gate_part).astype(jnp.bfloat16)
        partial_out = jnp.dot(mixed_in, w_final, preferred_element_type=jnp.float32)
        summed_out = lax.psum_scatter(partial_out, "ha", scatter_dimension=1, tiled=True)
        residual = lax.dynamic_slice_in_dim(x_in, out_start, out_cols, 1)
        mixed_parts.append((summed_out + bias_half + residual).astype(jnp.bfloat16))
        grad_final_part = jnp.einsum(
            "tc,td->cd", mixed_in, cot_rows, preferred_element_type=jnp.float32
        )
        grad_bias_out = grad_bias_out + jnp.sum(cot_rows.astype(jnp.float32), axis=0)
        grad_mixed = jnp.einsum("td,cd->tc", cot_rows, w_final, preferred_element_type=jnp.float32)
        grad_gate = grad_mixed * unit_out * ln_out_gain
        grad_gain_out = grad_gain_out + jnp.sum(grad_mixed * unit_out * gate_part, axis=0)
        grad_unit = grad_mixed * gate_part * ln_out_gain
        first_total, second_total = lax.psum(
            (jnp.sum(grad_unit, axis=1), jnp.sum(grad_unit * unit_out, axis=1)), "ha"
        )
        grad_attended = (
            inverse_out
            * (
                grad_unit
                - first_total[:, None] / full_cols
                - unit_out * second_total[:, None] / full_cols
            )
        ).astype(jnp.bfloat16)
        grad_heads = grad_attended.reshape(TOK_DEV, heads, DH)
        grad_weights = jnp.einsum(
            "qhd,khd->hqk", grad_heads, all_values, preferred_element_type=jnp.float32
        )
        grad_scores = score_grads(grad_weights, scores, allowed, query_count)
        grad_rel = grad_rel + diagonal_sums(grad_scores, query_pos[0], places[0], rel_bias.shape[1])
        grad_time = grad_time + jnp.einsum(
            "hqk,qkb->hb", grad_scores, bucket_hot, preferred_element_type=jnp.float32
        )
        grad_queries = (
            jnp.einsum("hqk,khd->qhd", grad_scores, all_keys, preferred_element_type=jnp.float32)
            * scale
        ).reshape(TOK_DEV, half_cols)
        key_part = (
            jnp.einsum("hqk,qhd->khd", grad_scores, query_heads, preferred_element_type=jnp.float32)
            * scale
        )
        value_part = jnp.einsum(
            "hqk,qhd->khd", weights, grad_heads, preferred_element_type=jnp.float32
        )
        stacked = jnp.stack(
            [key_part.reshape(group, half_cols), value_part.reshape(group, half_cols)]
        )
        owned_grads = lax.psum_scatter(stacked, "ka", scatter_dimension=1, tiled=True)
        grad_keys = owned_grads[0]
        grad_values = owned_grads[1]
        grad_act = jnp.stack([grad_gate, grad_values, grad_queries, grad_keys], axis=1)
        grad_pre = (grad_act * silu_slope(pre_act)).astype(jnp.bfloat16)
        grad_proj_part = jnp.einsum(
            "td,tgc->dgc", normed, grad_pre, preferred_element_type=jnp.float32
        )
        grad_bias_proj = grad_bias_proj + jnp.sum(grad_pre.astype(jnp.float32), axis=0)
        grad_normed = lax.psum(
            jnp.einsum("tgc,dgc->td", grad_pre, w_full, preferred_element_type=jnp.float32), "ha"
        )
        grad_gain_in = grad_gain_in + jnp.sum(grad_normed * unit_in, axis=0)
        grad_parts.append(
            cot_rows.astype(jnp.float32) + norm_back(grad_normed * ln_in_gain, unit_in, inverse_in)
        )
        local_pair = (grad_proj_part, grad_final_part)
        local_pair = (
            lax.psum_scatter(local_pair[0], ("pb", "ka"), scatter_dimension=0, tiled=True),
            lax.psum_scatter(local_pair[1], ("pb", "ka"), scatter_dimension=1, tiled=True),
        )
        weight_total = (
            local_pair if weight_total is None else jax.tree.map(jnp.add, weight_total, local_pair)
        )
    grad_start = jnp.concatenate(grad_parts, axis=0)
    outgoing = jnp.zeros((owners * capacity, width), jnp.float32).at[slot_index].set(grad_start)
    incoming = lax.all_to_all(
        outgoing.reshape(owners, capacity, width),
        ("pb", "ka"),
        split_axis=0,
        concat_axis=0,
        tiled=True,
    ).reshape(owners * capacity, width)
    table_grad = jax.ops.segment_sum(
        jnp.where(present[:, None], incoming, 0.0), local_rows, num_segments=table.shape[0]
    )
    small_total = lax.psum(
        (grad_gain_in, grad_bias_proj, grad_rel, grad_time, grad_gain_out, grad_bias_out),
        ("pb", "ka"),
    )
    mixed = jnp.concatenate(mixed_parts, axis=0)
    return (
        mixed,
        grad_start.astype(jnp.bfloat16),
        table_grad,
        small_total[0],
        weight_total[0],
        small_total[1],
        small_total[2],
        small_total[3],
        small_total[4],
        weight_total[1],
        small_total[5],
    )


MESH = pl.DeviceIdType.MESH


def remote(src, dst, send_sem, recv_sem, device):
    return pltpu.make_async_remote_copy(
        src_ref=src, dst_ref=dst, send_sem=send_sem, recv_sem=recv_sem, device_id=device, device_id_type=MESH
    )


def mm(a, b):
    return jnp.dot(a, b, preferred_element_type=F32)


def mm_nt(a, b):
    return lax.dot_general(a, b, (((1,), (1,)), ((), ())), preferred_element_type=F32)


def mm_tn(a, b):
    return lax.dot_general(a, b, (((0,), (0,)), ((), ())), preferred_element_type=F32)


def mm_exact(a, b):
    return jnp.dot(a, b, preferred_element_type=F32, precision=lax.Precision.HIGHEST)


def sigmoid(v):
    return 0.5 * jnp.tanh(0.5 * v) + 0.5


def skew(tile):
    return pltpu.roll(tile, 0, 1, stride=1, stride_axis=0)


def iota(shape, dim):
    return lax.broadcasted_iota(jnp.int32, shape, dim)


def one_hot(equal):
    return equal.astype(F32).astype(BF16)


def layer_norm(values):
    centered = values - jnp.mean(values, axis=1, keepdims=True)
    inverse = lax.rsqrt(jnp.mean(centered * centered, axis=1, keepdims=True) + epsilon)
    return centered * inverse, inverse


def layer_norm_back(grad_unit, unit, inverse):
    first = jnp.mean(grad_unit, axis=1, keepdims=True)
    second = jnp.mean(grad_unit * unit, axis=1, keepdims=True)
    return inverse * (grad_unit - first - unit * second)


class Place:
    def __init__(self):
        self.pbs, self.kas = lax.axis_size("pb"), lax.axis_size("ka")
        self.owners, self.zs = self.pbs * self.kas, self.pbs // 2
        self.pb, self.ka, self.ha = lax.axis_index("pb"), lax.axis_index("ka"), lax.axis_index("ha")
        self.z, self.core = self.pb // 2, self.pb % 2
        self.me = self.pb * self.kas + self.ka
        self.stream = 2 * self.ka + self.ha
        self.x_peer = (self.pb, self.ka, 1 - self.ha)
        self.y_peer = (self.pb, 1 - self.ka, self.ha)
        self.xy_peer = (self.pb, 1 - self.ka, 1 - self.ha)
        self.core_peer = (2 * self.z + 1 - self.core, self.ka, self.ha)
        self.quads = [
            (self.xy_peer, 1 - self.ka, 1 - self.ha),
            (self.x_peer, self.ka, 1 - self.ha),
            (self.y_peer, 1 - self.ka, self.ha),
        ]

    def partner(self, k):
        dz, dc, dk = k // 4, k // 2 % 2, k % 2
        z = [self.z, self.z + 1 - 2 * (self.z % 2), (self.z + 2) % 4, 3 - self.z][dz]
        core = 1 - self.core if dc else self.core
        ka = 1 - self.ka if dk else self.ka
        return (2 * z + core) * 2 + ka, (2 * z + core, ka, self.ha)

    def owner_to(self, d):
        index = lax.rem(self.me + d, self.owners)
        return index, (index // self.kas, index % self.kas, self.ha)

    def z_to(self, d):
        return lax.rem(self.z + d, self.zs)

    def z_device(self, d):
        return (2 * self.z_to(d) + self.core, self.ka, self.ha)

    def z_from(self, d):
        return 2 * lax.rem(self.z - d + self.zs, self.zs) + self.core


class Copies:
    def __init__(self, send, recv):
        self.send, self.recv, self.copies = send, recv, []

    def start(self, src, dst, device):
        i = len(self.copies)
        copy = remote(src, dst, self.send.at[i], self.recv.at[i], device)
        copy.start()
        self.copies.append(copy)

    def arrive(self, i):
        self.copies[i].wait_recv()

    def sent(self):
        for copy in self.copies:
            copy.wait_send()


class WeightSum:
    def __init__(self, at, order, s, name):
        self.at, self.order = at, order
        self.own, self.core_in = s[name + "own"], s[name + "core_in"]
        self.mine = [s[f"{name}mine{i}"] for i in range(len(order))]
        self.other = [s[f"{name}other{i}"] for i in range(len(order))]
        self.copies = Copies(s[name + "send"], s[name + "recv"])
        self.begun = [0]

    def pick(self, ref, step, index):
        done = "".join(self.order[: self.order.index(step)])
        left = [a for a in "xzy" if a not in done]
        at_axis = dict(zip(step, index))
        return ref.at[tuple(at_axis.get(a, slice(None)) for a in left)]

    def peers(self, step):
        at = self.at
        if step == "z":
            return [(at.z_device(d), (at.z_to(d),)) for d in range(1, at.zs)]
        if step == "x":
            return [(at.x_peer, (1 - at.ha,))]
        if step == "y":
            return [(at.y_peer, (1 - at.ka,))]
        return [(device, (to_ha, to_ka)) for device, to_ka, to_ha in at.quads]

    def own_index(self, step):
        return tuple({"x": self.at.ha, "y": self.at.ka, "z": self.at.z}[axis] for axis in step)

    def cores(self):
        self.copies.start(self.own.at[:, :, 1 - self.at.core], self.core_in, self.at.core_peer)

    def send(self, i):
        step = self.order[i]
        self.begun.append(len(self.copies.copies))
        for k, (device, index) in enumerate(self.peers(step)):
            self.copies.start(self.pick(self.mine[i], step, index), self.other[i].at[k], device)

    def received(self, i):
        step = self.order[i]
        total = self.pick(self.mine[i], step, self.own_index(step))[...].astype(F32)
        for k in range(len(self.peers(step))):
            self.copies.arrive(self.begun[i + 1] + k)
            total = total + self.other[i][k].astype(F32)
        return total

    def hop(self):
        i = len(self.begun) - 1
        if i == 0:
            self.copies.arrive(0)
            for h in range(2):
                total = self.own[h, :, self.at.core].astype(F32) + self.core_in[h].astype(F32)
                self.mine[0][h] = total.astype(BF16).reshape(self.mine[0].shape[1:])
        else:
            self.mine[i][...] = self.received(i - 1).astype(BF16)
        self.send(i)

    def finish(self):
        return self.received(len(self.order) - 1)


def weight_sum_scratch(name, order, zs, block, cols):
    dma = pltpu.SemaphoreType.DMA
    sizes = {"x": 2, "z": zs, "y": 2}
    found = {
        name + "own": pltpu.VMEM((2, zs, 2, 2 * block, cols), BF16),
        name + "core_in": pltpu.VMEM((2, zs, 2 * block, cols), BF16),
    }
    for i, step in enumerate(order):
        before = [sizes[a] for a in "xzy" if a not in "".join(order[:i])]
        after = [sizes[a] for a in "xzy" if a not in "".join(order[: i + 1])]
        found[f"{name}mine{i}"] = pltpu.VMEM((*before, block, cols), BF16)
        found[f"{name}other{i}"] = pltpu.VMEM(({"xy": 3, "z": zs - 1}.get(step, 1), *after, block, cols), BF16)
    found[name + "send"] = dma((1 + 3 + zs,))
    found[name + "recv"] = dma((1 + 3 + zs,))
    return found


ORDERS = {"a_": ("z", "xy"), "b0_": ("xy", "z"), "b1_": ("xy", "z")}
STEPS = {
    "pair 0": ("a_",),
    "rows sent": (),
    "tables": (),
    "given": ("b0_", "b1_"),
    "take 1": (),
    "take 2": ("b0_", "a_"),
    "take 3": (),
    "take 4": ("b1_",),
    "take 5": (),
}


def main_kernel(in_names, out_names, scratch_names, *refs):
    names = in_names + out_names + scratch_names
    s = dict(zip(names, refs, strict=True))
    s["limit_rows"] = 256
    at = Place()
    owners, zs, ka, ha = at.owners, at.zs, at.ka, at.ha
    count, width = s["context"].shape
    half = width // 2
    tok = count // MB
    group = 2 * tok
    capacity = 2 * count // owners
    block = s["w_uvqk"].shape[0] // 2
    heads_half = half // 64
    heads = 2 * heads_half
    pairs = half // 128
    buckets = s["time"].shape[1]
    gates_cols = 2 * half

    table, table_buf, table_sem = s["table"], s["table_buf"], s["table_sem"]
    chunks = table_sem.shape[0]
    chunk = table.shape[0] // chunks

    def local(i, src, dst):
        copy = pltpu.make_async_copy(src, dst, s["load_sem"].at[i])
        copy.start()
        return copy

    mine = pl.ds(pl.multiple_of(at.stream * tok, tok), tok)
    away = pl.ds(pl.multiple_of((2 * (1 - ka) + ha) * tok, tok), tok)
    loads = {}
    for i, name in enumerate(
        ("owner", "offset", "w_uvqk", "w_out", "b", "rel", "time", "gain_out", "gain_in", "b_out", "lengths", "times")
    ):
        loads[name] = local(i, s[name], s[name + "_v"])
    loads["ctx"] = local(12, s["context"].at[mine], s["ctx_v"].at[ka])
    loads["cot"] = local(13, s["cot"].at[mine], s["cot_v"].at[ka])
    own_cols = pl.ds(pl.multiple_of(ha * half, half), half)

    def table_copy(i):
        rows = pl.ds(pl.multiple_of(i * chunk, chunk), chunk)
        return pltpu.make_async_copy(table.at[rows, own_cols], table_buf.at[rows], table_sem.at[i])

    for i in range(chunks):
        table_copy(i).start()
    barrier = pltpu.get_barrier_semaphore()
    far, near = list(range(owners // 2, owners)), list(range(1, owners // 2))
    partners = [at.partner(k)[1] for k in far + near] + [at.x_peer, at.xy_peer]
    for device in partners:
        pl.semaphore_signal(barrier, inc=1, device_id=device, device_id_type=MESH)

    loads["owner"].wait()
    loads["offset"].wait()
    owner_row, offset_row = s["owner_v"][...], s["offset_v"][...]
    hits = (owner_row == iota((owners, count), 0)).astype(F32)
    earlier = mm(hits.astype(BF16), one_hot(iota((count, count), 0) < iota((count, count), 1)))
    rank = jnp.sum(hits * earlier, axis=0, keepdims=True).astype(jnp.int32)
    rank_hot = one_hot(rank == iota((128, count), 0))
    high = (offset_row // 64).astype(F32)
    low = (offset_row % 64 + 1).astype(F32)
    asked = 64.0 * mm_nt((hits * high).astype(BF16), rank_hot) + mm_nt((hits * low).astype(BF16), rank_hot) - 1.0
    asked = asked.astype(jnp.int32)
    for o in range(owners):
        s["requests"][o] = jnp.broadcast_to(asked[o : o + 1], (8, 128))
    place = owner_row * capacity + rank

    shard, w, small = s["shard"], s["w"], s["small"]
    loads["w_uvqk"].wait()
    for g in range(4):
        shard[:, g * half : (g + 1) * half] = s["w_uvqk_v"][:, g, :]
    loads["w_out"].wait()
    shard[:, 4 * half :] = s["w_out_v"][...]
    w[ha, at.pb] = shard[...]
    for name in ("b", "rel", "time", "gain_out"):
        loads[name].wait()
    small[ha, 0:4] = s["b_v"][...]
    small[ha, 4:8] = s["rel_v"][...]
    for i in range(2):
        for j in range(2):
            small[ha, 8 + i : 9 + i, j * buckets : (j + 1) * buckets] = s["time_v"][2 * i + j : 2 * i + j + 1]
    small[ha, 10:11] = s["gain_out_v"][...]

    pl.semaphore_wait(barrier, len(partners))

    def copies(name):
        return Copies(s[name + "_send"], s[name + "_recv"])

    requests, arrived = s["requests"], s["arrived"]
    req, item, emb_c, row_c, small_c = copies("req"), copies("item"), copies("emb"), copies("row"), copies("small")
    wz, wx, wy, wc = copies("wz"), copies("wx"), copies("wy"), copies("wc")
    for k in far + near:
        to, device = at.partner(k)
        req.start(requests.at[to], arrived.at[at.me], device)
    arrived[at.me] = requests[at.me]
    my_half = pl.ds(pl.multiple_of(ka * block, block), block)
    wz.start(shard.at[my_half], w.at[ha, at.pb, my_half], at.z_device(1))
    wx.start(shard, w.at[ha, at.pb], at.x_peer)
    small_c.start(small.at[ha], small.at[ha], at.x_peer)
    row_c.start(s["context"].at[away], s["ctx_v"].at[ka], at.y_peer)
    row_c.start(s["cot"].at[away], s["cot_v"].at[ka], at.y_peer)
    wc.start(shard, w.at[ha, at.pb], at.core_peer)

    for i in range(owners - 1):
        req.arrive(i)
    for d in range(2, zs):
        wz.start(shard.at[my_half], w.at[ha, at.pb, my_half], at.z_device(d))
    wide_pick = iota((capacity, 128), 1) == iota((capacity, 128), 0)

    def column_of(source):
        tile = jnp.broadcast_to(arrived[source, 0:1], (capacity, 128)).astype(F32)
        return jnp.sum(jnp.where(wide_pick, tile, 0.0), axis=1, keepdims=True)

    fetched, returned, parts, emb = s["fetched"], s["returned"], s["parts"], s["emb"]
    total = s["total"]
    askers = owners // 2

    def look_up(part):
        rounds = [(part * askers + d + 1) % owners for d in range(askers)]
        wanted = [column_of(at.owner_to(d)[0]) for d in rounds]
        column = jnp.concatenate(wanted, axis=0).astype(jnp.int32)
        total[...] = jnp.zeros_like(total)

        def step(i, carry):
            if part == 0:
                table_copy(i).wait()
            rows = pl.ds(pl.multiple_of(i * chunk, chunk), chunk)
            total[...] += mm(one_hot(column == iota((askers * capacity, chunk), 1) + i * chunk), table_buf[rows])
            return carry

        lax.fori_loop(0, chunks, step, 0)
        fetched[part] = total[...].astype(BF16).reshape(fetched.shape[1:])
        for i, d in enumerate(rounds):
            if d:
                item.start(fetched.at[part, i], returned.at[at.me], at.owner_to(d)[1])
            else:
                returned[at.me] = fetched[part, i]

    look_up(0)
    for d in range(1, zs):
        wz.arrive(d - 1)
        there = w.at[ha, at.z_from(d), my_half]
        wx.start(there, there, at.x_peer)
        wy.start(there, there, at.y_peer)
    look_up(1)
    wx.arrive(0)
    there = w.at[1 - ha, at.pb]
    wc.start(there, there, at.core_peer)
    for d in range(1, zs):
        wx.arrive(d)
        there = w.at[1 - ha, at.z_from(d), my_half]
        wy.start(there, there, at.y_peer)

    loads["lengths"].wait()
    loads["times"].wait()
    small_c.arrive(0)
    lane, row = iota((group, group), 1), iota((group, group), 0)
    lengths = s["lengths_v"][pl.ds(at.stream, 1), :]
    ends = jnp.zeros((1, 1), jnp.int32)
    member_row = jnp.zeros((group, group), jnp.int32)
    member_col = jnp.zeros((group, group), jnp.int32)
    inv_count = jnp.zeros((group, group), F32)
    for i in range(SEQ_GRP):
        length = lengths[:, i : i + 1]
        inside = (row >= ends) & (row < ends + length)
        inv_count = jnp.where(inside, 1.0 / jnp.maximum(length, 1).astype(F32), inv_count)
        ends = ends + length
        member_row = member_row + (ends <= row).astype(jnp.int32)
        member_col = member_col + (ends <= lane).astype(jnp.int32)
    allowed = (member_row == member_col) & (member_row < SEQ_GRP) & (lane <= row)
    maskscale = s["maskscale"]
    maskscale[...] = jnp.where(allowed, inv_count, 0.0)
    times_row = jnp.broadcast_to(s["times_v"][pl.ds(at.stream, 1), :], (group, group))
    times_col = jnp.sum(jnp.where(lane == row, times_row, 0).astype(F32), axis=1, keepdims=True).astype(jnp.int32)
    time_index = jnp.clip(times_col - times_row, 0, buckets - 1)
    turn = ((lane + row) % group == 0).astype(F32)
    rel_back = mm_exact(jnp.concatenate([small[0, 4:8, :], small[1, 4:8, :]], axis=0), turn)
    bias = s["bias"]
    for head in range(heads):
        hf, head_in = divmod(head, heads_half)
        begin = (head_in % 2) * buckets
        bucket_row = jnp.broadcast_to(small[hf, 8 + head_in // 2 : 9 + head_in // 2, begin : begin + buckets], (group, buckets))
        by_time = [
            jnp.take_along_axis(bucket_row, time_index[:, c : c + buckets], axis=1, mode="promise_in_bounds")
            for c in range(0, group, buckets)
        ]
        bias[head] = skew(jnp.broadcast_to(rel_back[head : head + 1], (group, group))) + jnp.concatenate(by_time, axis=1)

    for i in range(owners - 1):
        item.arrive(i)
    slot_hot = one_hot(place == iota((2 * count, count), 0))
    parts[...] = mm_tn(slot_hot, returned[...].reshape(2 * count, half)).astype(BF16).reshape(parts.shape)
    for device, to_ka, to_ha in at.quads:
        emb_c.start(parts.at[2 * to_ka + to_ha], emb.at[at.stream], device)
    emb[at.stream] = parts[at.stream]
    for d in range(1, zs):
        wy.arrive(d - 1)
        there = w.at[ha, at.z_from(d)]
        wc.start(there, there, at.core_peer)
    for d in range(1, zs):
        wy.arrive(zs - 2 + d)
        there = w.at[1 - ha, at.z_from(d)]
        wc.start(there, there, at.core_peer)
    slots = 2 * count
    low_lanes = iota((1, 128), 1) < capacity
    ids = []
    for i in range(owners // 2):
        ids.append(jnp.where(low_lanes, arrived[2 * i, 0:1], pltpu.roll(arrived[2 * i + 1, 0:1], capacity, 1)))
    ids_row = jnp.concatenate(ids, axis=1)
    ids_col = jnp.concatenate([column_of(o) for o in range(owners)], axis=0).astype(jnp.int32)
    last = table.shape[0]
    ids_row = jnp.where(ids_row < 0, last, ids_row)
    ids_col = jnp.where(ids_col < 0, last, ids_col)
    keys_row, keys_col = ids_row * slots + iota((1, slots), 1), ids_col * slots + iota((slots, 1), 0)
    order = jnp.sum((keys_col < keys_row).astype(F32), axis=0, keepdims=True).astype(jnp.int32)
    s["turn"][...] = one_hot(order == iota((slots, slots), 0))
    digits = jnp.concatenate([ids_row // 64, ids_row % 64] + [jnp.zeros((1, slots), jnp.int32)] * 6, axis=0)
    found = mm_nt(digits.astype(F32).astype(BF16), s["turn"][...])
    s["sorted_v"][...] = (64.0 * found[0:1] + found[1:2]).astype(jnp.int32)
    limits = iota((slots, 128), 1) * s["limit_rows"]
    s["limits_v"][...] = jnp.sum((ids_col < jnp.minimum(limits, last)).astype(F32), axis=0, keepdims=True).astype(jnp.int32)
    out_copies = [local(14, s["sorted_v"], s["sorted"]), local(15, s["limits_v"], s["limits"])]
    for i in range(2 * zs):
        wc.arrive(i)

    def w_half(hf, cols):
        return w[hf, :, :, cols].reshape(width, cols.stop - cols.start)

    out_cols = slice(4 * half, 5 * half)
    loads["cot"].wait()
    row_c.arrive(1)
    cot = s["cot_v"][...].reshape(group, width)
    grad_mixed = jnp.concatenate([mm(cot, w_half(hf, out_cols)) for hf in range(2)], axis=1)
    loads["gain_in"].wait()
    loads["b_out"].wait()
    loads["ctx"].wait()
    row_c.arrive(0)
    for i in range(3):
        emb_c.arrive(i)

    embedded = jnp.concatenate(
        [jnp.concatenate([emb[2 * i], emb[2 * i + 1]], axis=1).astype(F32) for i in range(2)], axis=0
    )
    start = s["ctx_v"][...].reshape(group, width).astype(F32) + embedded
    unit_in, inv_in = layer_norm(start)
    gain_in = s["gain_in_v"][...]
    normed = (unit_in * gain_in).astype(BF16)
    slope, qkv, w_att, sm = s["slope"], s["qkv"], s["w_att"], s["sm"]
    gates = []
    for hf in range(2):
        for g in range(4):
            cols = slice(g * half, (g + 1) * half)
            pre = mm(normed, w_half(hf, cols)) + small[hf, g : g + 1, :]
            sig = sigmoid(pre)
            act = pre * sig
            slope[hf, :, cols] = sig + act * (1.0 - sig)
            if g == 0:
                gates.append(act)
            else:
                qkv[hf, g - 1] = (act * 0.125 if g == 2 else act).astype(BF16)
    gate = jnp.concatenate(gates, axis=1)
    low_half = iota((group, 128), 1) < 64

    def split(tile):
        zero = jnp.zeros_like(tile)
        return jnp.where(low_half, tile, zero), jnp.where(low_half, zero, tile)

    attended = []
    for hf in range(2):
        for pair in range(pairs):
            cols = slice(pair * 128, (pair + 1) * 128)
            values, queries = split(qkv[hf, 0, :, cols]), split(qkv[hf, 1, :, cols])
            keys = qkv[hf, 2, :, cols]
            both = None
            for sub in range(2):
                head = hf * heads_half + pair * 2 + sub
                scores = mm_nt(queries[sub], keys) + bias[head]
                sig = sigmoid(scores)
                act = scores * sig
                weights = (act * maskscale[...]).astype(BF16)
                w_att[head] = weights
                sm[head] = (sig + act * (1.0 - sig)) * maskscale[...]
                part = mm(weights, values[sub])
                both = part if both is None else both + part
            attended.append(both)
    unit_out, inv_out = layer_norm(jnp.concatenate(attended, axis=1))
    gain_out = jnp.concatenate([small[0, 10:11, :], small[1, 10:11, :]], axis=1)
    mixed_in = (unit_out * gain_out * gate).astype(BF16)
    projected = None
    for hf in range(2):
        part = mm_nt(mixed_in[:, hf * half : (hf + 1) * half], w_half(hf, out_cols))
        projected = part if projected is None else projected + part
    mixed, mixed_rows = s["mixed"], s["mixed_v"]
    mixed[...] = (projected + s["b_out_v"][...] + start).astype(BF16)
    mixed_c = copies("mixed")
    for device, to_ka, to_ha in at.quads:
        here = mixed.at[pl.ds(to_ka * tok, tok), pl.ds(pl.multiple_of(to_ha * half, half), half)]
        mixed_c.start(here, mixed_rows.at[at.stream], device)
    own_rows = pl.ds(pl.multiple_of(ka * tok, tok), tok)
    mixed_rows[at.stream] = mixed[own_rows, pl.ds(pl.multiple_of(ha * half, half), half)]

    grad_pre, grad_small = s["grad_pre"], s["grad_small"]
    grad_raw = grad_mixed * unit_out
    grad_gate = grad_raw * gain_out
    grad_gain_out = jnp.sum(grad_raw * gate, axis=0, keepdims=True)
    grad_att = layer_norm_back(grad_mixed * gate * gain_out, unit_out, inv_out).astype(BF16)
    sum_a = WeightSum(at, ORDERS["a_"], s, "a_")
    sums_b = [WeightSum(at, ORDERS[f"b{i}_"], s, f"b{i}_") for i in range(pairs)]

    hops = {"a_": sum_a} | {f"b{i}_": part for i, part in enumerate(sums_b)}

    def steps_at(point):
        for name in STEPS[point]:
            hops[name].hop()

    def put(own, hf, first, value):
        cols = value.shape[1]
        own[hf, :, :, :, first : first + cols] = value.astype(BF16).reshape(own.shape[1:4] + (cols,))

    for hf in range(2):
        cols = slice(hf * half, (hf + 1) * half)
        grad_pre[hf, :, 0:half] = (grad_gate[:, cols] * slope[hf, :, 0:half]).astype(BF16)
        grad_small[hf, 10:11, :] = grad_gain_out[:, cols]
        put(s["a_own"], hf, 0, mm_tn(normed, grad_pre[hf, :, 0:half]))
        put(s["a_own"], hf, half, mm_tn(cot, mixed_in[:, cols]))
    sum_a.cores()

    gs = s["gs"]
    for pair in range(pairs):
        for hf in range(2):
            cols = slice(pair * 128, (pair + 1) * 128)
            values = qkv[hf, 0, :, cols]
            queries, keys = split(qkv[hf, 1, :, cols]), split(qkv[hf, 2, :, cols])
            grads = split(grad_att[:, hf * half + pair * 128 : hf * half + (pair + 1) * 128])
            sums = None
            for sub in range(2):
                head = hf * heads_half + pair * 2 + sub
                grad_scores = (mm_nt(grads[sub], values) * sm[head]).astype(BF16)
                gs[:, head * group : (head + 1) * group] = grad_scores
                found = (
                    mm_tn(w_att[head], grads[sub]),
                    mm(grad_scores, keys[sub]),
                    mm_tn(grad_scores, queries[sub]),
                )
                sums = found if sums is None else [a + b for a, b in zip(sums, found)]
            for g, part in ((1, sums[0]), (2, sums[1] * 0.125), (3, sums[2])):
                there = slice(g * half + pair * 128, g * half + (pair + 1) * 128)
                grad_pre[hf, :, there] = (part * slope[hf, :, there]).astype(BF16)
        if pair == 0:
            steps_at("pair 0")
    grad_normed = None
    for hf in range(2):
        part = mm_nt(grad_pre[hf], w_half(hf, slice(0, 4 * half)))
        grad_normed = part if grad_normed is None else grad_normed + part
    cot32 = cot.astype(F32)
    grad_start, grad_rows = s["grad_start"], s["grad_rows_v"]
    grad_start[...] = (cot32 + layer_norm_back(grad_normed * gain_in, unit_in, inv_in)).astype(BF16)
    back_c = copies("back")
    for first in (True, False):
        for device, to_ka, to_ha in at.quads:
            h = to_ha if first else 1 - to_ha
            cols = pl.ds(pl.multiple_of(h * half, half), half)
            here = grad_start.at[pl.ds(pl.multiple_of(to_ka * tok, tok), tok), cols]
            back_c.start(here, grad_rows.at[at.stream, :, cols], device)
    grad_rows[at.stream] = grad_start[own_rows]
    for pair in range(pairs):
        for hf in range(2):
            for g in range(1, 4):
                there = slice(g * half + pair * 128, g * half + (pair + 1) * 128)
                put(s[f"b{pair}_own"], hf, (g - 1) * 128, mm_tn(normed, grad_pre[hf, :, there]))
        sums_b[pair].cores()
    steps_at("rows sent")
    gain_grad = jnp.sum(grad_normed * unit_in, axis=0, keepdims=True)
    bout_grad = jnp.sum(cot32, axis=0, keepdims=True)
    for hf in range(2):
        sums = jnp.sum(grad_pre[hf].astype(F32), axis=0, keepdims=True)
        for g in range(4):
            grad_small[hf, g : g + 1, :] = sums[:, g * half : (g + 1) * half]
        grad_small[hf, 11:12, :] = gain_grad[:, hf * half : (hf + 1) * half]
        grad_small[hf, 12:13, :] = bout_grad[:, hf * half : (hf + 1) * half]
        grad_small[hf, 13:16, :] = jnp.zeros((3, half), F32)
    flip = (lane + row == group - 1).astype(F32)
    kept_pairs = lane + row <= group - 1
    hot_cols = one_hot(times_row == row)
    hot_back = one_hot(times_row == group - 1 - row)
    folded = mm(jnp.concatenate([flip.astype(BF16), hot_back], axis=0), gs[...])
    rel_rows, time_rows, early_rows = [], [], []
    for head in range(heads):
        places = slice(head * group, (head + 1) * group)
        rel_rows.append(jnp.sum(skew(folded[:group, places]), axis=0, keepdims=True))
        pairs_sum = mm_nt(folded[group:, places].astype(BF16), hot_cols)
        kept = jnp.where(kept_pairs, pairs_sum, 0.0)
        time_rows.append(jnp.sum(skew(kept), axis=0, keepdims=True))
        early_rows.append(jnp.sum(pairs_sum - kept, axis=0, keepdims=True))
    flipped = mm_exact(jnp.concatenate(rel_rows + time_rows, axis=0), flip)
    early = jnp.sum(jnp.concatenate(early_rows, axis=0), axis=1, keepdims=True)
    late = jnp.sum(flipped[heads:, buckets:], axis=1, keepdims=True)
    place_in = iota((heads, buckets), 1)
    time_grad = flipped[heads:, :buckets] + jnp.where(place_in == 0, early, 0.0) + jnp.where(place_in == buckets - 1, late, 0.0)
    for head in range(heads):
        hf, head_in = divmod(head, heads_half)
        begin = (head_in % 2) * buckets
        grad_small[hf, 4 + head_in : 5 + head_in, :] = flipped[head : head + 1]
        grad_small[hf, 8 + head_in // 2 : 9 + head_in // 2, begin : begin + buckets] = time_grad[head : head + 1]
    small_in, small_mine = s["small_in"], s["small_mine"]
    sum_c = copies("sum")
    sum_c.start(grad_small, small_in.at[0], at.core_peer)

    steps_at("tables")
    for i in range(3):
        back_c.arrive(i)
    outgoing, incoming = s["outgoing"], s["incoming"]
    slot_hot = one_hot(place == iota((2 * count, count), 0))
    outgoing[...] = mm(slot_hot, grad_rows[:, :, own_cols].reshape(count, half)).astype(BF16).reshape(outgoing.shape)
    give, hand = copies("give"), copies("hand")
    given = {}

    def start_give(*rounds):
        for k in rounds:
            to, device = at.partner(k)
            given[k] = len(give.copies)
            give.start(outgoing.at[to], incoming.at[ha, at.me], device)

    start_give(8, 9, 10, 11, 1, 2, 3, 4, 5, 6, 7)
    incoming[ha, at.me] = outgoing[at.me]
    hand.start(incoming.at[ha, at.me], incoming.at[ha, at.me], at.x_peer)

    def take(*rounds):
        for k in rounds:
            give.arrive(given[k])
            there = incoming.at[ha, at.partner(k)[0]]
            hand.start(there, there, at.x_peer)

    steps_at("given")
    take(1, 2, 3)
    sum_c.arrive(0)
    small_mine[0] = grad_small[...] + small_in[0]
    for i, (device, _, _) in enumerate(at.quads):
        sum_c.start(small_mine.at[0], small_in.at[1 + i], device)
    steps_at("take 1")
    take(8, 9)
    start_give(12, 13)
    steps_at("take 2")
    take(4, 5, 6, 7)
    steps_at("take 3")
    take(10, 11)
    start_give(14, 15)
    summed = small_mine[0]
    for i in range(1, 4):
        sum_c.arrive(i)
        summed = summed + small_in[i]
    small_mine[1] = summed
    for d in range(1, zs):
        sum_c.start(small_mine.at[1], small_in.at[3 + d], at.z_device(d))
    steps_at("take 4")
    take(12, 13)
    steps_at("take 5")
    take(14, 15)
    def in_order(h):
        cols = pl.ds(pl.multiple_of(h * half, half), half)
        s["rows_v"][:, cols] = mm(s["turn"][...], incoming[h].reshape(slots, half)).astype(BF16)

    in_order(ha)
    for i in range(3, 6):
        back_c.arrive(i)
    out_copies.append(local(16, grad_rows, s["grad_rows"]))
    for i in range(3):
        mixed_c.arrive(i)
    out_copies.append(local(17, mixed_rows, s["mixed_rows"]))
    grad_w = s["grad_w_v"]
    grad_w[:, 0:gates_cols] = sum_a.finish()
    for i in range(pairs):
        first = gates_cols + i * 384
        grad_w[:, first : first + 384] = sums_b[i].finish()
    summed = small_mine[1]
    for d in range(1, zs):
        sum_c.arrive(3 + d)
        summed = summed + small_in[3 + d]
    s["small_v"][...] = summed
    out_copies += [local(18, grad_w, s["grad_w"]), local(19, s["small_v"], s["small_sum"])]
    for i in range(owners):
        hand.arrive(i)
    cols = pl.ds(pl.multiple_of((1 - ha) * half, half), half)
    handed = incoming[1 - ha].reshape(slots, half)
    for i in range(slots // 256):
        rows = pl.ds(i * 256, 256)
        s["rows_v"][rows, cols] = mm(s["turn"][rows, :], handed).astype(BF16)
        out_copies.append(local(20 + i, s["rows_v"].at[rows], s["rows"].at[rows]))
    for copy in out_copies:
        copy.wait()
    for kind in (req, item, emb_c, row_c, small_c, wz, wx, wy, wc, mixed_c, back_c, give, hand, sum_c):
        kind.sent()
    for part in [sum_a] + sums_b:
        part.copies.sent()


def run_main(inputs):
    pbs, kas = lax.axis_size("pb"), lax.axis_size("ka")
    owners, zs = pbs * kas, pbs // 2
    count, width = inputs["context"].shape
    half, tok, capacity = width // 2, count // MB, 2 * count // owners
    group, heads = 2 * tok, width // 64
    shard_rows = inputs["w_uvqk"].shape[0]
    block = shard_rows // 2
    dma = pltpu.SemaphoreType.DMA
    outs = {
        "rows": jax.ShapeDtypeStruct((2 * count, width), BF16),
        "sorted": jax.ShapeDtypeStruct((1, 2 * count), jnp.int32),
        "limits": jax.ShapeDtypeStruct((1, 128), jnp.int32),
        "grad_rows": jax.ShapeDtypeStruct((MB, tok, width), BF16),
        "mixed_rows": jax.ShapeDtypeStruct((MB, tok, half), BF16),
        "grad_w": jax.ShapeDtypeStruct((block, 5 * half), F32),
        "small_sum": jax.ShapeDtypeStruct((2, 16, half), F32),
    }
    scratch = {
        "ctx_v": pltpu.VMEM((2, tok, width), BF16),
        "cot_v": pltpu.VMEM((2, tok, width), BF16),
        "requests": pltpu.VMEM((owners, 8, 128), jnp.int32),
        "arrived": pltpu.VMEM((owners, 8, 128), jnp.int32),
        "table_buf": pltpu.VMEM((inputs["table"].shape[0], half), BF16),
        "total": pltpu.VMEM((count, half), F32),
        "fetched": pltpu.VMEM((2, owners // 2, capacity, half), BF16),
        "returned": pltpu.VMEM((owners, capacity, half), BF16),
        "parts": pltpu.VMEM((MB, tok, half), BF16),
        "emb": pltpu.VMEM((MB, tok, half), BF16),
        "shard": pltpu.VMEM((shard_rows, 5 * half), BF16),
        "w": pltpu.VMEM((2, pbs, shard_rows, 5 * half), BF16),
        "small": pltpu.VMEM((2, 16, half), F32),
        "maskscale": pltpu.VMEM((group, group), F32),
        "bias": pltpu.VMEM((heads, group, group), F32),
        "slope": pltpu.VMEM((2, group, 4 * half), F32),
        "qkv": pltpu.VMEM((2, 3, group, half), BF16),
        "w_att": pltpu.VMEM((heads, group, group), BF16),
        "sm": pltpu.VMEM((heads, group, group), F32),
        "gs": pltpu.VMEM((group, heads * group), BF16),
        "grad_pre": pltpu.VMEM((2, group, 4 * half), BF16),
        "mixed": pltpu.VMEM((group, width), BF16),
        "grad_start": pltpu.VMEM((group, width), BF16),
        "grad_small": pltpu.VMEM((2, 16, half), F32),
        "outgoing": pltpu.VMEM((owners, capacity, half), BF16),
        "small_mine": pltpu.VMEM((2, 2, 16, half), F32),
        "small_in": pltpu.VMEM((3 + zs, 2, 16, half), F32),
        "incoming": pltpu.VMEM((2, owners, capacity, half), BF16),
        "rows_v": pltpu.VMEM((2 * count, width), BF16),
        "turn": pltpu.VMEM((2 * count, 2 * count), BF16),
        "sorted_v": pltpu.VMEM((1, 2 * count), jnp.int32),
        "limits_v": pltpu.VMEM((1, 128), jnp.int32),
        "grad_rows_v": pltpu.VMEM((MB, tok, width), BF16),
        "mixed_v": pltpu.VMEM((MB, tok, half), BF16),
        "grad_w_v": pltpu.VMEM((block, 5 * half), F32),
        "small_v": pltpu.VMEM((2, 16, half), F32),
        "load_sem": dma((20 + 2 * count // 256,)),
        "table_sem": dma((4,)),
    }
    for name in ("owner", "offset", "w_uvqk", "w_out", "b", "rel", "time", "gain_out", "gain_in", "b_out", "lengths", "times"):
        scratch[name + "_v"] = pltpu.VMEM(inputs[name].shape, inputs[name].dtype)
    for name, number in (
        ("req", owners - 1), ("item", owners - 1), ("emb", 3), ("row", 2), ("small", 1), ("wz", zs - 1), ("wx", zs),
        ("wy", 2 * zs - 2), ("wc", 2 * zs), ("mixed", 3), ("back", 6), ("give", owners - 1), ("hand", owners), ("sum", 3 + zs),
    ):
        scratch[name + "_send"] = dma((number,))
        scratch[name + "_recv"] = dma((number,))
    scratch |= weight_sum_scratch("a_", ORDERS["a_"], zs, block, 2 * half)
    for i in range(half // 128):
        scratch |= weight_sum_scratch(f"b{i}_", ORDERS[f"b{i}_"], zs, block, 384)
    hbm = pl.BlockSpec(memory_space=pltpu.HBM)
    found = pl.pallas_call(
        functools.partial(main_kernel, tuple(inputs), tuple(outs), tuple(scratch)),
        out_shape=tuple(outs.values()),
        in_specs=[hbm] * len(inputs),
        out_specs=(hbm,) * len(outs),
        scratch_shapes=list(scratch.values()),
        compiler_params=pltpu.CompilerParams(
            collective_id=1, has_side_effects=True, vmem_limit_bytes=58 * 1024 * 1024
        ),
    )(*inputs.values())
    return dict(zip(outs, found, strict=True))


def scatter_kernel(
    limits_in, sorted_in, rows_in, grad_w_in, small_in, mixed_in, grad_rows_in,
    out_ref, w_ref, w_out_ref, b_ref, rel_ref, time_ref, gain_in_ref, gain_out_ref, b_out_ref, mixed_out, grad_rows_out,
    limits, ids, rows, grad_w_ref, small_ref, mixed, grad_rows, tiles, load_sem, row_sem, tile_sem, pass_sem,
):
    pairs_in = [
        (limits_in, limits), (sorted_in, ids), (grad_w_in, grad_w_ref), (small_in, small_ref),
        (mixed_in, mixed), (grad_rows_in, grad_rows),
    ]
    depth = 256

    def load_rows(j):
        here = pl.ds(j * depth, depth)
        return pltpu.make_async_copy(rows_in.at[here], rows.at[here], row_sem.at[j])

    blocks = rows.shape[0] // depth
    loads = [pltpu.make_async_copy(src, dst, load_sem.at[i]) for i, (src, dst) in enumerate(pairs_in)]
    for load in loads[:2]:
        load.start()
    for j in range(blocks):
        load_rows(j).start()
    for load in loads[2:]:
        load.start()
    for load in loads[:2]:
        load.wait()
    load_rows(0).wait()
    slots, tile = tiles.shape[0], tiles.shape[1]
    count = out_ref.shape[0] // tile
    per_tile = tile // 256

    def write(i, slot):
        there = pl.ds(pl.multiple_of(i * tile, tile), tile)
        return pltpu.make_async_copy(tiles.at[slot], out_ref.at[there], tile_sem.at[slot])

    def step(i, carry):
        slot = lax.rem(i, slots)

        @pl.when(i >= slots)
        def _():
            write(i - slots, slot).wait()

        first = limits[0, i * per_tile] // depth
        end = (limits[0, (i + 1) * per_tile] + depth - 1) // depth

        def product(j):
            here = pl.ds(pl.multiple_of(j * depth, depth), depth)
            return mm(one_hot(ids[:, here] == iota((tile, depth), 0) + i * tile), rows[here, :])

        tiles[slot] = product(jnp.minimum(first, rows.shape[0] // depth - 1))

        def more(j, carry):
            tiles[slot] += product(j)
            return carry

        lax.fori_loop(first + 1, end, more, 0)
        write(i, slot).start()
        return carry

    crowded = limits[0, per_tile] > depth

    def other_rows():
        for j in range(1, blocks):
            load_rows(j).wait()

    pl.when(crowded)(other_rows)
    step(0, 0)
    pl.when(jnp.logical_not(crowded))(other_rows)
    lax.fori_loop(1, 3, step, 0)
    for load in loads[2:]:
        load.wait()
    passed = [
        pltpu.make_async_copy(mixed, mixed_out, pass_sem.at[0]),
        pltpu.make_async_copy(grad_rows, grad_rows_out, pass_sem.at[1]),
    ]
    for copy in passed:
        copy.start()
    lax.fori_loop(3, count, step, 0)
    half = w_ref.shape[2]
    buckets = time_ref.shape[1]
    w_ref[:, 0, :] = grad_w_ref[:, 0:half]
    w_out_ref[...] = grad_w_ref[:, half : 2 * half]
    for pair in range(half // 128):
        for g in range(1, 4):
            first = 2 * half + pair * 384 + (g - 1) * 128
            w_ref[:, g, pair * 128 : (pair + 1) * 128] = grad_w_ref[:, first : first + 128]
    ha = lax.axis_index("ha")
    b_ref[...] = small_ref[ha, 0:4, :]
    rel_ref[...] = small_ref[ha, 4:8, :]
    for i in range(2):
        for j in range(2):
            time_ref[2 * i + j : 2 * i + j + 1, :] = small_ref[ha, 8 + i : 9 + i, j * buckets : (j + 1) * buckets]
    gain_out_ref[...] = small_ref[ha, 10:11, :]
    for hf in range(2):
        gain_in_ref[:, hf * half : (hf + 1) * half] = small_ref[hf, 11:12, :]
        b_out_ref[:, hf * half : (hf + 1) * half] = small_ref[hf, 12:13, :]
    for k in range(slots):
        write(count - slots + k, (count - slots + k) % slots).wait()
    for copy in passed:
        copy.wait()


def scatter_rows(found, table_rows, buckets, tile=512, slots=4):
    rows, grad_w = found["rows"], found["grad_w"]
    width = rows.shape[1]
    half, block = width // 2, grad_w.shape[0]
    names = ("limits", "sorted", "rows", "grad_w", "small_sum", "mixed_rows", "grad_rows")
    shapes = [(block, 4, half), (block, half), (4, half), (4, half), (4, buckets), (1, width), (1, half), (1, width)]
    hbm, vmem = pl.BlockSpec(memory_space=pltpu.HBM), pl.BlockSpec(memory_space=pltpu.VMEM)
    outs = [jax.ShapeDtypeStruct(shape, F32) for shape in [(table_rows, width)] + shapes]
    outs += [jax.ShapeDtypeStruct(found[name].shape, BF16) for name in ("mixed_rows", "grad_rows")]
    return pl.pallas_call(
        scatter_kernel,
        out_shape=outs,
        in_specs=[hbm] * len(names),
        out_specs=[hbm] + [vmem] * len(shapes) + [hbm] * 2,
        scratch_shapes=[
            pltpu.SMEM(found["limits"].shape, jnp.int32),
            pltpu.VMEM(found["sorted"].shape, jnp.int32),
            pltpu.VMEM(rows.shape, BF16),
            pltpu.VMEM(grad_w.shape, F32),
            pltpu.VMEM(found["small_sum"].shape, F32),
            pltpu.VMEM(found["mixed_rows"].shape, BF16),
            pltpu.VMEM(found["grad_rows"].shape, BF16),
            pltpu.VMEM((slots, tile, width), F32),
            pltpu.SemaphoreType.DMA((len(names),)),
            pltpu.SemaphoreType.DMA((rows.shape[0] // 256,)),
            pltpu.SemaphoreType.DMA((slots,)),
            pltpu.SemaphoreType.DMA((2,)),
        ],
        compiler_params=pltpu.CompilerParams(vmem_limit_bytes=58 * 1024 * 1024),
    )(*(found[name] for name in names))


def local_streams(
    context,
    item_owner,
    item_offset,
    lengths,
    times,
    table,
    cotangent,
    ln_in_gain,
    w_uvqk,
    b_uvqk,
    rel_bias,
    time_bias,
    ln_out_gain,
    w_out,
    b_out,
):
    row_count, width = context.shape
    half = width // 2
    found = run_main(
        {
            "owner": item_owner.reshape(1, row_count),
            "offset": item_offset.reshape(1, row_count),
            "context": context,
            "cot": cotangent,
            "table": table,
            "w_uvqk": w_uvqk,
            "w_out": w_out.T,
            "b": b_uvqk,
            "rel": rel_bias,
            "time": time_bias,
            "gain_out": ln_out_gain.reshape(1, half),
            "gain_in": ln_in_gain.reshape(1, width),
            "b_out": b_out.reshape(1, width),
            "lengths": lengths[0],
            "times": times[0],
        }
    )
    (
        table_grad, grad_w, grad_w_out, grad_b, grad_rel, grad_time, grad_gain_in, grad_gain_out, grad_b_out, mixed, grad_rows,
    ) = scatter_rows(found, table.shape[0], time_bias.shape[1])
    return (
        mixed.reshape(row_count, half),
        grad_rows.reshape(row_count, width),
        table_grad,
        grad_gain_in.reshape(width),
        grad_w,
        grad_b,
        grad_rel,
        grad_time,
        grad_gain_out.reshape(half),
        grad_w_out.T,
        grad_b_out.reshape(width),
    )


def solution(mesh):
    one_stream = mesh.shape["ka"] * mesh.shape["ha"] == MB and mesh.shape["ka"] == 2 and mesh.shape["pb"] == 8
    return jax.shard_map(
        local_streams if one_stream else local_general,
        mesh=mesh,
        in_specs=(
            P(("pb", "ka"), None),
            P(("pb", "ka"), None),
            P(("pb", "ka")),
            P("pb", None, None),
            P("pb", None, None),
            P(("pb", "ka"), None),
            P(("pb", "ka"), None),
            P(),
            P("pb", None, "ha"),
            P(None, "ha"),
            P("ha", None),
            P("ha", None),
            P("ha"),
            P("ha", "pb"),
            P(),
        ),
        out_specs=(
            P(("pb", "ka"), "ha"),
            P(("pb", "ka"), None),
            P(("pb", "ka"), None),
            P(),
            P(("pb", "ka"), None, "ha"),
            P(None, "ha"),
            P("ha", None),
            P("ha", None),
            P("ha"),
            P("ha", ("pb", "ka")),
            P(),
        ),
        check_vma=False,
    )
```

```python
import functools

import jax
import jax.numpy as jnp
from jax import lax
from jax.experimental import pallas as pl
from jax.experimental.pallas import tpu as pltpu
from jax.sharding import PartitionSpec as P

DH = 64
TOK_DEV = 128
MB = 4
SEQ_GRP = 4
F32 = jnp.float32
BF16 = jnp.bfloat16


epsilon = 1e-05


def silu_slope(values):
    sigma = jax.nn.sigmoid(values)
    return sigma * (1.0 + values * (1.0 - sigma))


def norm_rows(values, gain):
    centered = values - jnp.mean(values, axis=-1, keepdims=True)
    inverse = lax.rsqrt(jnp.mean(centered * centered, axis=-1, keepdims=True) + epsilon)
    unit_rows = centered * inverse
    return (unit_rows * gain, unit_rows, inverse)


def norm_back(grad_unit, unit_rows, inverse):
    first_mean = jnp.mean(grad_unit, axis=-1, keepdims=True)
    second_mean = jnp.mean(grad_unit * unit_rows, axis=-1, keepdims=True)
    return inverse * (grad_unit - first_mean - unit_rows * second_mean)


def stream_layout(lengths_row, group):
    places = jnp.arange(group, dtype=jnp.int32)
    ends = jnp.cumsum(lengths_row, dtype=jnp.int32)
    member = jnp.sum((ends[None, :] <= places[:, None]).astype(jnp.int32), axis=1)
    onehot = (member[:, None] == jnp.arange(SEQ_GRP, dtype=jnp.int32)[None, :]).astype(jnp.float32)
    counted = jnp.maximum(jnp.sum(onehot * lengths_row.astype(jnp.float32)[None, :], axis=1), 1.0)
    return (places, member, counted)


def diagonal_bias(rel_bias, query_first, key_first, query_len, key_len):
    heads, group = rel_bias.shape
    span = query_len + key_len - 1
    padded = jnp.concatenate([jnp.zeros((heads, group), jnp.float32), rel_bias], axis=1)
    window = lax.dynamic_slice_in_dim(
        padded, query_first - key_first - key_len + 1 + group, span, 1
    )
    flipped = jnp.concatenate([window[:, ::-1], jnp.zeros((heads, 1), jnp.float32)], axis=1)
    skewed = jnp.tile(flipped, (1, query_len))[:, : query_len * span].reshape(
        heads, query_len, span
    )
    return skewed[:, :, query_len - 1 : query_len - 1 + key_len]


def diagonal_sums(grad_scores, query_first, key_first, group):
    heads, query_len, key_len = grad_scores.shape
    span = query_len + key_len - 1
    widened = jnp.pad(grad_scores.astype(jnp.float32), ((0, 0), (0, 0), (query_len - 1, 0)))
    flat = jnp.pad(widened.reshape(heads, query_len * span), ((0, 0), (0, query_len)))
    totals = jnp.sum(flat.reshape(heads, query_len, span + 1), axis=1)
    window = totals[:, :span][:, ::-1]
    placed = lax.dynamic_update_slice_in_dim(
        jnp.zeros((heads, 2 * group), jnp.float32),
        window,
        query_first - key_first - key_len + 1 + group,
        1,
    )
    return placed[:, group:]


def bucket_lookup(time_bias, bucket_hot):
    high = time_bias.astype(jnp.bfloat16)
    rest = time_bias - high.astype(jnp.float32)
    middle = rest.astype(jnp.bfloat16)
    lowest = (rest - middle.astype(jnp.float32)).astype(jnp.bfloat16)
    pieces = jnp.einsum(
        "phb,qkb->phqk",
        jnp.stack([high, middle, lowest]),
        bucket_hot,
        preferred_element_type=jnp.float32,
    )
    return pieces[0] + pieces[1] + pieces[2]


def tile_scores(query_heads, key_heads, query_info, key_info, rel_bias, time_bias):
    query_pos, query_member, query_count, query_stamp = query_info
    key_pos, key_member, key_stamp = key_info
    distance = query_pos[:, None] - key_pos[None, :]
    time_index = jnp.clip(query_stamp[:, None] - key_stamp[None, :], 0, time_bias.shape[1] - 1)
    bucket_hot = (
        time_index[:, :, None] == jnp.arange(time_bias.shape[1], dtype=jnp.int32)[None, None, :]
    ).astype(jnp.bfloat16)
    scores = jnp.einsum(
        "qhd,khd->hqk", query_heads, key_heads, preferred_element_type=jnp.float32
    ) * DH ** (-0.5)
    scores = (
        scores
        + diagonal_bias(rel_bias, query_pos[0], key_pos[0], query_pos.shape[0], key_pos.shape[0])
        + bucket_lookup(time_bias, bucket_hot)
    )
    allowed = (
        (query_member[:, None] == key_member[None, :])
        & (query_member[:, None] < SEQ_GRP)
        & (distance >= 0)
    )[None]
    weights = (jnp.where(allowed, jax.nn.silu(scores), 0.0) / query_count[None, :, None]).astype(
        jnp.bfloat16
    )
    return (scores, allowed, weights, bucket_hot)


def score_grads(grad_weights, scores, allowed, query_count):
    return (
        jnp.where(allowed, grad_weights / query_count[None, :, None], 0.0) * silu_slope(scores)
    ).astype(jnp.bfloat16)


def local_general(
    context,
    item_owner,
    item_offset,
    lengths,
    times,
    table,
    cotangent,
    ln_in_gain,
    w_uvqk,
    b_uvqk,
    rel_bias,
    time_bias,
    ln_out_gain,
    w_out,
    b_out,
):
    owners = lax.axis_size(("pb", "ka"))
    row_count = context.shape[0]
    width = context.shape[1]
    capacity = max(2, 2 * row_count // owners)
    owner_ids = item_owner[:, 0]
    owner_hits = (owner_ids[:, None] == jnp.arange(owners, dtype=jnp.int32)[None, :]).astype(
        jnp.int32
    )
    earlier = jnp.sum((jnp.cumsum(owner_hits, axis=0) - owner_hits) * owner_hits, axis=1)
    slot_index = owner_ids * capacity + earlier
    requests = jnp.zeros((owners * capacity,), jnp.int32).at[slot_index].set(item_offset + 1)
    arrived = lax.all_to_all(
        requests.reshape(owners, capacity), ("pb", "ka"), split_axis=0, concat_axis=0, tiled=True
    ).reshape(-1)
    present = arrived > 0
    local_rows = jnp.maximum(arrived - 1, 0)
    fetched = jnp.where(present[:, None], table[local_rows], jnp.zeros((), jnp.bfloat16))
    returned = lax.all_to_all(
        fetched.reshape(owners, capacity, width),
        ("pb", "ka"),
        split_axis=0,
        concat_axis=0,
        tiled=True,
    )
    embedded = returned.reshape(owners * capacity, width)[slot_index]
    start = context.astype(jnp.float32) + embedded.astype(jnp.float32)
    group = lax.axis_size("ka") * TOK_DEV
    block_start = lax.axis_index("ka") * TOK_DEV
    half_cols = w_out.shape[0]
    heads = half_cols // DH
    full_cols = half_cols * lax.axis_size("ha")
    out_cols = width // lax.axis_size("ha")
    out_start = lax.axis_index("ha") * out_cols
    bias_half = lax.dynamic_slice_in_dim(b_out, out_start, out_cols)
    scale = DH ** (-0.5)
    grad_gain_in = jnp.zeros(ln_in_gain.shape, jnp.float32)
    grad_bias_proj = jnp.zeros(b_uvqk.shape, jnp.float32)
    grad_rel = jnp.zeros(rel_bias.shape, jnp.float32)
    grad_time = jnp.zeros(time_bias.shape, jnp.float32)
    grad_gain_out = jnp.zeros(ln_out_gain.shape, jnp.float32)
    grad_bias_out = jnp.zeros(b_out.shape, jnp.float32)
    weight_total = None
    mixed_parts = []
    grad_parts = []
    for micro in range(MB):
        w_full, w_final = (
            lax.all_gather(w_uvqk, "pb", axis=0, tiled=True),
            lax.all_gather(w_out, "pb", axis=1, tiled=True),
        )
        x_in = start[micro * TOK_DEV : (micro + 1) * TOK_DEV]
        cot_rows = cotangent[micro * TOK_DEV : (micro + 1) * TOK_DEV]
        stamps = times[0, micro]
        places, member, counted = stream_layout(lengths[0, micro], group)
        query_pos = lax.dynamic_slice_in_dim(places, block_start, TOK_DEV)
        query_member = lax.dynamic_slice_in_dim(member, block_start, TOK_DEV)
        query_count = lax.dynamic_slice_in_dim(counted, block_start, TOK_DEV)
        query_stamp = lax.dynamic_slice_in_dim(stamps, block_start, TOK_DEV)
        normed_float, unit_in, inverse_in = norm_rows(x_in, ln_in_gain)
        normed = normed_float.astype(jnp.bfloat16)
        pre_act = (
            jnp.einsum("td,dgc->tgc", normed, w_full, preferred_element_type=jnp.float32) + b_uvqk
        )
        activated = jax.nn.silu(pre_act)
        gate_part = activated[:, 0]
        values = activated[:, 1].astype(jnp.bfloat16)
        queries = activated[:, 2].astype(jnp.bfloat16)
        key_rows = activated[:, 3].astype(jnp.bfloat16)
        key_pair = lax.all_gather(jnp.stack([key_rows, values]), "ka", axis=1, tiled=True)
        all_keys = key_pair[0].reshape(group, heads, DH)
        all_values = key_pair[1].reshape(group, heads, DH)
        query_heads = queries.reshape(TOK_DEV, heads, DH)
        scores, allowed, weights, bucket_hot = tile_scores(
            query_heads,
            all_keys,
            (query_pos, query_member, query_count, query_stamp),
            (places, member, stamps),
            rel_bias,
            time_bias,
        )
        attended = jnp.einsum(
            "hqk,khd->qhd", weights, all_values, preferred_element_type=jnp.float32
        ).reshape(TOK_DEV, half_cols)
        row_total, row_square = lax.psum(
            (jnp.sum(attended, axis=1), jnp.sum(attended * attended, axis=1)), "ha"
        )
        row_mean = row_total / full_cols
        inverse_out = lax.rsqrt(row_square / full_cols - row_mean * row_mean + epsilon)[:, None]
        unit_out = (attended - row_mean[:, None]) * inverse_out
        mixed_in = (unit_out * ln_out_gain * gate_part).astype(jnp.bfloat16)
        partial_out = jnp.dot(mixed_in, w_final, preferred_element_type=jnp.float32)
        summed_out = lax.psum_scatter(partial_out, "ha", scatter_dimension=1, tiled=True)
        residual = lax.dynamic_slice_in_dim(x_in, out_start, out_cols, 1)
        mixed_parts.append((summed_out + bias_half + residual).astype(jnp.bfloat16))
        grad_final_part = jnp.einsum(
            "tc,td->cd", mixed_in, cot_rows, preferred_element_type=jnp.float32
        )
        grad_bias_out = grad_bias_out + jnp.sum(cot_rows.astype(jnp.float32), axis=0)
        grad_mixed = jnp.einsum("td,cd->tc", cot_rows, w_final, preferred_element_type=jnp.float32)
        grad_gate = grad_mixed * unit_out * ln_out_gain
        grad_gain_out = grad_gain_out + jnp.sum(grad_mixed * unit_out * gate_part, axis=0)
        grad_unit = grad_mixed * gate_part * ln_out_gain
        first_total, second_total = lax.psum(
            (jnp.sum(grad_unit, axis=1), jnp.sum(grad_unit * unit_out, axis=1)), "ha"
        )
        grad_attended = (
            inverse_out
            * (
                grad_unit
                - first_total[:, None] / full_cols
                - unit_out * second_total[:, None] / full_cols
            )
        ).astype(jnp.bfloat16)
        grad_heads = grad_attended.reshape(TOK_DEV, heads, DH)
        grad_weights = jnp.einsum(
            "qhd,khd->hqk", grad_heads, all_values, preferred_element_type=jnp.float32
        )
        grad_scores = score_grads(grad_weights, scores, allowed, query_count)
        grad_rel = grad_rel + diagonal_sums(grad_scores, query_pos[0], places[0], rel_bias.shape[1])
        grad_time = grad_time + jnp.einsum(
            "hqk,qkb->hb", grad_scores, bucket_hot, preferred_element_type=jnp.float32
        )
        grad_queries = (
            jnp.einsum("hqk,khd->qhd", grad_scores, all_keys, preferred_element_type=jnp.float32)
            * scale
        ).reshape(TOK_DEV, half_cols)
        key_part = (
            jnp.einsum("hqk,qhd->khd", grad_scores, query_heads, preferred_element_type=jnp.float32)
            * scale
        )
        value_part = jnp.einsum(
            "hqk,qhd->khd", weights, grad_heads, preferred_element_type=jnp.float32
        )
        stacked = jnp.stack(
            [key_part.reshape(group, half_cols), value_part.reshape(group, half_cols)]
        )
        owned_grads = lax.psum_scatter(stacked, "ka", scatter_dimension=1, tiled=True)
        grad_keys = owned_grads[0]
        grad_values = owned_grads[1]
        grad_act = jnp.stack([grad_gate, grad_values, grad_queries, grad_keys], axis=1)
        grad_pre = (grad_act * silu_slope(pre_act)).astype(jnp.bfloat16)
        grad_proj_part = jnp.einsum(
            "td,tgc->dgc", normed, grad_pre, preferred_element_type=jnp.float32
        )
        grad_bias_proj = grad_bias_proj + jnp.sum(grad_pre.astype(jnp.float32), axis=0)
        grad_normed = lax.psum(
            jnp.einsum("tgc,dgc->td", grad_pre, w_full, preferred_element_type=jnp.float32), "ha"
        )
        grad_gain_in = grad_gain_in + jnp.sum(grad_normed * unit_in, axis=0)
        grad_parts.append(
            cot_rows.astype(jnp.float32) + norm_back(grad_normed * ln_in_gain, unit_in, inverse_in)
        )
        local_pair = (grad_proj_part, grad_final_part)
        local_pair = (
            lax.psum_scatter(local_pair[0], ("pb", "ka"), scatter_dimension=0, tiled=True),
            lax.psum_scatter(local_pair[1], ("pb", "ka"), scatter_dimension=1, tiled=True),
        )
        weight_total = (
            local_pair if weight_total is None else jax.tree.map(jnp.add, weight_total, local_pair)
        )
    grad_start = jnp.concatenate(grad_parts, axis=0)
    outgoing = jnp.zeros((owners * capacity, width), jnp.float32).at[slot_index].set(grad_start)
    incoming = lax.all_to_all(
        outgoing.reshape(owners, capacity, width),
        ("pb", "ka"),
        split_axis=0,
        concat_axis=0,
        tiled=True,
    ).reshape(owners * capacity, width)
    table_grad = jax.ops.segment_sum(
        jnp.where(present[:, None], incoming, 0.0), local_rows, num_segments=table.shape[0]
    )
    small_total = lax.psum(
        (grad_gain_in, grad_bias_proj, grad_rel, grad_time, grad_gain_out, grad_bias_out),
        ("pb", "ka"),
    )
    mixed = jnp.concatenate(mixed_parts, axis=0)
    return (
        mixed,
        grad_start.astype(jnp.bfloat16),
        table_grad,
        small_total[0],
        weight_total[0],
        small_total[1],
        small_total[2],
        small_total[3],
        small_total[4],
        weight_total[1],
        small_total[5],
    )


MESH = pl.DeviceIdType.MESH


def remote(src, dst, send_sem, recv_sem, device):
    return pltpu.make_async_remote_copy(
        src_ref=src, dst_ref=dst, send_sem=send_sem, recv_sem=recv_sem, device_id=device, device_id_type=MESH
    )


def mm(a, b):
    return jnp.dot(a, b, preferred_element_type=F32)


def mm_nt(a, b):
    return lax.dot_general(a, b, (((1,), (1,)), ((), ())), preferred_element_type=F32)


def mm_tn(a, b):
    return lax.dot_general(a, b, (((0,), (0,)), ((), ())), preferred_element_type=F32)


def mm_exact(a, b):
    return jnp.dot(a, b, preferred_element_type=F32, precision=lax.Precision.HIGHEST)


def sigmoid(v):
    return 0.5 * jnp.tanh(0.5 * v) + 0.5


def skew(tile):
    return pltpu.roll(tile, 0, 1, stride=1, stride_axis=0)


def iota(shape, dim):
    return lax.broadcasted_iota(jnp.int32, shape, dim)


def one_hot(equal):
    return equal.astype(F32).astype(BF16)


def layer_norm(values):
    centered = values - jnp.mean(values, axis=1, keepdims=True)
    inverse = lax.rsqrt(jnp.mean(centered * centered, axis=1, keepdims=True) + epsilon)
    return centered * inverse, inverse


def layer_norm_back(grad_unit, unit, inverse):
    first = jnp.mean(grad_unit, axis=1, keepdims=True)
    second = jnp.mean(grad_unit * unit, axis=1, keepdims=True)
    return inverse * (grad_unit - first - unit * second)


class Place:
    def __init__(self):
        self.pbs, self.kas = lax.axis_size("pb"), lax.axis_size("ka")
        self.owners, self.zs = self.pbs * self.kas, self.pbs // 2
        self.pb, self.ka, self.ha = lax.axis_index("pb"), lax.axis_index("ka"), lax.axis_index("ha")
        self.z, self.core = self.pb // 2, self.pb % 2
        self.me = self.pb * self.kas + self.ka
        self.stream = 2 * self.ka + self.ha
        self.x_peer = (self.pb, self.ka, 1 - self.ha)
        self.y_peer = (self.pb, 1 - self.ka, self.ha)
        self.xy_peer = (self.pb, 1 - self.ka, 1 - self.ha)
        self.core_peer = (2 * self.z + 1 - self.core, self.ka, self.ha)
        self.quads = [
            (self.xy_peer, 1 - self.ka, 1 - self.ha),
            (self.x_peer, self.ka, 1 - self.ha),
            (self.y_peer, 1 - self.ka, self.ha),
        ]

    def partner(self, k):
        dz, dc, dk = k // 4, k // 2 % 2, k % 2
        z = [self.z, self.z + 1 - 2 * (self.z % 2), (self.z + 2) % 4, 3 - self.z][dz]
        core = 1 - self.core if dc else self.core
        ka = 1 - self.ka if dk else self.ka
        return (2 * z + core) * 2 + ka, (2 * z + core, ka, self.ha)

    def owner_to(self, d):
        index = lax.rem(self.me + d, self.owners)
        return index, (index // self.kas, index % self.kas, self.ha)

    def z_to(self, d):
        return lax.rem(self.z + d, self.zs)

    def z_device(self, d):
        return (2 * self.z_to(d) + self.core, self.ka, self.ha)

    def z_from(self, d):
        return 2 * lax.rem(self.z - d + self.zs, self.zs) + self.core


class Copies:
    def __init__(self, send, recv):
        self.send, self.recv, self.copies = send, recv, []

    def start(self, src, dst, device):
        i = len(self.copies)
        copy = remote(src, dst, self.send.at[i], self.recv.at[i], device)
        copy.start()
        self.copies.append(copy)

    def arrive(self, i):
        self.copies[i].wait_recv()

    def sent(self):
        for copy in self.copies:
            copy.wait_send()


class WeightSum:
    def __init__(self, at, order, s, name):
        self.at, self.order = at, order
        self.own, self.core_in = s[name + "own"], s[name + "core_in"]
        self.mine = [s[f"{name}mine{i}"] for i in range(len(order))]
        self.other = [s[f"{name}other{i}"] for i in range(len(order))]
        self.copies = Copies(s[name + "send"], s[name + "recv"])
        self.begun = [0]

    def pick(self, ref, step, index):
        done = "".join(self.order[: self.order.index(step)])
        left = [a for a in "xzy" if a not in done]
        at_axis = dict(zip(step, index))
        return ref.at[tuple(at_axis.get(a, slice(None)) for a in left)]

    def peers(self, step):
        at = self.at
        if step == "z":
            return [(at.z_device(d), (at.z_to(d),)) for d in range(1, at.zs)]
        if step == "x":
            return [(at.x_peer, (1 - at.ha,))]
        if step == "y":
            return [(at.y_peer, (1 - at.ka,))]
        return [(device, (to_ha, to_ka)) for device, to_ka, to_ha in at.quads]

    def own_index(self, step):
        return tuple({"x": self.at.ha, "y": self.at.ka, "z": self.at.z}[axis] for axis in step)

    def cores(self):
        self.copies.start(self.own.at[:, :, 1 - self.at.core], self.core_in, self.at.core_peer)

    def send(self, i):
        step = self.order[i]
        self.begun.append(len(self.copies.copies))
        for k, (device, index) in enumerate(self.peers(step)):
            self.copies.start(self.pick(self.mine[i], step, index), self.other[i].at[k], device)

    def received(self, i):
        step = self.order[i]
        total = self.pick(self.mine[i], step, self.own_index(step))[...].astype(F32)
        for k in range(len(self.peers(step))):
            self.copies.arrive(self.begun[i + 1] + k)
            total = total + self.other[i][k].astype(F32)
        return total

    def hop(self):
        i = len(self.begun) - 1
        if i == 0:
            self.copies.arrive(0)
            for h in range(2):
                total = self.own[h, :, self.at.core].astype(F32) + self.core_in[h].astype(F32)
                self.mine[0][h] = total.astype(BF16).reshape(self.mine[0].shape[1:])
        else:
            self.mine[i][...] = self.received(i - 1).astype(BF16)
        self.send(i)

    def finish(self):
        return self.received(len(self.order) - 1)


def weight_sum_scratch(name, order, zs, block, cols):
    dma = pltpu.SemaphoreType.DMA
    sizes = {"x": 2, "z": zs, "y": 2}
    found = {
        name + "own": pltpu.VMEM((2, zs, 2, 2 * block, cols), BF16),
        name + "core_in": pltpu.VMEM((2, zs, 2 * block, cols), BF16),
    }
    for i, step in enumerate(order):
        before = [sizes[a] for a in "xzy" if a not in "".join(order[:i])]
        after = [sizes[a] for a in "xzy" if a not in "".join(order[: i + 1])]
        found[f"{name}mine{i}"] = pltpu.VMEM((*before, block, cols), BF16)
        found[f"{name}other{i}"] = pltpu.VMEM(({"xy": 3, "z": zs - 1}.get(step, 1), *after, block, cols), BF16)
    found[name + "send"] = dma((1 + 3 + zs,))
    found[name + "recv"] = dma((1 + 3 + zs,))
    return found


ORDERS = {"a_": ("z", "xy"), "b0_": ("xy", "z"), "b1_": ("xy", "z")}
STEPS = {
    "pair 0": ("a_",),
    "rows sent": (),
    "tables": (),
    "given": ("b0_", "b1_"),
    "take 1": (),
    "take 2": ("b0_", "a_"),
    "take 3": (),
    "take 4": ("b1_",),
    "take 5": (),
}


def main_kernel(in_names, out_names, scratch_names, *refs):
    names = in_names + out_names + scratch_names
    s = dict(zip(names, refs, strict=True))
    s["limit_rows"] = 256
    at = Place()
    owners, zs, ka, ha = at.owners, at.zs, at.ka, at.ha
    count, width = s["context"].shape
    half = width // 2
    tok = count // MB
    group = 2 * tok
    capacity = 2 * count // owners
    block = s["w_uvqk"].shape[0] // 2
    heads_half = half // 64
    heads = 2 * heads_half
    pairs = half // 128
    buckets = s["time"].shape[1]
    gates_cols = 2 * half

    table, table_buf, table_sem = s["table"], s["table_buf"], s["table_sem"]
    chunks = table_sem.shape[0]
    chunk = table.shape[0] // chunks

    def local(i, src, dst):
        copy = pltpu.make_async_copy(src, dst, s["load_sem"].at[i])
        copy.start()
        return copy

    mine = pl.ds(pl.multiple_of(at.stream * tok, tok), tok)
    away = pl.ds(pl.multiple_of((2 * (1 - ka) + ha) * tok, tok), tok)
    loads = {}
    for i, name in enumerate(
        ("owner", "offset", "w_uvqk", "w_out", "b", "rel", "time", "gain_out", "gain_in", "b_out", "lengths", "times")
    ):
        loads[name] = local(i, s[name], s[name + "_v"])
    loads["ctx"] = local(12, s["context"].at[mine], s["ctx_v"].at[ka])
    loads["cot"] = local(13, s["cot"].at[mine], s["cot_v"].at[ka])
    own_cols = pl.ds(pl.multiple_of(ha * half, half), half)

    def table_copy(i):
        rows = pl.ds(pl.multiple_of(i * chunk, chunk), chunk)
        return pltpu.make_async_copy(table.at[rows, own_cols], table_buf.at[rows], table_sem.at[i])

    for i in range(chunks):
        table_copy(i).start()
    barrier = pltpu.get_barrier_semaphore()
    far, near = list(range(owners // 2, owners)), list(range(1, owners // 2))
    partners = [at.partner(k)[1] for k in far + near] + [at.x_peer, at.xy_peer]
    for device in partners:
        pl.semaphore_signal(barrier, inc=1, device_id=device, device_id_type=MESH)

    loads["owner"].wait()
    loads["offset"].wait()
    owner_row, offset_row = s["owner_v"][...], s["offset_v"][...]
    hits = (owner_row == iota((owners, count), 0)).astype(F32)
    earlier = mm(hits.astype(BF16), one_hot(iota((count, count), 0) < iota((count, count), 1)))
    rank = jnp.sum(hits * earlier, axis=0, keepdims=True).astype(jnp.int32)
    rank_hot = one_hot(rank == iota((128, count), 0))
    high = (offset_row // 64).astype(F32)
    low = (offset_row % 64 + 1).astype(F32)
    asked = 64.0 * mm_nt((hits * high).astype(BF16), rank_hot) + mm_nt((hits * low).astype(BF16), rank_hot) - 1.0
    asked = asked.astype(jnp.int32)
    for o in range(owners):
        s["requests"][o] = jnp.broadcast_to(asked[o : o + 1], (8, 128))
    place = owner_row * capacity + rank

    shard, w, small = s["shard"], s["w"], s["small"]
    loads["w_uvqk"].wait()
    for g in range(4):
        shard[:, g * half : (g + 1) * half] = s["w_uvqk_v"][:, g, :]
    loads["w_out"].wait()
    shard[:, 4 * half :] = s["w_out_v"][...]
    w[ha, at.pb] = shard[...]
    for name in ("b", "rel", "time", "gain_out"):
        loads[name].wait()
    small[ha, 0:4] = s["b_v"][...]
    small[ha, 4:8] = s["rel_v"][...]
    for i in range(2):
        for j in range(2):
            small[ha, 8 + i : 9 + i, j * buckets : (j + 1) * buckets] = s["time_v"][2 * i + j : 2 * i + j + 1]
    small[ha, 10:11] = s["gain_out_v"][...]

    pl.semaphore_wait(barrier, len(partners))

    def copies(name):
        return Copies(s[name + "_send"], s[name + "_recv"])

    requests, arrived = s["requests"], s["arrived"]
    req, item, emb_c, row_c, small_c = copies("req"), copies("item"), copies("emb"), copies("row"), copies("small")
    wz, wx, wy, wc = copies("wz"), copies("wx"), copies("wy"), copies("wc")
    for k in far + near:
        to, device = at.partner(k)
        req.start(requests.at[to], arrived.at[at.me], device)
    arrived[at.me] = requests[at.me]
    my_half = pl.ds(pl.multiple_of(ka * block, block), block)
    wz.start(shard.at[my_half], w.at[ha, at.pb, my_half], at.z_device(1))
    wx.start(shard, w.at[ha, at.pb], at.x_peer)
    small_c.start(small.at[ha], small.at[ha], at.x_peer)
    row_c.start(s["context"].at[away], s["ctx_v"].at[ka], at.y_peer)
    row_c.start(s["cot"].at[away], s["cot_v"].at[ka], at.y_peer)
    wc.start(shard, w.at[ha, at.pb], at.core_peer)

    for i in range(owners - 1):
        req.arrive(i)
    for d in range(2, zs):
        wz.start(shard.at[my_half], w.at[ha, at.pb, my_half], at.z_device(d))
    wide_pick = iota((capacity, 128), 1) == iota((capacity, 128), 0)

    def column_of(source):
        tile = jnp.broadcast_to(arrived[source, 0:1], (capacity, 128)).astype(F32)
        return jnp.sum(jnp.where(wide_pick, tile, 0.0), axis=1, keepdims=True)

    fetched, returned, parts, emb = s["fetched"], s["returned"], s["parts"], s["emb"]
    total = s["total"]
    askers = owners // 2

    def look_up(part):
        rounds = [(part * askers + d + 1) % owners for d in range(askers)]
        wanted = [column_of(at.owner_to(d)[0]) for d in rounds]
        column = jnp.concatenate(wanted, axis=0).astype(jnp.int32)
        total[...] = jnp.zeros_like(total)

        def step(i, carry):
            if part == 0:
                table_copy(i).wait()
            rows = pl.ds(pl.multiple_of(i * chunk, chunk), chunk)
            total[...] += mm(one_hot(column == iota((askers * capacity, chunk), 1) + i * chunk), table_buf[rows])
            return carry

        lax.fori_loop(0, chunks, step, 0)
        fetched[part] = total[...].astype(BF16).reshape(fetched.shape[1:])
        for i, d in enumerate(rounds):
            if d:
                item.start(fetched.at[part, i], returned.at[at.me], at.owner_to(d)[1])
            else:
                returned[at.me] = fetched[part, i]

    look_up(0)
    for d in range(1, zs):
        wz.arrive(d - 1)
        there = w.at[ha, at.z_from(d), my_half]
        wx.start(there, there, at.x_peer)
        wy.start(there, there, at.y_peer)
    look_up(1)
    wx.arrive(0)
    there = w.at[1 - ha, at.pb]
    wc.start(there, there, at.core_peer)
    for d in range(1, zs):
        wx.arrive(d)
        there = w.at[1 - ha, at.z_from(d), my_half]
        wy.start(there, there, at.y_peer)

    loads["lengths"].wait()
    loads["times"].wait()
    small_c.arrive(0)
    lane, row = iota((group, group), 1), iota((group, group), 0)
    lengths = s["lengths_v"][pl.ds(at.stream, 1), :]
    ends = jnp.zeros((1, 1), jnp.int32)
    member_row = jnp.zeros((group, group), jnp.int32)
    member_col = jnp.zeros((group, group), jnp.int32)
    inv_count = jnp.zeros((group, group), F32)
    for i in range(SEQ_GRP):
        length = lengths[:, i : i + 1]
        inside = (row >= ends) & (row < ends + length)
        inv_count = jnp.where(inside, 1.0 / jnp.maximum(length, 1).astype(F32), inv_count)
        ends = ends + length
        member_row = member_row + (ends <= row).astype(jnp.int32)
        member_col = member_col + (ends <= lane).astype(jnp.int32)
    allowed = (member_row == member_col) & (member_row < SEQ_GRP) & (lane <= row)
    maskscale = s["maskscale"]
    maskscale[...] = jnp.where(allowed, inv_count, 0.0)
    times_row = jnp.broadcast_to(s["times_v"][pl.ds(at.stream, 1), :], (group, group))
    times_col = jnp.sum(jnp.where(lane == row, times_row, 0).astype(F32), axis=1, keepdims=True).astype(jnp.int32)
    time_index = jnp.clip(times_col - times_row, 0, buckets - 1)
    turn = ((lane + row) % group == 0).astype(F32)
    rel_back = mm_exact(jnp.concatenate([small[0, 4:8, :], small[1, 4:8, :]], axis=0), turn)
    bias = s["bias"]
    for head in range(heads):
        hf, head_in = divmod(head, heads_half)
        begin = (head_in % 2) * buckets
        bucket_row = jnp.broadcast_to(small[hf, 8 + head_in // 2 : 9 + head_in // 2, begin : begin + buckets], (group, buckets))
        by_time = [
            jnp.take_along_axis(bucket_row, time_index[:, c : c + buckets], axis=1, mode="promise_in_bounds")
            for c in range(0, group, buckets)
        ]
        bias[head] = skew(jnp.broadcast_to(rel_back[head : head + 1], (group, group))) + jnp.concatenate(by_time, axis=1)

    for i in range(owners - 1):
        item.arrive(i)
    slot_hot = one_hot(place == iota((2 * count, count), 0))
    parts[...] = mm_tn(slot_hot, returned[...].reshape(2 * count, half)).astype(BF16).reshape(parts.shape)
    for device, to_ka, to_ha in at.quads:
        emb_c.start(parts.at[2 * to_ka + to_ha], emb.at[at.stream], device)
    emb[at.stream] = parts[at.stream]
    for d in range(1, zs):
        wy.arrive(d - 1)
        there = w.at[ha, at.z_from(d)]
        wc.start(there, there, at.core_peer)
    for d in range(1, zs):
        wy.arrive(zs - 2 + d)
        there = w.at[1 - ha, at.z_from(d)]
        wc.start(there, there, at.core_peer)
    slots = 2 * count
    low_lanes = iota((1, 128), 1) < capacity
    ids = []
    for i in range(owners // 2):
        ids.append(jnp.where(low_lanes, arrived[2 * i, 0:1], pltpu.roll(arrived[2 * i + 1, 0:1], capacity, 1)))
    ids_row = jnp.concatenate(ids, axis=1)
    ids_col = jnp.concatenate([column_of(o) for o in range(owners)], axis=0).astype(jnp.int32)
    last = table.shape[0]
    ids_row = jnp.where(ids_row < 0, last, ids_row)
    ids_col = jnp.where(ids_col < 0, last, ids_col)
    keys_row, keys_col = ids_row * slots + iota((1, slots), 1), ids_col * slots + iota((slots, 1), 0)
    order = jnp.sum((keys_col < keys_row).astype(F32), axis=0, keepdims=True).astype(jnp.int32)
    s["turn"][...] = one_hot(order == iota((slots, slots), 0))
    digits = jnp.concatenate([ids_row // 64, ids_row % 64] + [jnp.zeros((1, slots), jnp.int32)] * 6, axis=0)
    found = mm_nt(digits.astype(F32).astype(BF16), s["turn"][...])
    s["sorted_v"][...] = (64.0 * found[0:1] + found[1:2]).astype(jnp.int32)
    limits = iota((slots, 128), 1) * s["limit_rows"]
    s["limits_v"][...] = jnp.sum((ids_col < jnp.minimum(limits, last)).astype(F32), axis=0, keepdims=True).astype(jnp.int32)
    out_copies = [local(14, s["sorted_v"], s["sorted"]), local(15, s["limits_v"], s["limits"])]
    for i in range(2 * zs):
        wc.arrive(i)

    def w_half(hf, cols):
        return w[hf, :, :, cols].reshape(width, cols.stop - cols.start)

    out_cols = slice(4 * half, 5 * half)
    loads["cot"].wait()
    row_c.arrive(1)
    cot = s["cot_v"][...].reshape(group, width)
    grad_mixed = jnp.concatenate([mm(cot, w_half(hf, out_cols)) for hf in range(2)], axis=1)
    loads["gain_in"].wait()
    loads["b_out"].wait()
    loads["ctx"].wait()
    row_c.arrive(0)
    for i in range(3):
        emb_c.arrive(i)

    embedded = jnp.concatenate(
        [jnp.concatenate([emb[2 * i], emb[2 * i + 1]], axis=1).astype(F32) for i in range(2)], axis=0
    )
    start = s["ctx_v"][...].reshape(group, width).astype(F32) + embedded
    unit_in, inv_in = layer_norm(start)
    gain_in = s["gain_in_v"][...]
    normed = (unit_in * gain_in).astype(BF16)
    slope, qkv, w_att, sm = s["slope"], s["qkv"], s["w_att"], s["sm"]
    gates = []
    for hf in range(2):
        for g in range(4):
            cols = slice(g * half, (g + 1) * half)
            pre = mm(normed, w_half(hf, cols)) + small[hf, g : g + 1, :]
            sig = sigmoid(pre)
            act = pre * sig
            slope[hf, :, cols] = sig + act * (1.0 - sig)
            if g == 0:
                gates.append(act)
            else:
                qkv[hf, g - 1] = (act * 0.125 if g == 2 else act).astype(BF16)
    gate = jnp.concatenate(gates, axis=1)
    low_half = iota((group, 128), 1) < 64

    def split(tile):
        zero = jnp.zeros_like(tile)
        return jnp.where(low_half, tile, zero), jnp.where(low_half, zero, tile)

    attended = []
    for hf in range(2):
        for pair in range(pairs):
            cols = slice(pair * 128, (pair + 1) * 128)
            values, queries = split(qkv[hf, 0, :, cols]), split(qkv[hf, 1, :, cols])
            keys = qkv[hf, 2, :, cols]
            both = None
            for sub in range(2):
                head = hf * heads_half + pair * 2 + sub
                scores = mm_nt(queries[sub], keys) + bias[head]
                sig = sigmoid(scores)
                act = scores * sig
                weights = (act * maskscale[...]).astype(BF16)
                w_att[head] = weights
                sm[head] = (sig + act * (1.0 - sig)) * maskscale[...]
                part = mm(weights, values[sub])
                both = part if both is None else both + part
            attended.append(both)
    unit_out, inv_out = layer_norm(jnp.concatenate(attended, axis=1))
    gain_out = jnp.concatenate([small[0, 10:11, :], small[1, 10:11, :]], axis=1)
    mixed_in = (unit_out * gain_out * gate).astype(BF16)
    projected = None
    for hf in range(2):
        part = mm_nt(mixed_in[:, hf * half : (hf + 1) * half], w_half(hf, out_cols))
        projected = part if projected is None else projected + part
    mixed, mixed_rows = s["mixed"], s["mixed_v"]
    mixed[...] = (projected + s["b_out_v"][...] + start).astype(BF16)
    mixed_c = copies("mixed")
    for device, to_ka, to_ha in at.quads:
        here = mixed.at[pl.ds(to_ka * tok, tok), pl.ds(pl.multiple_of(to_ha * half, half), half)]
        mixed_c.start(here, mixed_rows.at[at.stream], device)
    own_rows = pl.ds(pl.multiple_of(ka * tok, tok), tok)
    mixed_rows[at.stream] = mixed[own_rows, pl.ds(pl.multiple_of(ha * half, half), half)]

    grad_pre, grad_small = s["grad_pre"], s["grad_small"]
    grad_raw = grad_mixed * unit_out
    grad_gate = grad_raw * gain_out
    grad_gain_out = jnp.sum(grad_raw * gate, axis=0, keepdims=True)
    grad_att = layer_norm_back(grad_mixed * gate * gain_out, unit_out, inv_out).astype(BF16)
    sum_a = WeightSum(at, ORDERS["a_"], s, "a_")
    sums_b = [WeightSum(at, ORDERS[f"b{i}_"], s, f"b{i}_") for i in range(pairs)]

    hops = {"a_": sum_a} | {f"b{i}_": part for i, part in enumerate(sums_b)}

    def steps_at(point):
        for name in STEPS[point]:
            hops[name].hop()

    def put(own, hf, first, value):
        cols = value.shape[1]
        own[hf, :, :, :, first : first + cols] = value.astype(BF16).reshape(own.shape[1:4] + (cols,))

    for hf in range(2):
        cols = slice(hf * half, (hf + 1) * half)
        grad_pre[hf, :, 0:half] = (grad_gate[:, cols] * slope[hf, :, 0:half]).astype(BF16)
        grad_small[hf, 10:11, :] = grad_gain_out[:, cols]
        put(s["a_own"], hf, 0, mm_tn(normed, grad_pre[hf, :, 0:half]))
        put(s["a_own"], hf, half, mm_tn(cot, mixed_in[:, cols]))
    sum_a.cores()

    gs = s["gs"]
    for pair in range(pairs):
        for hf in range(2):
            cols = slice(pair * 128, (pair + 1) * 128)
            values = qkv[hf, 0, :, cols]
            queries, keys = split(qkv[hf, 1, :, cols]), split(qkv[hf, 2, :, cols])
            grads = split(grad_att[:, hf * half + pair * 128 : hf * half + (pair + 1) * 128])
            sums = None
            for sub in range(2):
                head = hf * heads_half + pair * 2 + sub
                grad_scores = (mm_nt(grads[sub], values) * sm[head]).astype(BF16)
                gs[:, head * group : (head + 1) * group] = grad_scores
                found = (
                    mm_tn(w_att[head], grads[sub]),
                    mm(grad_scores, keys[sub]),
                    mm_tn(grad_scores, queries[sub]),
                )
                sums = found if sums is None else [a + b for a, b in zip(sums, found)]
            for g, part in ((1, sums[0]), (2, sums[1] * 0.125), (3, sums[2])):
                there = slice(g * half + pair * 128, g * half + (pair + 1) * 128)
                grad_pre[hf, :, there] = (part * slope[hf, :, there]).astype(BF16)
        if pair == 0:
            steps_at("pair 0")
    grad_normed = None
    for hf in range(2):
        part = mm_nt(grad_pre[hf], w_half(hf, slice(0, 4 * half)))
        grad_normed = part if grad_normed is None else grad_normed + part
    cot32 = cot.astype(F32)
    grad_start, grad_rows = s["grad_start"], s["grad_rows_v"]
    grad_start[...] = (cot32 + layer_norm_back(grad_normed * gain_in, unit_in, inv_in)).astype(BF16)
    back_c = copies("back")
    for first in (True, False):
        for device, to_ka, to_ha in at.quads:
            h = to_ha if first else 1 - to_ha
            cols = pl.ds(pl.multiple_of(h * half, half), half)
            here = grad_start.at[pl.ds(pl.multiple_of(to_ka * tok, tok), tok), cols]
            back_c.start(here, grad_rows.at[at.stream, :, cols], device)
    grad_rows[at.stream] = grad_start[own_rows]
    for pair in range(pairs):
        for hf in range(2):
            for g in range(1, 4):
                there = slice(g * half + pair * 128, g * half + (pair + 1) * 128)
                put(s[f"b{pair}_own"], hf, (g - 1) * 128, mm_tn(normed, grad_pre[hf, :, there]))
        sums_b[pair].cores()
    steps_at("rows sent")
    gain_grad = jnp.sum(grad_normed * unit_in, axis=0, keepdims=True)
    bout_grad = jnp.sum(cot32, axis=0, keepdims=True)
    for hf in range(2):
        sums = jnp.sum(grad_pre[hf].astype(F32), axis=0, keepdims=True)
        for g in range(4):
            grad_small[hf, g : g + 1, :] = sums[:, g * half : (g + 1) * half]
        grad_small[hf, 11:12, :] = gain_grad[:, hf * half : (hf + 1) * half]
        grad_small[hf, 12:13, :] = bout_grad[:, hf * half : (hf + 1) * half]
        grad_small[hf, 13:16, :] = jnp.zeros((3, half), F32)
    flip = (lane + row == group - 1).astype(F32)
    kept_pairs = lane + row <= group - 1
    hot_cols = one_hot(times_row == row)
    hot_back = one_hot(times_row == group - 1 - row)
    folded = mm(jnp.concatenate([flip.astype(BF16), hot_back], axis=0), gs[...])
    rel_rows, time_rows, early_rows = [], [], []
    for head in range(heads):
        places = slice(head * group, (head + 1) * group)
        rel_rows.append(jnp.sum(skew(folded[:group, places]), axis=0, keepdims=True))
        pairs_sum = mm_nt(folded[group:, places].astype(BF16), hot_cols)
        kept = jnp.where(kept_pairs, pairs_sum, 0.0)
        time_rows.append(jnp.sum(skew(kept), axis=0, keepdims=True))
        early_rows.append(jnp.sum(pairs_sum - kept, axis=0, keepdims=True))
    flipped = mm_exact(jnp.concatenate(rel_rows + time_rows, axis=0), flip)
    early = jnp.sum(jnp.concatenate(early_rows, axis=0), axis=1, keepdims=True)
    late = jnp.sum(flipped[heads:, buckets:], axis=1, keepdims=True)
    place_in = iota((heads, buckets), 1)
    time_grad = flipped[heads:, :buckets] + jnp.where(place_in == 0, early, 0.0) + jnp.where(place_in == buckets - 1, late, 0.0)
    for head in range(heads):
        hf, head_in = divmod(head, heads_half)
        begin = (head_in % 2) * buckets
        grad_small[hf, 4 + head_in : 5 + head_in, :] = flipped[head : head + 1]
        grad_small[hf, 8 + head_in // 2 : 9 + head_in // 2, begin : begin + buckets] = time_grad[head : head + 1]
    small_in, small_mine = s["small_in"], s["small_mine"]
    sum_c = copies("sum")
    sum_c.start(grad_small, small_in.at[0], at.core_peer)

    steps_at("tables")
    for i in range(3):
        back_c.arrive(i)
    outgoing, incoming = s["outgoing"], s["incoming"]
    slot_hot = one_hot(place == iota((2 * count, count), 0))
    outgoing[...] = mm(slot_hot, grad_rows[:, :, own_cols].reshape(count, half)).astype(BF16).reshape(outgoing.shape)
    give, hand = copies("give"), copies("hand")
    given = {}

    def start_give(*rounds):
        for k in rounds:
            to, device = at.partner(k)
            given[k] = len(give.copies)
            give.start(outgoing.at[to], incoming.at[ha, at.me], device)

    start_give(8, 9, 10, 11, 1, 2, 3, 4, 5, 6, 7)
    incoming[ha, at.me] = outgoing[at.me]
    hand.start(incoming.at[ha, at.me], incoming.at[ha, at.me], at.x_peer)

    def take(*rounds):
        for k in rounds:
            give.arrive(given[k])
            there = incoming.at[ha, at.partner(k)[0]]
            hand.start(there, there, at.x_peer)

    steps_at("given")
    take(1, 2, 3)
    sum_c.arrive(0)
    small_mine[0] = grad_small[...] + small_in[0]
    for i, (device, _, _) in enumerate(at.quads):
        sum_c.start(small_mine.at[0], small_in.at[1 + i], device)
    steps_at("take 1")
    take(8, 9)
    start_give(12, 13)
    steps_at("take 2")
    take(4, 5, 6, 7)
    steps_at("take 3")
    take(10, 11)
    start_give(14, 15)
    summed = small_mine[0]
    for i in range(1, 4):
        sum_c.arrive(i)
        summed = summed + small_in[i]
    small_mine[1] = summed
    for d in range(1, zs):
        sum_c.start(small_mine.at[1], small_in.at[3 + d], at.z_device(d))
    steps_at("take 4")
    take(12, 13)
    steps_at("take 5")
    take(14, 15)
    def in_order(h):
        cols = pl.ds(pl.multiple_of(h * half, half), half)
        s["rows_v"][:, cols] = mm(s["turn"][...], incoming[h].reshape(slots, half)).astype(BF16)

    in_order(ha)
    for i in range(3, 6):
        back_c.arrive(i)
    out_copies.append(local(16, grad_rows, s["grad_rows"]))
    for i in range(3):
        mixed_c.arrive(i)
    out_copies.append(local(17, mixed_rows, s["mixed_rows"]))
    grad_w = s["grad_w_v"]
    grad_w[:, 0:gates_cols] = sum_a.finish()
    for i in range(pairs):
        first = gates_cols + i * 384
        grad_w[:, first : first + 384] = sums_b[i].finish()
    summed = small_mine[1]
    for d in range(1, zs):
        sum_c.arrive(3 + d)
        summed = summed + small_in[3 + d]
    s["small_v"][...] = summed
    out_copies += [local(18, grad_w, s["grad_w"]), local(19, s["small_v"], s["small_sum"])]
    for i in range(owners):
        hand.arrive(i)
    cols = pl.ds(pl.multiple_of((1 - ha) * half, half), half)
    handed = incoming[1 - ha].reshape(slots, half)
    for i in range(slots // 256):
        rows = pl.ds(i * 256, 256)
        s["rows_v"][rows, cols] = mm(s["turn"][rows, :], handed).astype(BF16)
        out_copies.append(local(20 + i, s["rows_v"].at[rows], s["rows"].at[rows]))
    for copy in out_copies:
        copy.wait()
    for kind in (req, item, emb_c, row_c, small_c, wz, wx, wy, wc, mixed_c, back_c, give, hand, sum_c):
        kind.sent()
    for part in [sum_a] + sums_b:
        part.copies.sent()


def run_main(inputs):
    pbs, kas = lax.axis_size("pb"), lax.axis_size("ka")
    owners, zs = pbs * kas, pbs // 2
    count, width = inputs["context"].shape
    half, tok, capacity = width // 2, count // MB, 2 * count // owners
    group, heads = 2 * tok, width // 64
    shard_rows = inputs["w_uvqk"].shape[0]
    block = shard_rows // 2
    dma = pltpu.SemaphoreType.DMA
    outs = {
        "rows": jax.ShapeDtypeStruct((2 * count, width), BF16),
        "sorted": jax.ShapeDtypeStruct((1, 2 * count), jnp.int32),
        "limits": jax.ShapeDtypeStruct((1, 128), jnp.int32),
        "grad_rows": jax.ShapeDtypeStruct((MB, tok, width), BF16),
        "mixed_rows": jax.ShapeDtypeStruct((MB, tok, half), BF16),
        "grad_w": jax.ShapeDtypeStruct((block, 5 * half), F32),
        "small_sum": jax.ShapeDtypeStruct((2, 16, half), F32),
    }
    scratch = {
        "ctx_v": pltpu.VMEM((2, tok, width), BF16),
        "cot_v": pltpu.VMEM((2, tok, width), BF16),
        "requests": pltpu.VMEM((owners, 8, 128), jnp.int32),
        "arrived": pltpu.VMEM((owners, 8, 128), jnp.int32),
        "table_buf": pltpu.VMEM((inputs["table"].shape[0], half), BF16),
        "total": pltpu.VMEM((count, half), F32),
        "fetched": pltpu.VMEM((2, owners // 2, capacity, half), BF16),
        "returned": pltpu.VMEM((owners, capacity, half), BF16),
        "parts": pltpu.VMEM((MB, tok, half), BF16),
        "emb": pltpu.VMEM((MB, tok, half), BF16),
        "shard": pltpu.VMEM((shard_rows, 5 * half), BF16),
        "w": pltpu.VMEM((2, pbs, shard_rows, 5 * half), BF16),
        "small": pltpu.VMEM((2, 16, half), F32),
        "maskscale": pltpu.VMEM((group, group), F32),
        "bias": pltpu.VMEM((heads, group, group), F32),
        "slope": pltpu.VMEM((2, group, 4 * half), F32),
        "qkv": pltpu.VMEM((2, 3, group, half), BF16),
        "w_att": pltpu.VMEM((heads, group, group), BF16),
        "sm": pltpu.VMEM((heads, group, group), F32),
        "gs": pltpu.VMEM((group, heads * group), BF16),
        "grad_pre": pltpu.VMEM((2, group, 4 * half), BF16),
        "mixed": pltpu.VMEM((group, width), BF16),
        "grad_start": pltpu.VMEM((group, width), BF16),
        "grad_small": pltpu.VMEM((2, 16, half), F32),
        "outgoing": pltpu.VMEM((owners, capacity, half), BF16),
        "small_mine": pltpu.VMEM((2, 2, 16, half), F32),
        "small_in": pltpu.VMEM((3 + zs, 2, 16, half), F32),
        "incoming": pltpu.VMEM((2, owners, capacity, half), BF16),
        "rows_v": pltpu.VMEM((2 * count, width), BF16),
        "turn": pltpu.VMEM((2 * count, 2 * count), BF16),
        "sorted_v": pltpu.VMEM((1, 2 * count), jnp.int32),
        "limits_v": pltpu.VMEM((1, 128), jnp.int32),
        "grad_rows_v": pltpu.VMEM((MB, tok, width), BF16),
        "mixed_v": pltpu.VMEM((MB, tok, half), BF16),
        "grad_w_v": pltpu.VMEM((block, 5 * half), F32),
        "small_v": pltpu.VMEM((2, 16, half), F32),
        "load_sem": dma((20 + 2 * count // 256,)),
        "table_sem": dma((2,)),
    }
    for name in ("owner", "offset", "w_uvqk", "w_out", "b", "rel", "time", "gain_out", "gain_in", "b_out", "lengths", "times"):
        scratch[name + "_v"] = pltpu.VMEM(inputs[name].shape, inputs[name].dtype)
    for name, number in (
        ("req", owners - 1), ("item", owners - 1), ("emb", 3), ("row", 2), ("small", 1), ("wz", zs - 1), ("wx", zs),
        ("wy", 2 * zs - 2), ("wc", 2 * zs), ("mixed", 3), ("back", 6), ("give", owners - 1), ("hand", owners), ("sum", 3 + zs),
    ):
        scratch[name + "_send"] = dma((number,))
        scratch[name + "_recv"] = dma((number,))
    scratch |= weight_sum_scratch("a_", ORDERS["a_"], zs, block, 2 * half)
    for i in range(half // 128):
        scratch |= weight_sum_scratch(f"b{i}_", ORDERS[f"b{i}_"], zs, block, 384)
    hbm = pl.BlockSpec(memory_space=pltpu.HBM)
    found = pl.pallas_call(
        functools.partial(main_kernel, tuple(inputs), tuple(outs), tuple(scratch)),
        out_shape=tuple(outs.values()),
        in_specs=[hbm] * len(inputs),
        out_specs=(hbm,) * len(outs),
        scratch_shapes=list(scratch.values()),
        compiler_params=pltpu.CompilerParams(
            collective_id=1, has_side_effects=True, vmem_limit_bytes=58 * 1024 * 1024
        ),
    )(*inputs.values())
    return dict(zip(outs, found, strict=True))


def scatter_kernel(
    limits_in, sorted_in, rows_in, grad_w_in, small_in, mixed_in, grad_rows_in,
    out_ref, w_ref, w_out_ref, b_ref, rel_ref, time_ref, gain_in_ref, gain_out_ref, b_out_ref, mixed_out, grad_rows_out,
    limits, ids, rows, grad_w_ref, small_ref, mixed, grad_rows, tiles, load_sem, row_sem, tile_sem, pass_sem,
):
    pairs_in = [
        (limits_in, limits), (sorted_in, ids), (grad_w_in, grad_w_ref), (small_in, small_ref),
        (mixed_in, mixed), (grad_rows_in, grad_rows),
    ]
    depth = 256

    def load_rows(j):
        here = pl.ds(j * depth, depth)
        return pltpu.make_async_copy(rows_in.at[here], rows.at[here], row_sem.at[j])

    blocks = rows.shape[0] // depth
    loads = [pltpu.make_async_copy(src, dst, load_sem.at[i]) for i, (src, dst) in enumerate(pairs_in)]
    for load in loads[:2]:
        load.start()
    for j in range(blocks):
        load_rows(j).start()
    for load in loads[2:]:
        load.start()
    for load in loads[:2]:
        load.wait()
    load_rows(0).wait()
    slots, tile = tiles.shape[0], tiles.shape[1]
    count = out_ref.shape[0] // tile
    per_tile = tile // 256

    def write(i, slot):
        there = pl.ds(pl.multiple_of(i * tile, tile), tile)
        return pltpu.make_async_copy(tiles.at[slot], out_ref.at[there], tile_sem.at[slot])

    def step(i, carry):
        slot = lax.rem(i, slots)

        @pl.when(i >= slots)
        def _():
            write(i - slots, slot).wait()

        first = limits[0, i * per_tile] // depth
        end = (limits[0, (i + 1) * per_tile] + depth - 1) // depth

        def product(j):
            here = pl.ds(pl.multiple_of(j * depth, depth), depth)
            return mm(one_hot(ids[:, here] == iota((tile, depth), 0) + i * tile), rows[here, :])

        tiles[slot] = product(jnp.minimum(first, rows.shape[0] // depth - 1))

        def more(j, carry):
            tiles[slot] += product(j)
            return carry

        lax.fori_loop(first + 1, end, more, 0)
        write(i, slot).start()
        return carry

    crowded = limits[0, per_tile] > depth

    def other_rows():
        for j in range(1, blocks):
            load_rows(j).wait()

    pl.when(crowded)(other_rows)
    step(0, 0)
    pl.when(jnp.logical_not(crowded))(other_rows)
    lax.fori_loop(1, 3, step, 0)
    for load in loads[2:]:
        load.wait()
    passed = [
        pltpu.make_async_copy(mixed, mixed_out, pass_sem.at[0]),
        pltpu.make_async_copy(grad_rows, grad_rows_out, pass_sem.at[1]),
    ]
    for copy in passed:
        copy.start()
    lax.fori_loop(3, count, step, 0)
    half = w_ref.shape[2]
    buckets = time_ref.shape[1]
    w_ref[:, 0, :] = grad_w_ref[:, 0:half]
    w_out_ref[...] = grad_w_ref[:, half : 2 * half]
    for pair in range(half // 128):
        for g in range(1, 4):
            first = 2 * half + pair * 384 + (g - 1) * 128
            w_ref[:, g, pair * 128 : (pair + 1) * 128] = grad_w_ref[:, first : first + 128]
    ha = lax.axis_index("ha")
    b_ref[...] = small_ref[ha, 0:4, :]
    rel_ref[...] = small_ref[ha, 4:8, :]
    for i in range(2):
        for j in range(2):
            time_ref[2 * i + j : 2 * i + j + 1, :] = small_ref[ha, 8 + i : 9 + i, j * buckets : (j + 1) * buckets]
    gain_out_ref[...] = small_ref[ha, 10:11, :]
    for hf in range(2):
        gain_in_ref[:, hf * half : (hf + 1) * half] = small_ref[hf, 11:12, :]
        b_out_ref[:, hf * half : (hf + 1) * half] = small_ref[hf, 12:13, :]
    for k in range(slots):
        write(count - slots + k, (count - slots + k) % slots).wait()
    for copy in passed:
        copy.wait()


def scatter_rows(found, table_rows, buckets, tile=512, slots=4):
    rows, grad_w = found["rows"], found["grad_w"]
    width = rows.shape[1]
    half, block = width // 2, grad_w.shape[0]
    names = ("limits", "sorted", "rows", "grad_w", "small_sum", "mixed_rows", "grad_rows")
    shapes = [(block, 4, half), (block, half), (4, half), (4, half), (4, buckets), (1, width), (1, half), (1, width)]
    hbm, vmem = pl.BlockSpec(memory_space=pltpu.HBM), pl.BlockSpec(memory_space=pltpu.VMEM)
    outs = [jax.ShapeDtypeStruct(shape, F32) for shape in [(table_rows, width)] + shapes]
    outs += [jax.ShapeDtypeStruct(found[name].shape, BF16) for name in ("mixed_rows", "grad_rows")]
    return pl.pallas_call(
        scatter_kernel,
        out_shape=outs,
        in_specs=[hbm] * len(names),
        out_specs=[hbm] + [vmem] * len(shapes) + [hbm] * 2,
        scratch_shapes=[
            pltpu.SMEM(found["limits"].shape, jnp.int32),
            pltpu.VMEM(found["sorted"].shape, jnp.int32),
            pltpu.VMEM(rows.shape, BF16),
            pltpu.VMEM(grad_w.shape, F32),
            pltpu.VMEM(found["small_sum"].shape, F32),
            pltpu.VMEM(found["mixed_rows"].shape, BF16),
            pltpu.VMEM(found["grad_rows"].shape, BF16),
            pltpu.VMEM((slots, tile, width), F32),
            pltpu.SemaphoreType.DMA((len(names),)),
            pltpu.SemaphoreType.DMA((rows.shape[0] // 256,)),
            pltpu.SemaphoreType.DMA((slots,)),
            pltpu.SemaphoreType.DMA((2,)),
        ],
        compiler_params=pltpu.CompilerParams(vmem_limit_bytes=58 * 1024 * 1024),
    )(*(found[name] for name in names))


def local_streams(
    context,
    item_owner,
    item_offset,
    lengths,
    times,
    table,
    cotangent,
    ln_in_gain,
    w_uvqk,
    b_uvqk,
    rel_bias,
    time_bias,
    ln_out_gain,
    w_out,
    b_out,
):
    row_count, width = context.shape
    half = width // 2
    found = run_main(
        {
            "owner": item_owner.reshape(1, row_count),
            "offset": item_offset.reshape(1, row_count),
            "context": context,
            "cot": cotangent,
            "table": table,
            "w_uvqk": w_uvqk,
            "w_out": w_out.T,
            "b": b_uvqk,
            "rel": rel_bias,
            "time": time_bias,
            "gain_out": ln_out_gain.reshape(1, half),
            "gain_in": ln_in_gain.reshape(1, width),
            "b_out": b_out.reshape(1, width),
            "lengths": lengths[0],
            "times": times[0],
        }
    )
    (
        table_grad, grad_w, grad_w_out, grad_b, grad_rel, grad_time, grad_gain_in, grad_gain_out, grad_b_out, mixed, grad_rows,
    ) = scatter_rows(found, table.shape[0], time_bias.shape[1])
    return (
        mixed.reshape(row_count, half),
        grad_rows.reshape(row_count, width),
        table_grad,
        grad_gain_in.reshape(width),
        grad_w,
        grad_b,
        grad_rel,
        grad_time,
        grad_gain_out.reshape(half),
        grad_w_out.T,
        grad_b_out.reshape(width),
    )


def solution(mesh):
    one_stream = mesh.shape["ka"] * mesh.shape["ha"] == MB and mesh.shape["ka"] == 2 and mesh.shape["pb"] == 8
    return jax.shard_map(
        local_streams if one_stream else local_general,
        mesh=mesh,
        in_specs=(
            P(("pb", "ka"), None),
            P(("pb", "ka"), None),
            P(("pb", "ka")),
            P("pb", None, None),
            P("pb", None, None),
            P(("pb", "ka"), None),
            P(("pb", "ka"), None),
            P(),
            P("pb", None, "ha"),
            P(None, "ha"),
            P("ha", None),
            P("ha", None),
            P("ha"),
            P("ha", "pb"),
            P(),
        ),
        out_specs=(
            P(("pb", "ka"), "ha"),
            P(("pb", "ka"), None),
            P(("pb", "ka"), None),
            P(),
            P(("pb", "ka"), None, "ha"),
            P(None, "ha"),
            P("ha", None),
            P("ha", None),
            P("ha"),
            P("ha", ("pb", "ka")),
            P(),
        ),
        check_vma=False,
    )
```
